256 devices in a mesh: img: 64 (over z, x, core), rep: 4 (over y).
Axes of the slice: x: 4, y: 4, z: 8, core: 2. Of those that a mesh axis runs over, the one named last changes fastest.
Arguments:
- tokens: bfloat16 [512, 24, 1024], P('img'), may hold values from -6 to 6
- proj_in: bfloat16 [1024, 768], replicated, may hold values from -0.1875 to 0.1875
- attn_query: bfloat16 [768, 768], replicated, may hold values from -1 to 1
- attn_keyval: bfloat16 [768, 1536], replicated, may hold values from -1 to 1
- attn_output: bfloat16 [768, 768], replicated, may hold values from -0.21875 to 0.21875
- mlp_up: bfloat16 [768, 1536], replicated, may hold values from -0.21875 to 0.21875
- mlp_down: bfloat16 [1536, 768], replicated, may hold values from -0.15625 to 0.15625
- pair_list: int32 [8192, 2], P(('img', 'rep')), may hold values from 0 to 511, as said below
- conf_level: int32 [8192], P(('img', 'rep')), may hold values from 0 to 15
- conf_table: float32 [16], replicated, may hold values from 0.1 to 1
Outputs:
- joined: bfloat16 [512, 24, 768], P('img')
The draws below stay inside these ranges and needn't reach their ends.
Inputs may be any that keep to these rules, and one draw needn't show every extreme that they name: `pair_list`: the two images of a pair differ. Among the 64 image entries of the pairs of one device, at most 2 lie in the images o * 8 to (o + 1) * 8 - 1 of one index o of img, and on every device some o has exactly 2.
All inputs are finite; a program needn't handle non-finite values.
Results may differ from the reference program's by a relative error of at most 0.014.
Values may be sent and summed in bfloat16 or wider, within the bound.
A program may use at most 128 MiB of HBM per device.

```python
import math
import jax
import jax.numpy as jnp
from jax import lax

E = 1024
HEAD_DIM = 64
D = 768
FF = 1536
TOK = 24
IMG_DEV = 8
CAP = 2
LEVELS = 16
PAIR_DEV = 32
IMAGES = 512
PAIRS = 8192


def draw_pair_list(key, part):
    key = jax.random.fold_in(key, 7)
    owner_count = IMAGES // IMG_DEV
    worker_count = PAIRS // PAIR_DEV
    slot_count = owner_count * CAP
    end_count = 2 * PAIR_DEV

    def draw_worker(worker_key):
        key_a, key_b, key_c, key_d = jax.random.split(worker_key, 4)
        slot_owner = jnp.arange(slot_count, dtype=jnp.int32) // CAP
        first_owner = jax.random.randint(key_a, (), 0, owner_count, dtype=jnp.int32)
        scores = jax.random.permutation(key_b, slot_count).astype(jnp.int32)
        scores = jnp.where(slot_owner == first_owner, scores - slot_count, scores)
        ordered = jnp.argsort(scores, stable=True)
        chosen = slot_owner[ordered][:end_count]
        chosen = chosen[jax.random.permutation(key_c, end_count)]
        local_idx = jax.random.randint(key_d, (end_count,), 0, IMG_DEV, dtype=jnp.int32)
        left_img = chosen[:PAIR_DEV] * IMG_DEV + local_idx[:PAIR_DEV]
        right_local = local_idx[PAIR_DEV:]
        clashes = (chosen[:PAIR_DEV] == chosen[PAIR_DEV:]) & (local_idx[:PAIR_DEV] == right_local)
        right_local = jnp.where(clashes, (right_local + 1) % IMG_DEV, right_local)
        right_img = chosen[PAIR_DEV:] * IMG_DEV + right_local
        return jnp.stack([left_img, right_img], axis=1)
    worker_keys = jax.random.split(key, worker_count)
    return jax.vmap(draw_worker)(worker_keys).reshape(PAIRS, 2).astype(jnp.int32)


def draw_attn_query(key, part):
    key = jax.random.fold_in(key, 11)
    key_a = jax.random.fold_in(key, 0)
    matrix = jnp.clip(jax.random.normal(key_a, (D, D), jnp.float32), -6.0, 6.0) / jnp.sqrt(jnp.float32(D))
    return matrix.astype(jnp.bfloat16)


def draw_attn_keyval(key, part):
    key = jax.random.fold_in(key, 13)
    key_a = jax.random.fold_in(key, 0)
    matrix = jnp.clip(jax.random.normal(key_a, (D, 2 * D), jnp.float32), -6.0, 6.0) / jnp.sqrt(jnp.float32(D))
    return matrix.astype(jnp.bfloat16)


def place_ends(values, stream_key, low, top_value):
    place = [jax.random.randint(jax.random.fold_in(stream_key, axis), (), 0, length) for axis, length in enumerate(values.shape)]
    main_axis = values.shape.index(max(values.shape))
    neighbour = place[:main_axis] + [(place[main_axis] + 1) % values.shape[main_axis]] + place[main_axis + 1:]
    return values.at[tuple(place)].set(low).at[tuple(neighbour)].set(top_value)


def block_levels(key, shape, pieces, low, top_value):
    def one(axis_at, parts):
        draws = jax.random.uniform(jax.random.fold_in(jax.random.fold_in(key, 6), axis_at), (parts,), jnp.float32, low / len(pieces), top_value / len(pieces))
        return jnp.repeat(jnp.exp(draws), shape[axis_at] // parts).reshape((-1,) + (1,) * (len(shape) - axis_at - 1))

    loudness = one(*pieces[0])
    for cut in pieces[1:]:
        loudness = loudness * one(*cut)
    return loudness


def noise(stream_key, shape, width, most, shards=(), kind=jnp.bfloat16):
    entries = width * jax.random.normal(stream_key, shape, jnp.float32)
    if shards:
        entries = entries * block_levels(stream_key, shape, shards, -0.22, 0.18)
    return jnp.clip(entries, -most, most).astype(kind)


def setup_inputs(seed: int = 0) -> dict:
    arg_keys = jax.random.split(jax.random.key(seed), 11)
    return {
        "tokens": noise(arg_keys[0], (IMAGES, TOK, E), 1.0, 6.0, ((0, 64),)),
        "proj_in": noise(arg_keys[1], (E, D), E ** -0.5, 0.1875),
        "attn_query": draw_attn_query(jax.random.fold_in(arg_keys[10], 71), 0),
        "attn_keyval": draw_attn_keyval(jax.random.fold_in(arg_keys[10], 71), 0),
        "attn_output": noise(arg_keys[4], (D, D), D ** -0.5, 0.21875),
        "mlp_up": noise(arg_keys[5], (D, FF), D ** -0.5, 0.21875),
        "mlp_down": noise(arg_keys[6], (FF, D), FF ** -0.5, 0.15625),
        "pair_list": draw_pair_list(jax.random.fold_in(arg_keys[10], 71), 0),
        "conf_level": place_ends(jax.random.randint(arg_keys[8], (PAIRS,), 0, LEVELS), jax.random.fold_in(arg_keys[8], 1), 0, LEVELS - 1).astype(jnp.int32),
        "conf_table": jnp.clip(jnp.exp(jax.random.uniform(arg_keys[9], (LEVELS,), jnp.float32, math.log(0.1), math.log(1.0))), 0.1, 1.0),
    }


def normalize(values):
    centred = values - lax.optimization_barrier(jnp.mean(values, axis=-1, keepdims=True))
    spread = lax.optimization_barrier(jnp.mean(centred * centred, axis=-1, keepdims=True))
    return centred * lax.rsqrt(spread + 1e-06)

def pair_features(query_side, memory_side, attn_query, attn_keyval, attn_output, mlp_up, mlp_down, confidence):
    pair_count, tok_count, model_width = query_side.shape
    head_count = model_width // HEAD_DIM
    query_norm = normalize(query_side.astype(jnp.float32)).astype(jnp.bfloat16).reshape(-1, model_width)
    memory_norm = normalize(memory_side.astype(jnp.float32)).astype(jnp.bfloat16).reshape(-1, model_width)
    queries = jnp.dot(query_norm, attn_query, preferred_element_type=jnp.float32).astype(jnp.bfloat16)
    queries = queries.reshape(pair_count, tok_count, head_count, HEAD_DIM)
    keyvals = jnp.dot(memory_norm, attn_keyval, preferred_element_type=jnp.float32).astype(jnp.bfloat16)
    keyvals = keyvals.reshape(pair_count, tok_count, 2, head_count, HEAD_DIM)
    scores = jnp.einsum('bqhd,bkhd->bhqk', queries.astype(jnp.float32), keyvals[:, :, 0].astype(jnp.float32))
    scores = scores / jnp.sqrt(jnp.float32(HEAD_DIM))
    scores = scores - lax.optimization_barrier(jnp.max(scores, axis=-1, keepdims=True))
    expd = jnp.exp(scores)
    attention = (expd / lax.optimization_barrier(jnp.sum(expd, axis=-1, keepdims=True))).astype(jnp.bfloat16)
    attended = jnp.einsum('bhqk,bkhd->bqhd', attention.astype(jnp.float32), keyvals[:, :, 1].astype(jnp.float32))
    attended = attended.astype(jnp.bfloat16).reshape(-1, model_width)
    hidden = query_side.astype(jnp.float32).reshape(-1, model_width) + jnp.dot(attended, attn_output, preferred_element_type=jnp.float32)
    hidden_norm = normalize(hidden).astype(jnp.bfloat16)
    expanded = jax.nn.gelu(jnp.dot(hidden_norm, mlp_up, preferred_element_type=jnp.float32), approximate=False).astype(jnp.bfloat16)
    output = hidden + jnp.dot(expanded, mlp_down, preferred_element_type=jnp.float32)
    output = output.reshape(pair_count, tok_count, model_width)
    return (confidence[:, None, None] * output).astype(jnp.bfloat16)

def reference(tokens, proj_in, attn_query, attn_keyval, attn_output, mlp_up, mlp_down, pair_list, conf_level, conf_table):
    projected = jnp.dot(tokens.reshape(-1, E), proj_in, preferred_element_type=jnp.float32).astype(jnp.bfloat16)
    projected = projected.reshape(IMAGES, TOK, D)
    confidence = conf_table[conf_level]

    def add_block(image_sums, block):
        pair_block, conf_block = block
        features = pair_features(projected[pair_block[:, 0]], projected[pair_block[:, 1]], attn_query, attn_keyval, attn_output, mlp_up, mlp_down, conf_block).astype(jnp.float32)
        image_sums = image_sums.at[pair_block[:, 0]].add(features)
        image_sums = image_sums.at[pair_block[:, 1]].add(features)
        return (image_sums, None)
    image_sums = jnp.zeros((IMAGES, TOK, D), jnp.float32)
    image_sums, unused = lax.scan(add_block, image_sums, (pair_list.reshape(-1, PAIR_DEV, 2), confidence.reshape(-1, PAIR_DEV)))
    return image_sums.astype(jnp.bfloat16)
```

```python
import jax
import jax.numpy as jnp
from jax import lax
from jax.experimental import pallas as pl
from jax.experimental.pallas import tpu as pltpu
from jax.sharding import PartitionSpec as P

HEAD_DIM = 64
TOK = 24
IMG_DEV = 8
NX, NY, NZ = 4, 4, 8
BLK = IMG_DEV * TOK
SIDE = 4 * BLK
DEVS = NX * NY * NZ * 2
PAIR_DEV = 32
GROUP = 8
SLOTS = 64
MESH = pl.DeviceIdType.MESH
F32 = jnp.float32
BF16 = jnp.bfloat16


def place():
    img = lax.axis_index("img")
    return img // 8, (img // 2) % 4, img % 2, lax.axis_index("rep")


def dev(z, x, c, y):
    return ((z * NX + x) * 2 + c, y)


def remote(src, dst, send, recv, to):
    return pltpu.make_async_remote_copy(
        src_ref=src,
        dst_ref=dst,
        send_sem=send,
        recv_sem=recv,
        device_id=to,
        device_id_type=MESH,
    )


def peers_of(z, x, c, y):
    peers = []
    for d in range(1, 8):
        k = (x * 2 + c + d) % 8
        peers.append(dev(z, k // 2, k % 2, y))
    for d in range(1, NZ):
        peers.append(dev((z + d) % NZ, x, c, y))
    for d in range(1, NY):
        peers.append(dev(z, x, c, (y + d) % NY))
    return peers


def barrier_all(z, x, c, y):
    barrier = pltpu.get_barrier_semaphore()
    peers = peers_of(z, x, c, y)
    for p in peers:
        pl.semaphore_signal(barrier, inc=1, device_id=p, device_id_type=MESH)
    return barrier, len(peers)


def gather_kernel(
    tok_ref,
    proj_ref,
    mine_ref,
    a_out,
    b_out,
    list_out,
    own,
    a_send,
    a_recv,
    b_send,
    b_recv,
    f_send,
    f_recv,
    loc,
    lx_send,
    lx_recv,
    lz_send,
    lz_recv,
    ly_send,
    ly_recv,
):
    z, x, c, y = place()
    barrier, n_peers = barrier_all(z, x, c, y)
    me8 = x * 2 + c
    row0 = y * 64 + z * 8
    list_out[pl.ds(row0 + me8, 1)] = mine_ref[...]
    own[...] = jnp.dot(tok_ref[...], proj_ref[...], preferred_element_type=F32).astype(BF16)
    pl.semaphore_wait(barrier, n_peers)

    lx = []
    for d in range(1, 8):
        k = (me8 + d) % 8
        mine = list_out.at[pl.ds(row0 + me8, 1)]
        cp = remote(mine, mine, lx_send.at[d], lx_recv.at[d], dev(z, k // 2, k % 2, y))
        cp.start()
        lx.append(cp)

    s_b = (z // 4) * 2 + c
    b_dst = b_out.at[pl.ds(pl.multiple_of(s_b * BLK, BLK), BLK)]
    z0 = (z - y + NZ) % NZ
    z1 = (z - y + NZ + 4) % NZ
    self_b = y == 0
    b1 = remote(own, b_dst, b_send.at[1], b_recv.at[z // 4], dev(z1, x, c, y))
    b1.start()
    b0 = remote(own, b_dst, b_send.at[0], b_recv.at[z // 4], dev(z0, x, c, y))
    b0_local = pltpu.make_async_copy(own, b_dst, loc.at[0])

    @pl.when(jnp.logical_not(self_b))
    def _():
        b0.start()

    @pl.when(self_b)
    def _():
        b0_local.start()

    s_a = (x % 2) * 2 + c
    a_dst = a_out.at[pl.ds(pl.multiple_of(s_a * BLK, BLK), BLK)]
    half = x // 2
    self_a = half == c
    a_cps = []
    for d in (2, 1, 3):
        cp = remote(own, a_dst, a_send.at[d], a_recv.at[s_a], dev(z, (x + d) % NX, half, y))
        cp.start()
        a_cps.append(cp)
    a0 = remote(own, a_dst, a_send.at[0], a_recv.at[s_a], dev(z, x, half, y))
    a0_local = pltpu.make_async_copy(own, a_dst, loc.at[1])

    @pl.when(jnp.logical_not(self_a))
    def _():
        a0.start()

    @pl.when(self_a)
    def _():
        a0_local.start()

    for cp in lx:
        cp.wait_recv()
    lz = []
    for d in range(1, NZ):
        rows = list_out.at[pl.ds(row0, 8)]
        cp = remote(rows, rows, lz_send.at[d], lz_recv.at[d], dev((z + d) % NZ, x, c, y))
        cp.start()
        lz.append(cp)
    for cp in lz:
        cp.wait_recv()
    ly = []
    for d in range(1, NY):
        rows = list_out.at[pl.ds(y * 64, 64)]
        cp = remote(rows, rows, ly_send.at[d], ly_recv.at[d], dev(z, x, c, (y + d) % NY))
        cp.start()
        ly.append(cp)

    sib = dev(z, x, 1 - c, y)
    fwd = []
    for t in range(2):
        slot = b_out.at[pl.ds(pl.multiple_of((t * 2 + c) * BLK, BLK), BLK)]
        arrived = remote(own, slot, b_send.at[t], b_recv.at[t], sib)
        here = jnp.logical_and(self_b, z // 4 == t)

        @pl.when(jnp.logical_not(here))
        def _(arrived=arrived):
            arrived.wait_recv()

        @pl.when(here)
        def _():
            b0_local.wait()

        cp = remote(slot, slot, f_send.at[t], f_recv.at[t], sib)
        cp.start()
        fwd.append(cp)

    for s in range(4):
        slot = a_out.at[pl.ds(s * BLK, BLK)]
        arrived = remote(own, slot, a_send.at[0], a_recv.at[s], sib)
        here = jnp.logical_and(self_a, s_a == s)

        @pl.when(jnp.logical_not(here))
        def _(arrived=arrived):
            arrived.wait_recv()

        @pl.when(here)
        def _():
            a0_local.wait()

    for t in range(2):
        slot = b_out.at[pl.ds(pl.multiple_of((t * 2 + 1 - c) * BLK, BLK), BLK)]
        remote(slot, slot, f_send.at[t], f_recv.at[t], sib).wait_recv()
    for cp in ly:
        cp.wait_recv()

    for cp in lx + lz + ly + a_cps + fwd + [b1]:
        cp.wait_send()

    @pl.when(jnp.logical_not(self_b))
    def _():
        b0.wait_send()

    @pl.when(jnp.logical_not(self_a))
    def _():
        a0.wait_send()


def gather(tokens, proj_in, mine):
    width = proj_in.shape[1]
    dma = pltpu.SemaphoreType.DMA
    vmem = pl.BlockSpec(memory_space=pltpu.VMEM)
    anym = pl.BlockSpec(memory_space=pl.ANY)
    return pl.pallas_call(
        gather_kernel,
        out_shape=(
            jax.ShapeDtypeStruct((SIDE, width), BF16),
            jax.ShapeDtypeStruct((SIDE, width), BF16),
            jax.ShapeDtypeStruct((DEVS, 1, 128), jnp.int32),
        ),
        in_specs=[vmem] * 3,
        out_specs=(anym, anym, vmem),
        scratch_shapes=[
            pltpu.VMEM((BLK, width), BF16),
            dma((4,)),
            dma((4,)),
            dma((2,)),
            dma((2,)),
            dma((2,)),
            dma((2,)),
            dma((2,)),
            dma((8,)),
            dma((8,)),
            dma((8,)),
            dma((8,)),
            dma((4,)),
            dma((4,)),
        ],
        compiler_params=pltpu.CompilerParams(
            collective_id=0, has_side_effects=True, vmem_limit_bytes=32 * 1024 * 1024
        ),
        name="gather_blocks",
    )(tokens, proj_in, mine)


def norm(v):
    centred = v - jnp.mean(v, axis=-1, keepdims=True)
    spread = jnp.mean(centred * centred, axis=-1, keepdims=True)
    return centred * lax.rsqrt(spread + 1e-06)


def cell_kernel(
    ids_ref,
    table_ref,
    list_ref,
    a_ref,
    b_ref,
    wq_hbm,
    wkv_hbm,
    wo_hbm,
    up_hbm,
    down_hbm,
    pa_ref,
    pb_ref,
    wq,
    wkv,
    wo,
    up,
    down,
    side,
    qs,
    ks,
    vs,
    acc_a,
    acc_b,
    rank_t,
    val_t,
    slots_v,
    slots_s,
    att,
    ffn,
    sems,
):
    width = wq.shape[0]
    heads_quad = 4
    quad = heads_quad * HEAD_DIM
    copies = [
        pltpu.make_async_copy(h, v, sems.at[i])
        for i, (h, v) in enumerate(
            ((wq_hbm, wq), (wkv_hbm, wkv), (wo_hbm, wo), (up_hbm, up), (down_hbm, down))
        )
    ]
    for cp in copies:
        cp.start()

    a_id, b_x, b_j = ids_ref[0], ids_ref[1], ids_ref[2]
    flat = list_ref[...].reshape(DEVS, 128)
    flat_t = flat.astype(F32).T.astype(jnp.int32)
    a_img = flat_t[:PAIR_DEV]
    b_img = flat_t[PAIR_DEV : 2 * PAIR_DEV]
    level = flat_t[2 * PAIR_DEV : 3 * PAIR_DEV]
    hit = (
        (lax.shift_right_logical(a_img, 5) == a_id)
        & ((lax.shift_right_logical(b_img, 4) & 3) == b_x)
        & ((lax.shift_right_logical(b_img, 6) & 3) == b_j)
    )
    hit_f = hit.astype(F32)
    r_i = lax.broadcasted_iota(jnp.int32, (DEVS, DEVS), 0)
    c_i = lax.broadcasted_iota(jnp.int32, (DEVS, DEVS), 1)
    upper = (r_i <= c_i).astype(BF16)
    across = jnp.dot(hit_f.astype(BF16), upper, preferred_element_type=F32)
    totals = across[:, DEVS - 1 : DEVS]
    k_r = lax.broadcasted_iota(jnp.int32, (PAIR_DEV, PAIR_DEV), 0)
    k_c = lax.broadcasted_iota(jnp.int32, (PAIR_DEV, PAIR_DEV), 1)
    lower = (k_c < k_r).astype(BF16)
    before = jnp.dot(
        lower,
        jnp.broadcast_to(totals, (PAIR_DEV, 128)).astype(BF16),
        preferred_element_type=F32,
    )[:, :1]
    rank = (across + before).astype(jnp.int32) - 1
    rank_t[...] = jnp.where(hit, rank, -1)
    val_t[...] = ((a_img & 31) * 32 + (lax.shift_right_logical(b_img, 8) * 16 + (b_img & 15))) * 16 + level
    count = jnp.sum(hit_f).astype(jnp.int32)

    acc_a[...] = jnp.zeros_like(acc_a)
    acc_b[...] = jnp.zeros_like(acc_b)

    copies[0].wait()
    copies[1].wait()
    for i in range(4):
        rows = pl.ds(i * BLK, BLK)
        q_side = a_ref[rows, :].astype(F32)
        side[pl.ds(i * IMG_DEV, IMG_DEV)] = q_side.reshape(IMG_DEV, TOK, width)
        qn = norm(q_side).astype(BF16)
        q = jnp.dot(qn, wq[...], preferred_element_type=F32).astype(BF16).astype(F32)
        qs[pl.ds(i * IMG_DEV, IMG_DEV)] = (q * (HEAD_DIM**-0.5)).reshape(IMG_DEV, TOK, width)
        mn = norm(b_ref[rows, :].astype(F32)).astype(BF16)
        k = jnp.dot(mn, wkv[:, :width], preferred_element_type=F32)
        ks[pl.ds(i * IMG_DEV, IMG_DEV)] = k.reshape(IMG_DEV, TOK, width)
        v = jnp.dot(mn, wkv[:, width:], preferred_element_type=F32)
        vs[pl.ds(i * IMG_DEV, IMG_DEV)] = v.reshape(IMG_DEV, TOK, width)
    for cp in copies[2:]:
        cp.wait()

    lane_head = lax.broadcasted_iota(jnp.int32, (TOK, quad), 1) // HEAD_DIM

    def attend(a_loc, b_loc):
        out = []
        for p in range(width // quad):
            cols = slice(p * quad, (p + 1) * quad)
            q = qs[a_loc, :, cols]
            k = ks[b_loc, :, cols].astype(BF16)
            v = vs[b_loc, :, cols].astype(BF16)
            q4 = jnp.concatenate(
                [jnp.where(lane_head == h, q, 0.0) for h in range(heads_quad)], axis=0
            ).astype(BF16)
            s = lax.dot_general(q4, k, (((1,), (1,)), ((), ())), preferred_element_type=F32)
            e = jnp.exp(s - jnp.max(s, axis=-1, keepdims=True))
            probs = (e / jnp.sum(e, axis=-1, keepdims=True)).astype(BF16)
            r = jnp.dot(probs, v, preferred_element_type=F32)
            o = r[3 * TOK :]
            for h in (2, 1, 0):
                o = jnp.where(lane_head == h, r[h * TOK : (h + 1) * TOK], o)
            out.append(o)
        return jnp.concatenate(out, axis=1)

    def slot_block(block, carry):
        base = block * SLOTS
        slot = lax.broadcasted_iota(jnp.int32, (SLOTS, DEVS), 0) + base
        found = jnp.zeros((SLOTS, DEVS), jnp.int32)
        for k in range(PAIR_DEV):
            found += jnp.where(rank_t[k : k + 1, :] == slot, val_t[k : k + 1, :], 0)
        col = jnp.sum(found.astype(F32), axis=1, keepdims=True).astype(jnp.int32)
        slots_v[...] = jnp.broadcast_to(col, (SLOTS, 128))
        cp = pltpu.make_async_copy(slots_v, slots_s, sems.at[5])
        cp.start()
        cp.wait()
        here = jnp.minimum(count - base, SLOTS)

        def group(g, carry2):
            locs = []
            for i in range(GROUP):
                word = slots_s[g * GROUP + i, 0]
                a_loc = word // 512
                b_loc = (word // 16) % 32
                locs.append((a_loc, b_loc, word % 16))
                att[pl.ds(i * TOK, TOK), :] = attend(a_loc, b_loc)
            query = jnp.concatenate([side[a_loc] for a_loc, _, _ in locs], axis=0)
            hidden = query + jnp.dot(
                att[...].astype(BF16), wo[...], preferred_element_type=F32
            )
            hn = norm(hidden).astype(BF16)
            u = jnp.dot(hn, up[...], preferred_element_type=F32)
            ex = (0.5 * u) * (1.0 + lax.erf(u * (0.5**0.5)))
            out = hidden + jnp.dot(ex.astype(BF16), down[...], preferred_element_type=F32)
            ffn[...] = out
            for i in range(GROUP):
                a_loc, b_loc, lev = locs[i]

                @pl.when(g * GROUP + i < here)
                def _(i=i, a_loc=a_loc, b_loc=b_loc, lev=lev):
                    feature = table_ref[lev] * ffn[pl.ds(i * TOK, TOK), :]
                    feature = feature.astype(BF16).astype(F32)
                    acc_a[a_loc] = acc_a[a_loc] + feature
                    acc_b[b_loc] = acc_b[b_loc] + feature

            return carry2

        lax.fori_loop(0, (here + GROUP - 1) // GROUP, group, 0)
        return carry

    lax.fori_loop(0, (count + SLOTS - 1) // SLOTS, slot_block, 0)
    pa_ref[...] = acc_a[...].reshape(SIDE, width).astype(BF16)
    pb_ref[...] = acc_b[...].reshape(SIDE, width).astype(BF16)


def cell(ids, table, pairs, a_blk, b_blk, wq, wkv, wo, up, down, interpret=False):
    width, ff = up.shape
    vmem = pl.BlockSpec(memory_space=pltpu.VMEM)
    smem = pl.BlockSpec(memory_space=pltpu.SMEM)
    anym = pl.BlockSpec(memory_space=pl.ANY)
    images = 4 * IMG_DEV
    return pl.pallas_call(
        cell_kernel,
        out_shape=(
            jax.ShapeDtypeStruct((SIDE, width), BF16),
            jax.ShapeDtypeStruct((SIDE, width), BF16),
        ),
        in_specs=[smem, smem, vmem, vmem, vmem] + [anym] * 5,
        out_specs=(vmem, vmem),
        scratch_shapes=[
            pltpu.VMEM((width, width), BF16),
            pltpu.VMEM((width, 2 * width), BF16),
            pltpu.VMEM((width, width), BF16),
            pltpu.VMEM((width, ff), BF16),
            pltpu.VMEM((ff, width), BF16),
            pltpu.VMEM((images, TOK, width), F32),
            pltpu.VMEM((images, TOK, width), F32),
            pltpu.VMEM((images, TOK, width), F32),
            pltpu.VMEM((images, TOK, width), F32),
            pltpu.VMEM((images, TOK, width), F32),
            pltpu.VMEM((images, TOK, width), F32),
            pltpu.VMEM((PAIR_DEV, DEVS), jnp.int32),
            pltpu.VMEM((PAIR_DEV, DEVS), jnp.int32),
            pltpu.VMEM((SLOTS, 128), jnp.int32),
            pltpu.SMEM((SLOTS, 128), jnp.int32),
            pltpu.VMEM((GROUP * TOK, width), F32),
            pltpu.VMEM((GROUP * TOK, width), F32),
            pltpu.SemaphoreType.DMA((6,)),
        ],
        compiler_params=pltpu.CompilerParams(vmem_limit_bytes=52 * 1024 * 1024),
        name="cell_pairs",
        interpret=interpret,
    )(ids, table, pairs, a_blk, b_blk, wq, wkv, wo, up, down)


def reduce_kernel(
    pa_ref,
    pb_ref,
    out_ref,
    ra,
    rsib,
    sb,
    rz,
    tot,
    ry,
    a_send,
    a_recv,
    s_send,
    s_recv,
    z_send,
    z_recv,
    y_send,
    y_recv,
    o_send,
    o_recv,
):
    z, x, c, y = place()
    barrier, n_peers = barrier_all(z, x, c, y)
    pl.semaphore_wait(barrier, n_peers)
    sib = dev(z, x, 1 - c, y)

    def rows(s):
        return pl.ds(pl.multiple_of(s * BLK, BLK), BLK)

    sib_cps = []
    for t in range(2):
        cp = remote(pb_ref.at[rows(t * 2 + 1 - c)], rsib.at[t], s_send.at[t], s_recv.at[t], sib)
        cp.start()
        sib_cps.append(cp)

    a_cps = []
    for s in range(4):
        xt = 2 * c + s // 2
        here = jnp.logical_and(xt == x, c == s % 2)
        cp = remote(pa_ref.at[rows(s)], ra.at[x], a_send.at[s], a_recv.at[x], dev(z, xt, s % 2, y))
        a_cps.append((here, cp))

        @pl.when(jnp.logical_not(here))
        def _(cp=cp):
            cp.start()

        @pl.when(here)
        def _(s=s):
            ra[x] = pa_ref[rows(s), :]

    j = (z + y) % 4
    z_cps = []
    for t in range(2):
        sib_cps[t].wait_recv()
        total = pb_ref[rows(t * 2 + c), :].astype(F32) + rsib[t].astype(F32)
        sb[t] = total.astype(BF16)
        zt = j + 4 * t
        here = zt == z
        cp = remote(sb.at[t], rz.at[z // 4], z_send.at[t], z_recv.at[z // 4], dev(zt, x, c, y))
        z_cps.append((here, cp))

        @pl.when(jnp.logical_not(here))
        def _(cp=cp):
            cp.start()

        @pl.when(here)
        def _(t=t):
            rz[t] = sb[t]

    for s in range(4):
        here = jnp.logical_and(s == x, x // 2 == c)

        @pl.when(jnp.logical_not(here))
        def _(s=s):
            remote(pa_ref.at[rows(0)], ra.at[s], a_send.at[0], a_recv.at[s], sib).wait_recv()

    total = ra[0].astype(F32) + ra[1].astype(F32) + ra[2].astype(F32) + ra[3].astype(F32)
    for t in range(2):
        here = jnp.logical_and(y == 0, z // 4 == t)

        @pl.when(jnp.logical_not(here))
        def _(t=t):
            remote(sb.at[t], rz.at[t], z_send.at[0], z_recv.at[t], sib).wait_recv()

    tot[...] = (total + rz[0].astype(F32) + rz[1].astype(F32)).astype(BF16)

    part = BLK // NY

    def y_rows(yy):
        return pl.ds(pl.multiple_of(yy * part, part), part)

    y_cps = []
    for d in range(1, NY):
        yt = (y + d) % NY
        cp = remote(tot.at[y_rows(yt)], ry.at[d], y_send.at[d], y_recv.at[d], dev(z, x, c, yt))
        cp.start()
        y_cps.append(cp)
    mine = tot[y_rows(y), :].astype(F32)
    for d in range(1, NY):
        y_cps[d - 1].wait_recv()
        mine = mine + ry[d].astype(F32)
    out_ref[y_rows(y), :] = mine.astype(BF16)
    o_cps = []
    for d in range(1, NY):
        yt = (y + d) % NY
        piece = out_ref.at[y_rows(y)]
        cp = remote(piece, piece, o_send.at[d], o_recv.at[d], dev(z, x, c, yt))
        cp.start()
        o_cps.append(cp)
    for d in range(1, NY):
        piece = out_ref.at[y_rows((y - d + NY) % NY)]
        remote(piece, piece, o_send.at[d], o_recv.at[d], sib).wait_recv()

    for cp in sib_cps + y_cps + o_cps:
        cp.wait_send()
    for here, cp in a_cps + z_cps:

        @pl.when(jnp.logical_not(here))
        def _(cp=cp):
            cp.wait_send()


def reduce_back(pa, pb):
    width = pa.shape[1]
    dma = pltpu.SemaphoreType.DMA
    vmem = pl.BlockSpec(memory_space=pltpu.VMEM)
    return pl.pallas_call(
        reduce_kernel,
        out_shape=jax.ShapeDtypeStruct((BLK, width), BF16),
        in_specs=[vmem] * 2,
        out_specs=vmem,
        scratch_shapes=[
            pltpu.VMEM((4, BLK, width), BF16),
            pltpu.VMEM((2, BLK, width), BF16),
            pltpu.VMEM((2, BLK, width), BF16),
            pltpu.VMEM((2, BLK, width), BF16),
            pltpu.VMEM((BLK, width), BF16),
            pltpu.VMEM((NY, BLK // NY, width), BF16),
            dma((4,)),
            dma((4,)),
            dma((2,)),
            dma((2,)),
            dma((2,)),
            dma((2,)),
            dma((4,)),
            dma((4,)),
            dma((4,)),
            dma((4,)),
        ],
        compiler_params=pltpu.CompilerParams(
            collective_id=1, has_side_effects=True, vmem_limit_bytes=32 * 1024 * 1024
        ),
        name="reduce_back",
    )(pa, pb)


def body(
    tokens,
    proj_in,
    attn_query,
    attn_keyval,
    attn_output,
    mlp_up,
    mlp_down,
    pair_list,
    conf_level,
    conf_table,
):
    img_dev, tok_count, enc_width = tokens.shape
    z, x, c, y = place()
    mine = jnp.concatenate(
        [pair_list[:, 0], pair_list[:, 1], conf_level, jnp.zeros((PAIR_DEV,), jnp.int32)]
    ).reshape(1, 1, 128)
    a_blk, b_blk, pairs = gather(tokens.reshape(img_dev * tok_count, enc_width), proj_in, mine)
    ids = jnp.stack([z * 2 + c, x, (z + y) % 4, 0]).astype(jnp.int32)
    pa, pb = cell(
        ids, conf_table, pairs, a_blk, b_blk, attn_query, attn_keyval, attn_output, mlp_up, mlp_down
    )
    joined = reduce_back(pa, pb)
    return joined.reshape(img_dev, tok_count, joined.shape[1])


def solution(mesh):
    placed = (
        P("img", None, None),
        P(),
        P(),
        P(),
        P(),
        P(),
        P(),
        P(("img", "rep"), None),
        P(("img", "rep")),
        P(),
    )
    return jax.shard_map(
        body, mesh=mesh, in_specs=placed, out_specs=P("img", None, None), check_vma=False
    )
```

```python
import jax
import jax.numpy as jnp
from jax import lax
from jax.experimental import pallas as pl
from jax.experimental.pallas import tpu as pltpu
from jax.sharding import PartitionSpec as P

HEAD_DIM = 64
TOK = 24
IMG_DEV = 8
NX, NY, NZ = 4, 4, 8
BLK = IMG_DEV * TOK
SIDE = 4 * BLK
DEVS = NX * NY * NZ * 2
PAIR_DEV = 32
GROUP = 8
SLOTS = 64
CHUNKS = 2
CHUNK = BLK // CHUNKS
MESH = pl.DeviceIdType.MESH
F32 = jnp.float32
BF16 = jnp.bfloat16


def place():
    img = lax.axis_index("img")
    return img // 8, (img // 2) % 4, img % 2, lax.axis_index("rep")


def dev(z, x, c, y):
    return ((z * NX + x) * 2 + c, y)


def remote(src, dst, send, recv, to):
    return pltpu.make_async_remote_copy(
        src_ref=src,
        dst_ref=dst,
        send_sem=send,
        recv_sem=recv,
        device_id=to,
        device_id_type=MESH,
    )


def peers_of(z, x, c, y):
    peers = []
    for d in range(1, 8):
        k = (x * 2 + c + d) % 8
        peers.append(dev(z, k // 2, k % 2, y))
    for d in range(1, NZ):
        peers.append(dev((z + d) % NZ, x, c, y))
    for d in range(1, NY):
        peers.append(dev(z, x, c, (y + d) % NY))
    return peers


def barrier_all(z, x, c, y):
    barrier = pltpu.get_barrier_semaphore()
    peers = peers_of(z, x, c, y)
    for p in peers:
        pl.semaphore_signal(barrier, inc=1, device_id=p, device_id_type=MESH)
    return barrier, len(peers)


def gather_kernel(
    tok_hbm,
    proj_hbm,
    pair_ref,
    level_ref,
    a_out,
    b_out,
    list_out,
    tok,
    proj,
    own,
    a_send,
    a_recv,
    b_send,
    b_recv,
    f_send,
    f_recv,
    loc,
    lx_send,
    lx_recv,
    lz_send,
    lz_recv,
    ly_send,
    ly_recv,
):
    z, x, c, y = place()
    tok_in = pltpu.make_async_copy(tok_hbm, tok, loc.at[2])
    proj_in = pltpu.make_async_copy(proj_hbm, proj, loc.at[3])
    tok_in.start()
    proj_in.start()
    barrier, n_peers = barrier_all(z, x, c, y)
    me8 = x * 2 + c
    row_me = y * 64 + me8 * 8 + z
    list_out[row_me, :, 0:PAIR_DEV] = pair_ref[0:1, :]
    list_out[row_me, :, PAIR_DEV : 2 * PAIR_DEV] = pair_ref[1:2, :]
    list_out[row_me, :, 2 * PAIR_DEV : 3 * PAIR_DEV] = level_ref[...]
    list_out[row_me, :, 3 * PAIR_DEV :] = jnp.zeros((1, 128 - 3 * PAIR_DEV), jnp.int32)
    pl.semaphore_wait(barrier, n_peers)

    lz = []
    for d in range(1, NZ):
        mine = list_out.at[pl.ds(row_me, 1)]
        cp = remote(mine, mine, lz_send.at[d], lz_recv.at[d], dev((z + d) % NZ, x, c, y))
        cp.start()
        lz.append(cp)
    tok_in.wait()
    proj_in.wait()
    own[...] = jnp.dot(tok[...], proj[...], preferred_element_type=F32).astype(BF16)

    s_b = (z // 4) * 2 + c
    b_dst = b_out.at[pl.ds(pl.multiple_of(s_b * BLK, BLK), BLK)]
    z0 = (z - y + NZ) % NZ
    z1 = (z - y + NZ + 4) % NZ
    self_b = y == 0
    b1 = remote(own, b_dst, b_send.at[1], b_recv.at[z // 4], dev(z1, x, c, y))
    b1.start()
    b0 = remote(own, b_dst, b_send.at[0], b_recv.at[z // 4], dev(z0, x, c, y))
    b0_local = pltpu.make_async_copy(own, b_dst, loc.at[0])

    @pl.when(jnp.logical_not(self_b))
    def _():
        b0.start()

    @pl.when(self_b)
    def _():
        b0_local.start()

    for cp in lz:
        cp.wait_recv()
    lx = []
    for d in range(1, 8):
        k = (me8 + d) % 8
        rows = list_out.at[pl.ds(y * 64 + me8 * 8, 8)]
        cp = remote(rows, rows, lx_send.at[d], lx_recv.at[d], dev(z, k // 2, k % 2, y))
        cp.start()
        lx.append(cp)

    s_a = (x % 2) * 2 + c
    a_dst = a_out.at[pl.ds(pl.multiple_of(s_a * BLK, BLK), BLK)]
    half = x // 2
    self_a = half == c
    a_cps = []
    for d in (2, 1, 3):
        cp = remote(own, a_dst, a_send.at[d], a_recv.at[s_a], dev(z, (x + d) % NX, half, y))
        cp.start()
        a_cps.append(cp)
    a0 = remote(own, a_dst, a_send.at[0], a_recv.at[s_a], dev(z, x, half, y))
    a0_local = pltpu.make_async_copy(own, a_dst, loc.at[1])

    @pl.when(jnp.logical_not(self_a))
    def _():
        a0.start()

    @pl.when(self_a)
    def _():
        a0_local.start()

    for cp in lx:
        cp.wait_recv()
    ly = []
    for d in range(1, NY):
        rows = list_out.at[pl.ds(y * 64, 64)]
        cp = remote(rows, rows, ly_send.at[d], ly_recv.at[d], dev(z, x, c, (y + d) % NY))
        cp.start()
        ly.append(cp)

    sib = dev(z, x, 1 - c, y)
    fwd = []
    for t in range(2):
        slot = b_out.at[pl.ds(pl.multiple_of((t * 2 + c) * BLK, BLK), BLK)]
        arrived = remote(own, slot, b_send.at[t], b_recv.at[t], sib)
        here = jnp.logical_and(self_b, z // 4 == t)

        @pl.when(jnp.logical_not(here))
        def _(arrived=arrived):
            arrived.wait_recv()

        @pl.when(here)
        def _():
            b0_local.wait()

        cp = remote(slot, slot, f_send.at[t], f_recv.at[t], sib)
        cp.start()
        fwd.append(cp)

    for s in range(4):
        slot = a_out.at[pl.ds(s * BLK, BLK)]
        arrived = remote(own, slot, a_send.at[0], a_recv.at[s], sib)
        here = jnp.logical_and(self_a, s_a == s)

        @pl.when(jnp.logical_not(here))
        def _(arrived=arrived):
            arrived.wait_recv()

        @pl.when(here)
        def _():
            a0_local.wait()

    for t in range(2):
        slot = b_out.at[pl.ds(pl.multiple_of((t * 2 + 1 - c) * BLK, BLK), BLK)]
        remote(slot, slot, f_send.at[t], f_recv.at[t], sib).wait_recv()
    for cp in ly:
        cp.wait_recv()

    for cp in lx + lz + ly + a_cps + fwd + [b1]:
        cp.wait_send()

    @pl.when(jnp.logical_not(self_b))
    def _():
        b0.wait_send()

    @pl.when(jnp.logical_not(self_a))
    def _():
        a0.wait_send()


def gather(tokens, proj_in, pairs_t, levels):
    width = proj_in.shape[1]
    dma = pltpu.SemaphoreType.DMA
    vmem = pl.BlockSpec(memory_space=pltpu.VMEM)
    anym = pl.BlockSpec(memory_space=pl.ANY)
    return pl.pallas_call(
        gather_kernel,
        out_shape=(
            jax.ShapeDtypeStruct((SIDE, width), BF16),
            jax.ShapeDtypeStruct((SIDE, width), BF16),
            jax.ShapeDtypeStruct((DEVS, 1, 128), jnp.int32),
        ),
        in_specs=[anym, anym, vmem, vmem],
        out_specs=(anym, anym, vmem),
        scratch_shapes=[
            pltpu.VMEM(tokens.shape, BF16),
            pltpu.VMEM(proj_in.shape, BF16),
            pltpu.VMEM((BLK, width), BF16),
            dma((4,)),
            dma((4,)),
            dma((2,)),
            dma((2,)),
            dma((2,)),
            dma((2,)),
            dma((4,)),
            dma((8,)),
            dma((8,)),
            dma((8,)),
            dma((8,)),
            dma((4,)),
            dma((4,)),
        ],
        compiler_params=pltpu.CompilerParams(
            collective_id=0, has_side_effects=True, vmem_limit_bytes=32 * 1024 * 1024
        ),
        name="gather_blocks",
    )(tokens, proj_in, pairs_t, levels)


def norm(v):
    centred = v - jnp.mean(v, axis=-1, keepdims=True)
    spread = jnp.mean(centred * centred, axis=-1, keepdims=True)
    return centred * lax.rsqrt(spread + 1e-06)


def cell_kernel(
    ids_ref,
    table_ref,
    list_ref,
    a_hbm,
    b_hbm,
    wq_hbm,
    wkv_hbm,
    wo_hbm,
    up_hbm,
    down_hbm,
    pa_ref,
    pb_ref,
    a_ref,
    b_ref,
    wq,
    wkv,
    wo,
    up,
    down,
    side,
    qs,
    ks,
    vs,
    acc_a,
    acc_b,
    rank_t,
    val_t,
    slots_v,
    slots_s,
    att,
    ffn,
    sems,
):
    width = wq.shape[0]
    heads_quad = 4
    quad = heads_quad * HEAD_DIM
    copies = [
        pltpu.make_async_copy(h, v, sems.at[i])
        for i, (h, v) in enumerate(
            (
                (a_hbm, a_ref),
                (wq_hbm, wq),
                (b_hbm, b_ref),
                (wkv_hbm, wkv),
                (wo_hbm, wo),
                (up_hbm, up),
                (down_hbm, down),
            )
        )
    ]
    for cp in copies:
        cp.start()

    a_id, b_x, b_j = ids_ref[0], ids_ref[1], ids_ref[2]
    flat = list_ref[...].reshape(DEVS, 128)
    flat_t = flat.astype(F32).T.astype(jnp.int32)
    a_img = flat_t[:PAIR_DEV]
    b_img = flat_t[PAIR_DEV : 2 * PAIR_DEV]
    level = flat_t[2 * PAIR_DEV : 3 * PAIR_DEV]
    hit = (
        (lax.shift_right_logical(a_img, 5) == a_id)
        & ((lax.shift_right_logical(b_img, 4) & 3) == b_x)
        & ((lax.shift_right_logical(b_img, 6) & 3) == b_j)
    )
    hit_f = hit.astype(F32)
    r_i = lax.broadcasted_iota(jnp.int32, (DEVS, DEVS), 0)
    c_i = lax.broadcasted_iota(jnp.int32, (DEVS, DEVS), 1)
    upper = (r_i <= c_i).astype(BF16)
    across = jnp.dot(hit_f.astype(BF16), upper, preferred_element_type=F32)
    totals = across[:, DEVS - 1 : DEVS]
    k_r = lax.broadcasted_iota(jnp.int32, (PAIR_DEV, PAIR_DEV), 0)
    k_c = lax.broadcasted_iota(jnp.int32, (PAIR_DEV, PAIR_DEV), 1)
    lower = (k_c < k_r).astype(BF16)
    before = jnp.dot(
        lower,
        jnp.broadcast_to(totals, (PAIR_DEV, 128)).astype(BF16),
        preferred_element_type=F32,
    )[:, :1]
    rank = (across + before).astype(jnp.int32) - 1
    rank_t[...] = jnp.where(hit, rank, -1)
    val_t[...] = ((a_img & 31) * 32 + (lax.shift_right_logical(b_img, 8) * 16 + (b_img & 15))) * 16 + level
    count = jnp.sum(hit_f).astype(jnp.int32)

    acc_a[...] = jnp.zeros_like(acc_a)
    acc_b[...] = jnp.zeros_like(acc_b)

    for cp in copies[:4]:
        cp.wait()
    for i in range(4):
        rows = pl.ds(i * BLK, BLK)
        q_side = a_ref[rows, :].astype(F32)
        side[pl.ds(i * IMG_DEV, IMG_DEV)] = q_side.reshape(IMG_DEV, TOK, width)
        qn = norm(q_side).astype(BF16)
        q = jnp.dot(qn, wq[...], preferred_element_type=F32).astype(BF16).astype(F32)
        qs[pl.ds(i * IMG_DEV, IMG_DEV)] = (q * (HEAD_DIM**-0.5)).reshape(IMG_DEV, TOK, width)
        mn = norm(b_ref[rows, :].astype(F32)).astype(BF16)
        k = jnp.dot(mn, wkv[:, :width], preferred_element_type=F32)
        ks[pl.ds(i * IMG_DEV, IMG_DEV)] = k.reshape(IMG_DEV, TOK, width)
        v = jnp.dot(mn, wkv[:, width:], preferred_element_type=F32)
        vs[pl.ds(i * IMG_DEV, IMG_DEV)] = v.reshape(IMG_DEV, TOK, width)
    for cp in copies[4:]:
        cp.wait()

    lane_head = lax.broadcasted_iota(jnp.int32, (TOK, quad), 1) // HEAD_DIM

    def attend(a_loc, b_loc):
        out = []
        for p in range(width // quad):
            cols = slice(p * quad, (p + 1) * quad)
            q = qs[a_loc, :, cols]
            k = ks[b_loc, :, cols].astype(BF16)
            v = vs[b_loc, :, cols].astype(BF16)
            q4 = jnp.concatenate(
                [jnp.where(lane_head == h, q, 0.0) for h in range(heads_quad)], axis=0
            ).astype(BF16)
            s = lax.dot_general(k, q4, (((1,), (1,)), ((), ())), preferred_element_type=F32)
            e = jnp.exp(s - jnp.max(s, axis=0, keepdims=True))
            probs = (e / jnp.sum(e, axis=0, keepdims=True)).astype(BF16)
            r = lax.dot_general(probs, v, (((0,), (0,)), ((), ())), preferred_element_type=F32)
            o = r[3 * TOK :]
            for h in (2, 1, 0):
                o = jnp.where(lane_head == h, r[h * TOK : (h + 1) * TOK], o)
            out.append(o)
        return jnp.concatenate(out, axis=1)

    def slot_block(block, carry):
        base = block * SLOTS
        slot = lax.broadcasted_iota(jnp.int32, (SLOTS, DEVS), 0) + base
        found = jnp.zeros((SLOTS, DEVS), jnp.int32)
        for k in range(PAIR_DEV):
            found += jnp.where(rank_t[k : k + 1, :] == slot, val_t[k : k + 1, :], 0)
        col = jnp.sum(found.astype(F32), axis=1, keepdims=True).astype(jnp.int32)
        slots_v[...] = jnp.broadcast_to(col, (SLOTS, 128))
        cp = pltpu.make_async_copy(slots_v, slots_s, sems.at[7])
        cp.start()
        cp.wait()
        here = jnp.minimum(count - base, SLOTS)

        def group(g, carry2):
            locs = []
            for i in range(GROUP):
                word = slots_s[g * GROUP + i, 0]
                a_loc = word // 512
                b_loc = (word // 16) % 32
                locs.append((a_loc, b_loc, word % 16))
                att[pl.ds(i * TOK, TOK), :] = attend(a_loc, b_loc)
            query = jnp.concatenate([side[a_loc] for a_loc, _, _ in locs], axis=0)
            hidden = query + jnp.dot(
                att[...].astype(BF16), wo[...], preferred_element_type=F32
            )
            hn = norm(hidden).astype(BF16)
            u = jnp.dot(hn, up[...], preferred_element_type=F32)
            ex = (0.5 * u) * (1.0 + lax.erf(u * (0.5**0.5)))
            out = hidden + jnp.dot(ex.astype(BF16), down[...], preferred_element_type=F32)
            ffn[...] = out
            for i in range(GROUP):
                a_loc, b_loc, lev = locs[i]

                @pl.when(g * GROUP + i < here)
                def _(i=i, a_loc=a_loc, b_loc=b_loc, lev=lev):
                    feature = table_ref[lev] * ffn[pl.ds(i * TOK, TOK), :]
                    feature = feature.astype(BF16).astype(F32)
                    acc_a[a_loc] = acc_a[a_loc] + feature
                    acc_b[b_loc] = acc_b[b_loc] + feature

            return carry2

        lax.fori_loop(0, (here + GROUP - 1) // GROUP, group, 0)
        return carry

    lax.fori_loop(0, (count + SLOTS - 1) // SLOTS, slot_block, 0)
    pa_ref[...] = acc_a[...].reshape(SIDE, width).astype(BF16)
    pb_ref[...] = acc_b[...].reshape(SIDE, width).astype(BF16)


def cell(ids, table, pairs, a_blk, b_blk, wq, wkv, wo, up, down, interpret=False):
    width, ff = up.shape
    vmem = pl.BlockSpec(memory_space=pltpu.VMEM)
    smem = pl.BlockSpec(memory_space=pltpu.SMEM)
    anym = pl.BlockSpec(memory_space=pl.ANY)
    images = 4 * IMG_DEV
    return pl.pallas_call(
        cell_kernel,
        out_shape=(
            jax.ShapeDtypeStruct((SIDE, width), BF16),
            jax.ShapeDtypeStruct((SIDE, width), BF16),
        ),
        in_specs=[smem, smem, vmem] + [anym] * 7,
        out_specs=(vmem, vmem),
        scratch_shapes=[
            pltpu.VMEM((SIDE, width), BF16),
            pltpu.VMEM((SIDE, width), BF16),
            pltpu.VMEM((width, width), BF16),
            pltpu.VMEM((width, 2 * width), BF16),
            pltpu.VMEM((width, width), BF16),
            pltpu.VMEM((width, ff), BF16),
            pltpu.VMEM((ff, width), BF16),
            pltpu.VMEM((images, TOK, width), F32),
            pltpu.VMEM((images, TOK, width), F32),
            pltpu.VMEM((images, TOK, width), F32),
            pltpu.VMEM((images, TOK, width), F32),
            pltpu.VMEM((images, TOK, width), F32),
            pltpu.VMEM((images, TOK, width), F32),
            pltpu.VMEM((PAIR_DEV, DEVS), jnp.int32),
            pltpu.VMEM((PAIR_DEV, DEVS), jnp.int32),
            pltpu.VMEM((SLOTS, 128), jnp.int32),
            pltpu.SMEM((SLOTS, 128), jnp.int32),
            pltpu.VMEM((GROUP * TOK, width), F32),
            pltpu.VMEM((GROUP * TOK, width), F32),
            pltpu.SemaphoreType.DMA((8,)),
        ],
        compiler_params=pltpu.CompilerParams(vmem_limit_bytes=52 * 1024 * 1024),
        name="cell_pairs",
        interpret=interpret,
    )(ids, table, pairs, a_blk, b_blk, wq, wkv, wo, up, down)


def reduce_kernel(
    pa_hbm,
    pb_hbm,
    out_ref,
    pb,
    ra,
    rsib,
    sb,
    rz,
    tot,
    ry,
    loc,
    a_send,
    a_recv,
    s_send,
    s_recv,
    z_send,
    z_recv,
    y_send,
    y_recv,
    o_send,
    o_recv,
):
    z, x, c, y = place()

    def rows(s, h):
        return pl.ds(pl.multiple_of(s * BLK + h * CHUNK, CHUNK), CHUNK)

    def block(s):
        return pl.ds(pl.multiple_of(s * BLK, BLK), BLK)

    keep = []
    for t in range(2):
        cp = pltpu.make_async_copy(pb_hbm.at[block(t * 2 + c)], pb.at[t], loc.at[t])
        cp.start()
        keep.append(cp)
    self_a = x // 2 == c
    own_a = pltpu.make_async_copy(pa_hbm.at[block((x % 2) * 2 + c)], ra.at[x], loc.at[2])

    @pl.when(self_a)
    def _():
        own_a.start()

    barrier, n_peers = barrier_all(z, x, c, y)
    pl.semaphore_wait(barrier, n_peers)
    sib = dev(z, x, 1 - c, y)

    sib_cps = {}
    for h in range(CHUNKS):
        for t in range(2):
            i = h * 2 + t
            sib_cps[i] = remote(
                pb_hbm.at[rows(t * 2 + 1 - c, h)],
                rsib.at[t, pl.ds(h * CHUNK, CHUNK)],
                s_send.at[i],
                s_recv.at[i],
                sib,
            )
            sib_cps[i].start()

    a_cps = []
    for h in range(CHUNKS):
        for s in range(4):
            xt = 2 * c + s // 2
            here = jnp.logical_and(xt == x, c == s % 2)
            cp = remote(
                pa_hbm.at[rows(s, h)],
                ra.at[x, pl.ds(h * CHUNK, CHUNK)],
                a_send.at[h * 4 + s],
                a_recv.at[h * 4 + x],
                dev(z, xt, s % 2, y),
            )
            a_cps.append((here, cp))

            @pl.when(jnp.logical_not(here))
            def _(cp=cp):
                cp.start()

    j = (z + y) % 4
    z_cps = []
    for cp in keep:
        cp.wait()
    for h in range(CHUNKS):
        part = pl.ds(h * CHUNK, CHUNK)
        for t in range(2):
            sib_cps[h * 2 + t].wait_recv()
            total = pb[t, part].astype(F32) + rsib[t, part].astype(F32)
            sb[t, part] = total.astype(BF16)
            zt = j + 4 * t
            here = zt == z
            cp = remote(
                sb.at[t, part],
                rz.at[z // 4, part],
                z_send.at[h * 2 + t],
                z_recv.at[h * 2 + z // 4],
                dev(zt, x, c, y),
            )
            z_cps.append((here, cp))

            @pl.when(jnp.logical_not(here))
            def _(cp=cp):
                cp.start()

            @pl.when(here)
            def _(t=t, part=part):
                rz[t, part] = sb[t, part]

    @pl.when(self_a)
    def _():
        own_a.wait()

    share = BLK // NY

    def y_rows(yy):
        return pl.ds(pl.multiple_of(yy * share, share), share)

    for h in range(CHUNKS):
        part = pl.ds(h * CHUNK, CHUNK)
        for s in range(4):
            here = jnp.logical_and(s == x, self_a)

            @pl.when(jnp.logical_not(here))
            def _(s=s, part=part, h=h):
                remote(
                    pa_hbm.at[rows(0, 0)], ra.at[s, part], a_send.at[0], a_recv.at[h * 4 + s], sib
                ).wait_recv()

        total = (
            ra[0, part].astype(F32)
            + ra[1, part].astype(F32)
            + ra[2, part].astype(F32)
            + ra[3, part].astype(F32)
        )
        for t in range(2):
            here = jnp.logical_and(y == 0, z // 4 == t)

            @pl.when(jnp.logical_not(here))
            def _(t=t, part=part, h=h):
                remote(
                    sb.at[t, part], rz.at[t, part], z_send.at[0], z_recv.at[h * 2 + t], sib
                ).wait_recv()

        tot[part] = (total + rz[0, part].astype(F32) + rz[1, part].astype(F32)).astype(BF16)
        for d in range(1, NY):
            yt = (y + d) % NY

            @pl.when(yt * CHUNKS // NY == h)
            def _(d=d, yt=yt):
                remote(
                    tot.at[y_rows(yt)], ry.at[d], y_send.at[d], y_recv.at[d], dev(z, x, c, yt)
                ).start()

    y_cps = []
    for d in range(1, NY):
        yt = (y + d) % NY
        y_cps.append(
            remote(tot.at[y_rows(yt)], ry.at[d], y_send.at[d], y_recv.at[d], dev(z, x, c, yt))
        )
    mine = tot[y_rows(y), :].astype(F32)
    for d in range(1, NY):
        y_cps[d - 1].wait_recv()
        mine = mine + ry[d].astype(F32)
    out_ref[y_rows(y), :] = mine.astype(BF16)
    o_cps = []
    for d in range(1, NY):
        yt = (y + d) % NY
        piece = out_ref.at[y_rows(y)]
        cp = remote(piece, piece, o_send.at[d], o_recv.at[d], dev(z, x, c, yt))
        cp.start()
        o_cps.append(cp)
    for d in range(1, NY):
        piece = out_ref.at[y_rows((y - d + NY) % NY)]
        remote(piece, piece, o_send.at[d], o_recv.at[d], sib).wait_recv()

    for cp in list(sib_cps.values()) + y_cps + o_cps:
        cp.wait_send()
    for here, cp in a_cps + z_cps:

        @pl.when(jnp.logical_not(here))
        def _(cp=cp):
            cp.wait_send()


def reduce_back(pa, pb):
    width = pa.shape[1]
    dma = pltpu.SemaphoreType.DMA
    vmem = pl.BlockSpec(memory_space=pltpu.VMEM)
    return pl.pallas_call(
        reduce_kernel,
        out_shape=jax.ShapeDtypeStruct((BLK, width), BF16),
        in_specs=[pl.BlockSpec(memory_space=pl.ANY)] * 2,
        out_specs=vmem,
        scratch_shapes=[
            pltpu.VMEM((2, BLK, width), BF16),
            pltpu.VMEM((4, BLK, width), BF16),
            pltpu.VMEM((2, BLK, width), BF16),
            pltpu.VMEM((2, BLK, width), BF16),
            pltpu.VMEM((2, BLK, width), BF16),
            pltpu.VMEM((BLK, width), BF16),
            pltpu.VMEM((NY, BLK // NY, width), BF16),
            dma((3,)),
            dma((4 * CHUNKS,)),
            dma((4 * CHUNKS,)),
            dma((2 * CHUNKS,)),
            dma((2 * CHUNKS,)),
            dma((2 * CHUNKS,)),
            dma((2 * CHUNKS,)),
            dma((4,)),
            dma((4,)),
            dma((4,)),
            dma((4,)),
        ],
        compiler_params=pltpu.CompilerParams(
            collective_id=1, has_side_effects=True, vmem_limit_bytes=32 * 1024 * 1024
        ),
        name="reduce_back",
    )(pa, pb)


def body(
    tokens,
    proj_in,
    attn_query,
    attn_keyval,
    attn_output,
    mlp_up,
    mlp_down,
    pair_list,
    conf_level,
    conf_table,
):
    img_dev, tok_count, enc_width = tokens.shape
    z, x, c, y = place()
    a_blk, b_blk, pairs = gather(
        tokens.reshape(img_dev * tok_count, enc_width),
        proj_in,
        pair_list.T,
        conf_level.reshape(1, PAIR_DEV),
    )
    ids = jnp.stack([z * 2 + c, x, (z + y) % 4, 0]).astype(jnp.int32)
    pa, pb = cell(
        ids, conf_table, pairs, a_blk, b_blk, attn_query, attn_keyval, attn_output, mlp_up, mlp_down
    )
    joined = reduce_back(pa, pb)
    return joined.reshape(img_dev, tok_count, joined.shape[1])


def solution(mesh):
    placed = (
        P("img", None, None),
        P(),
        P(),
        P(),
        P(),
        P(),
        P(),
        P(("img", "rep"), None),
        P(("img", "rep")),
        P(),
    )
    return jax.shard_map(
        body, mesh=mesh, in_specs=placed, out_specs=P("img", None, None), check_vma=False
    )
```

```python
import jax
import jax.numpy as jnp
from jax import lax
from jax.experimental import pallas as pl
from jax.experimental.pallas import tpu as pltpu
from jax.sharding import PartitionSpec as P

HEAD_DIM = 64
TOK = 24
IMG_DEV = 8
NX, NY, NZ = 4, 4, 8
BLK = IMG_DEV * TOK
SIDE = 4 * BLK
DEVS = NX * NY * NZ * 2
PAIR_DEV = 32
GROUP = 16
HALF = 8
SLOTS = 64
CHUNKS = 2
CHUNK = BLK // CHUNKS
SHARE = BLK // NY
MESH = pl.DeviceIdType.MESH
F32 = jnp.float32
BF16 = jnp.bfloat16


def place():
    img = lax.axis_index("img")
    return img // 8, (img // 2) % 4, img % 2, lax.axis_index("rep")


def dev(z, x, c, y):
    return ((z * NX + x) * 2 + c, y)


def remote(src, dst, send, recv, to):
    return pltpu.make_async_remote_copy(
        src_ref=src,
        dst_ref=dst,
        send_sem=send,
        recv_sem=recv,
        device_id=to,
        device_id_type=MESH,
    )


def row_peers(z, x, c, y):
    ks = [(x * 2 + c + d) % 8 for d in range(1, 8)]
    return [dev(z, k // 2, k % 2, y) for k in ks]


def z_peers(z, x, c, y):
    return [dev((z + d) % NZ, x, c, y) for d in range(1, NZ)]


def y_peers(z, x, c, y):
    return [dev(z, x, c, (y + d) % NY) for d in range(1, NY)]


def barrier_all(z, x, c, y):
    barrier = pltpu.get_barrier_semaphore()
    peers = row_peers(z, x, c, y) + z_peers(z, x, c, y) + y_peers(z, x, c, y)
    for p in peers:
        pl.semaphore_signal(barrier, inc=1, device_id=p, device_id_type=MESH)
    return barrier, len(peers)


def gather_kernel(
    tok_hbm,
    proj_hbm,
    pair_ref,
    level_ref,
    a_out,
    b_out,
    list_out,
    tok,
    proj,
    own,
    a_send,
    a_recv,
    b_send,
    b_recv,
    f_send,
    f_recv,
    loc,
    lx_send,
    lx_recv,
    lz_send,
    lz_recv,
    ly_send,
    ly_recv,
):
    z, x, c, y = place()
    tok_in = pltpu.make_async_copy(tok_hbm, tok, loc.at[2])
    proj_in = pltpu.make_async_copy(proj_hbm, proj, loc.at[3])
    tok_in.start()
    proj_in.start()
    barrier, n_peers = barrier_all(z, x, c, y)
    me8 = x * 2 + c
    row_me = y * 64 + me8 * 8 + z
    list_out[row_me, :, 0:PAIR_DEV] = pair_ref[0:1, :]
    list_out[row_me, :, PAIR_DEV : 2 * PAIR_DEV] = pair_ref[1:2, :]
    list_out[row_me, :, 2 * PAIR_DEV : 3 * PAIR_DEV] = level_ref[...]
    list_out[row_me, :, 3 * PAIR_DEV :] = jnp.zeros((1, 128 - 3 * PAIR_DEV), jnp.int32)
    pl.semaphore_wait(barrier, n_peers)

    lz = []
    for d in range(1, NZ):
        mine = list_out.at[pl.ds(row_me, 1)]
        cp = remote(mine, mine, lz_send.at[d], lz_recv.at[d], dev((z + d) % NZ, x, c, y))
        cp.start()
        lz.append(cp)
    tok_in.wait()
    proj_in.wait()
    own[...] = jnp.dot(tok[...], proj[...], preferred_element_type=F32).astype(BF16)

    s_b = (z // 4) * 2 + c
    b_dst = b_out.at[pl.ds(pl.multiple_of(s_b * BLK, BLK), BLK)]
    z0 = (z - y + NZ) % NZ
    z1 = (z - y + NZ + 4) % NZ
    self_b = y == 0
    b1 = remote(own, b_dst, b_send.at[1], b_recv.at[z // 4], dev(z1, x, c, y))
    b1.start()
    b0 = remote(own, b_dst, b_send.at[0], b_recv.at[z // 4], dev(z0, x, c, y))
    b0_local = pltpu.make_async_copy(own, b_dst, loc.at[0])

    @pl.when(jnp.logical_not(self_b))
    def _():
        b0.start()

    @pl.when(self_b)
    def _():
        b0_local.start()

    for cp in lz:
        cp.wait_recv()
    lx = []
    for d in range(1, 8):
        k = (me8 + d) % 8
        rows = list_out.at[pl.ds(y * 64 + me8 * 8, 8)]
        cp = remote(rows, rows, lx_send.at[d], lx_recv.at[d], dev(z, k // 2, k % 2, y))
        cp.start()
        lx.append(cp)

    s_a = (x % 2) * 2 + c
    a_dst = a_out.at[pl.ds(pl.multiple_of(s_a * BLK, BLK), BLK)]
    half = x // 2
    self_a = half == c
    a_cps = []
    for d in (2, 1, 3):
        cp = remote(own, a_dst, a_send.at[d], a_recv.at[s_a], dev(z, (x + d) % NX, half, y))
        cp.start()
        a_cps.append(cp)
    a0 = remote(own, a_dst, a_send.at[0], a_recv.at[s_a], dev(z, x, half, y))
    a0_local = pltpu.make_async_copy(own, a_dst, loc.at[1])

    @pl.when(jnp.logical_not(self_a))
    def _():
        a0.start()

    @pl.when(self_a)
    def _():
        a0_local.start()

    for cp in lx:
        cp.wait_recv()
    ly = []
    for d in range(1, NY):
        rows = list_out.at[pl.ds(y * 64, 64)]
        cp = remote(rows, rows, ly_send.at[d], ly_recv.at[d], dev(z, x, c, (y + d) % NY))
        cp.start()
        ly.append(cp)

    sib = dev(z, x, 1 - c, y)
    fwd = []
    for t in range(2):
        slot = b_out.at[pl.ds(pl.multiple_of((t * 2 + c) * BLK, BLK), BLK)]
        arrived = remote(own, slot, b_send.at[t], b_recv.at[t], sib)
        here = jnp.logical_and(self_b, z // 4 == t)

        @pl.when(jnp.logical_not(here))
        def _(arrived=arrived):
            arrived.wait_recv()

        @pl.when(here)
        def _():
            b0_local.wait()

        cp = remote(slot, slot, f_send.at[t], f_recv.at[t], sib)
        cp.start()
        fwd.append(cp)

    for s in range(4):
        slot = a_out.at[pl.ds(s * BLK, BLK)]
        arrived = remote(own, slot, a_send.at[0], a_recv.at[s], sib)
        here = jnp.logical_and(self_a, s_a == s)

        @pl.when(jnp.logical_not(here))
        def _(arrived=arrived):
            arrived.wait_recv()

        @pl.when(here)
        def _():
            a0_local.wait()

    for t in range(2):
        slot = b_out.at[pl.ds(pl.multiple_of((t * 2 + 1 - c) * BLK, BLK), BLK)]
        remote(slot, slot, f_send.at[t], f_recv.at[t], sib).wait_recv()
    for cp in ly:
        cp.wait_recv()

    for cp in lx + lz + ly + a_cps + fwd + [b1]:
        cp.wait_send()

    @pl.when(jnp.logical_not(self_b))
    def _():
        b0.wait_send()

    @pl.when(jnp.logical_not(self_a))
    def _():
        a0.wait_send()


def gather(tokens, proj_in, pairs_t, levels):
    width = proj_in.shape[1]
    dma = pltpu.SemaphoreType.DMA
    vmem = pl.BlockSpec(memory_space=pltpu.VMEM)
    anym = pl.BlockSpec(memory_space=pltpu.HBM)
    return pl.pallas_call(
        gather_kernel,
        out_shape=(
            jax.ShapeDtypeStruct((SIDE, width), BF16),
            jax.ShapeDtypeStruct((SIDE, width), BF16),
            jax.ShapeDtypeStruct((DEVS, 1, 128), jnp.int32),
        ),
        in_specs=[anym, anym, vmem, vmem],
        out_specs=(anym, anym, vmem),
        scratch_shapes=[
            pltpu.VMEM(tokens.shape, BF16),
            pltpu.VMEM(proj_in.shape, BF16),
            pltpu.VMEM((BLK, width), BF16),
            dma((4,)),
            dma((4,)),
            dma((2,)),
            dma((2,)),
            dma((2,)),
            dma((2,)),
            dma((4,)),
            dma((8,)),
            dma((8,)),
            dma((8,)),
            dma((8,)),
            dma((4,)),
            dma((4,)),
        ],
        compiler_params=pltpu.CompilerParams(
            collective_id=0, has_side_effects=True, vmem_limit_bytes=32 * 1024 * 1024
        ),
        name="gather_blocks",
    )(tokens, proj_in, pairs_t, levels)


def norm(v):
    centred = v - jnp.mean(v, axis=-1, keepdims=True)
    spread = jnp.mean(centred * centred, axis=-1, keepdims=True)
    return centred * lax.rsqrt(spread + 1e-06)


def cell_kernel(
    ids_ref,
    table_ref,
    list_ref,
    a_hbm,
    b_hbm,
    wq_hbm,
    wkv_hbm,
    wo_hbm,
    up_hbm,
    down_hbm,
    pa_ref,
    pb_ref,
    a_ref,
    b_ref,
    wq,
    wkv,
    wo,
    up,
    down,
    side,
    qs,
    ks,
    vs,
    acc_a,
    acc_b,
    rank_t,
    val_t,
    slots_v,
    slots_s,
    att,
    ffn,
    sems,
):
    width = wq.shape[0]
    heads_quad = 4
    quad = heads_quad * HEAD_DIM
    copies = [
        pltpu.make_async_copy(h, v, sems.at[i])
        for i, (h, v) in enumerate(
            (
                (a_hbm, a_ref),
                (wq_hbm, wq),
                (b_hbm, b_ref),
                (wkv_hbm, wkv),
                (wo_hbm, wo),
                (up_hbm, up),
                (down_hbm, down),
            )
        )
    ]
    for cp in copies:
        cp.start()

    a_id, b_x, b_j = ids_ref[0], ids_ref[1], ids_ref[2]
    flat = list_ref[...].reshape(DEVS, 128)
    flat_t = flat.astype(F32).T.astype(jnp.int32)
    a_img = flat_t[:PAIR_DEV]
    b_img = flat_t[PAIR_DEV : 2 * PAIR_DEV]
    level = flat_t[2 * PAIR_DEV : 3 * PAIR_DEV]
    hit = (
        (lax.shift_right_logical(a_img, 5) == a_id)
        & ((lax.shift_right_logical(b_img, 4) & 3) == b_x)
        & ((lax.shift_right_logical(b_img, 6) & 3) == b_j)
    )
    hit_f = hit.astype(F32)
    r_i = lax.broadcasted_iota(jnp.int32, (DEVS, DEVS), 0)
    c_i = lax.broadcasted_iota(jnp.int32, (DEVS, DEVS), 1)
    upper = (r_i <= c_i).astype(BF16)
    across = jnp.dot(hit_f.astype(BF16), upper, preferred_element_type=F32)
    totals = across[:, DEVS - 1 : DEVS]
    k_r = lax.broadcasted_iota(jnp.int32, (PAIR_DEV, PAIR_DEV), 0)
    k_c = lax.broadcasted_iota(jnp.int32, (PAIR_DEV, PAIR_DEV), 1)
    lower = (k_c < k_r).astype(BF16)
    before = jnp.dot(
        lower,
        jnp.broadcast_to(totals, (PAIR_DEV, 128)).astype(BF16),
        preferred_element_type=F32,
    )[:, :1]
    rank = (across + before).astype(jnp.int32) - 1
    rank_t[...] = jnp.where(hit, rank, -1)
    val_t[...] = ((a_img & 31) * 32 + (lax.shift_right_logical(b_img, 8) * 16 + (b_img & 15))) * 16 + level
    count = jnp.sum(hit_f).astype(jnp.int32)

    def fetch_slots():
        return pltpu.make_async_copy(slots_v, slots_s, sems.at[7])

    def select(block):
        slot = lax.broadcasted_iota(jnp.int32, (SLOTS, DEVS), 0) + block * SLOTS
        found = jnp.zeros((SLOTS, DEVS), jnp.int32)
        for k in range(PAIR_DEV):
            found += jnp.where(rank_t[k : k + 1, :] == slot, val_t[k : k + 1, :], 0)
        col = jnp.sum(found.astype(F32), axis=1, keepdims=True).astype(jnp.int32)
        slots_v[...] = jnp.broadcast_to(col, (SLOTS, 128))
        fetch_slots().start()

    select(0)
    acc_a[...] = jnp.zeros_like(acc_a)
    acc_b[...] = jnp.zeros_like(acc_b)

    for cp in copies[:4]:
        cp.wait()
    for i in range(4):
        rows = pl.ds(i * BLK, BLK)
        q_side = a_ref[rows, :].astype(F32)
        side[pl.ds(i * IMG_DEV, IMG_DEV)] = q_side.reshape(IMG_DEV, TOK, width)
        qn = norm(q_side).astype(BF16)
        q = jnp.dot(qn, wq[...], preferred_element_type=F32).astype(BF16).astype(F32)
        qs[pl.ds(i * IMG_DEV, IMG_DEV)] = (q * (HEAD_DIM**-0.5)).reshape(IMG_DEV, TOK, width)
        mn = norm(b_ref[rows, :].astype(F32)).astype(BF16)
        k = jnp.dot(mn, wkv[:, :width], preferred_element_type=F32)
        ks[pl.ds(i * IMG_DEV, IMG_DEV)] = k.reshape(IMG_DEV, TOK, width)
        v = jnp.dot(mn, wkv[:, width:], preferred_element_type=F32)
        vs[pl.ds(i * IMG_DEV, IMG_DEV)] = v.reshape(IMG_DEV, TOK, width)
    for cp in copies[4:]:
        cp.wait()

    lane_head = lax.broadcasted_iota(jnp.int32, (TOK, quad), 1) // HEAD_DIM

    def attend(a_loc, b_loc):
        out = []
        for p in range(width // quad):
            cols = slice(p * quad, (p + 1) * quad)
            q = qs[a_loc, :, cols]
            k = ks[b_loc, :, cols].astype(BF16)
            v = vs[b_loc, :, cols].astype(BF16)
            q4 = jnp.concatenate(
                [jnp.where(lane_head == h, q, 0.0) for h in range(heads_quad)], axis=0
            ).astype(BF16)
            s = lax.dot_general(k, q4, (((1,), (1,)), ((), ())), preferred_element_type=F32)
            e = jnp.exp(s - jnp.max(s, axis=0, keepdims=True))
            probs = (e / jnp.sum(e, axis=0, keepdims=True)).astype(BF16)
            r = lax.dot_general(probs, v, (((0,), (0,)), ((), ())), preferred_element_type=F32)
            o = r[3 * TOK :]
            for h in (2, 1, 0):
                o = jnp.where(lane_head == h, r[h * TOK : (h + 1) * TOK], o)
            out.append(o)
        return jnp.concatenate(out, axis=1)

    def group(first, here, pairs_in):
        locs = []
        for i in range(pairs_in):
            word = slots_s[first + i, 0]
            a_loc = word // 512
            b_loc = (word // 16) % 32
            locs.append((a_loc, b_loc, word % 16))
            att[pl.ds(i * TOK, TOK), :] = attend(a_loc, b_loc)
        rows = pl.ds(0, pairs_in * TOK)
        query = jnp.concatenate([side[a_loc] for a_loc, _, _ in locs], axis=0)
        hidden = query + jnp.dot(att[rows, :].astype(BF16), wo[...], preferred_element_type=F32)
        hn = norm(hidden).astype(BF16)
        u = jnp.dot(hn, up[...], preferred_element_type=F32)
        ex = (0.5 * u) * (1.0 + lax.erf(u * (0.5**0.5)))
        ffn[rows, :] = hidden + jnp.dot(
            ex.astype(BF16), down[...], preferred_element_type=F32
        )
        for i in range(pairs_in):
            a_loc, b_loc, lev = locs[i]

            @pl.when(first + i < here)
            def _(i=i, a_loc=a_loc, b_loc=b_loc, lev=lev):
                feature = table_ref[lev] * ffn[pl.ds(i * TOK, TOK), :]
                feature = feature.astype(BF16).astype(F32)
                acc_a[a_loc] = acc_a[a_loc] + feature
                acc_b[b_loc] = acc_b[b_loc] + feature

    def slot_block(block, carry):
        here = jnp.minimum(count - block * SLOTS, SLOTS)
        wide = (here + GROUP - HALF - 1) // GROUP

        def wide_group(g, carry2):
            group(g * GROUP, here, GROUP)
            return carry2

        lax.fori_loop(0, wide, wide_group, 0)

        @pl.when(wide * GROUP < here)
        def _():
            group(wide * GROUP, here, HALF)

        @pl.when((block + 1) * SLOTS < count)
        def _():
            select(block + 1)
            fetch_slots().wait()

        return carry

    fetch_slots().wait()
    lax.fori_loop(0, (count + SLOTS - 1) // SLOTS, slot_block, 0)
    pa_ref[...] = acc_a[...].reshape(SIDE, width).astype(BF16)
    pb_ref[...] = acc_b[...].reshape(SIDE, width).astype(BF16)


def cell(ids, table, pairs, a_blk, b_blk, wq, wkv, wo, up, down, interpret=False):
    width, ff = up.shape
    vmem = pl.BlockSpec(memory_space=pltpu.VMEM)
    smem = pl.BlockSpec(memory_space=pltpu.SMEM)
    anym = pl.BlockSpec(memory_space=pltpu.HBM)
    images = 4 * IMG_DEV
    return pl.pallas_call(
        cell_kernel,
        out_shape=(
            jax.ShapeDtypeStruct((SIDE, width), BF16),
            jax.ShapeDtypeStruct((SIDE, width), BF16),
        ),
        in_specs=[smem, smem, vmem] + [anym] * 7,
        out_specs=(vmem, vmem),
        scratch_shapes=[
            pltpu.VMEM((SIDE, width), BF16),
            pltpu.VMEM((SIDE, width), BF16),
            pltpu.VMEM((width, width), BF16),
            pltpu.VMEM((width, 2 * width), BF16),
            pltpu.VMEM((width, width), BF16),
            pltpu.VMEM((width, ff), BF16),
            pltpu.VMEM((ff, width), BF16),
            pltpu.VMEM((images, TOK, width), F32),
            pltpu.VMEM((images, TOK, width), F32),
            pltpu.VMEM((images, TOK, width), F32),
            pltpu.VMEM((images, TOK, width), F32),
            pltpu.VMEM((images, TOK, width), F32),
            pltpu.VMEM((images, TOK, width), F32),
            pltpu.VMEM((PAIR_DEV, DEVS), jnp.int32),
            pltpu.VMEM((PAIR_DEV, DEVS), jnp.int32),
            pltpu.VMEM((SLOTS, 128), jnp.int32),
            pltpu.SMEM((SLOTS, 128), jnp.int32),
            pltpu.VMEM((GROUP * TOK, width), F32),
            pltpu.VMEM((GROUP * TOK, width), F32),
            pltpu.SemaphoreType.DMA((8,)),
        ],
        compiler_params=pltpu.CompilerParams(vmem_limit_bytes=52 * 1024 * 1024),
        name="cell_pairs",
        interpret=interpret,
    )(ids, table, pairs, a_blk, b_blk, wq, wkv, wo, up, down)


def reduce_kernel(
    pa_hbm,
    pb_hbm,
    out_ref,
    pb,
    ra,
    rsib,
    sb,
    rz,
    tot,
    ry,
    loc,
    a_send,
    a_recv,
    s_send,
    s_recv,
    z_send,
    z_recv,
    y_send,
    y_recv,
    o_send,
    o_recv,
):
    z, x, c, y = place()
    self_a = x // 2 == c
    self_b = y == 0

    def rows(s, h):
        return pl.ds(pl.multiple_of(s * BLK + h * CHUNK, CHUNK), CHUNK)

    def block(s):
        return pl.ds(pl.multiple_of(s * BLK, BLK), BLK)

    def y_rows(yy):
        return pl.ds(pl.multiple_of(yy * SHARE, SHARE), SHARE)

    keep = []
    for t in range(2):
        cp = pltpu.make_async_copy(pb_hbm.at[block(t * 2 + c)], pb.at[t], loc.at[t])
        cp.start()
        keep.append(cp)
    own_a = pltpu.make_async_copy(pa_hbm.at[block((x % 2) * 2 + c)], ra.at[x], loc.at[2])

    @pl.when(self_a)
    def _():
        own_a.start()

    barrier = pltpu.get_barrier_semaphore()
    for p in row_peers(z, x, c, y) + y_peers(z, x, c, y):
        pl.semaphore_signal(barrier, inc=1, device_id=p, device_id_type=MESH)
    for ys in range(NY):
        for zh in range(2):
            zs = (z + NZ - ys) % 4 + 4 * zh
            here = jnp.logical_and(ys == y, zs == z)

            @pl.when(jnp.logical_not(here))
            def _(zs=zs, ys=ys):
                pl.semaphore_signal(
                    barrier, inc=1, device_id=dev(zs, x, c, ys), device_id_type=MESH
                )

    pl.semaphore_wait(barrier, 7 + NY - 1 + 2 * NY - jnp.where(self_b, 1, 0))
    sib = dev(z, x, 1 - c, y)

    sib_cps = {}
    for h in range(CHUNKS):
        for t in range(2):
            i = h * 2 + t
            sib_cps[i] = remote(
                pb_hbm.at[rows(t * 2 + 1 - c, h)],
                rsib.at[t, pl.ds(h * CHUNK, CHUNK)],
                s_send.at[i],
                s_recv.at[i],
                sib,
            )
            sib_cps[i].start()

    a_cps = []
    for h in range(CHUNKS):
        for s in range(4):
            xt = 2 * c + s // 2
            here = jnp.logical_and(xt == x, c == s % 2)
            cp = remote(
                pa_hbm.at[rows(s, h)],
                ra.at[x, pl.ds(h * CHUNK, CHUNK)],
                a_send.at[h * 4 + s],
                a_recv.at[h * 4 + x],
                dev(z, xt, s % 2, y),
            )
            a_cps.append((here, cp))

            @pl.when(jnp.logical_not(here))
            def _(cp=cp):
                cp.start()

    j = (z + y) % 4
    z_cps = []
    slot = y * 2 + z // 4
    for cp in keep:
        cp.wait()
    for h in range(CHUNKS):
        part = pl.ds(h * CHUNK, CHUNK)
        for t in range(2):
            sib_cps[h * 2 + t].wait_recv()
            total = pb[t, part].astype(F32) + rsib[t, part].astype(F32)
            sb[t, part] = total.astype(BF16)
            zt = j + 4 * t
            for q in range(h * NY // CHUNKS, (h + 1) * NY // CHUNKS):
                piece = pl.ds(q * SHARE, SHARE)
                here = jnp.logical_and(zt == z, q == y)
                cp = remote(
                    sb.at[t, piece],
                    rz.at[slot],
                    z_send.at[q * 2 + t],
                    z_recv.at[slot],
                    dev(zt, x, c, q),
                )
                z_cps.append((here, cp))

                @pl.when(jnp.logical_not(here))
                def _(cp=cp):
                    cp.start()

                @pl.when(here)
                def _(t=t, piece=piece):
                    rz[slot] = sb[t, piece]

    @pl.when(self_a)
    def _():
        own_a.wait()

    for h in range(CHUNKS):
        part = pl.ds(h * CHUNK, CHUNK)
        for s in range(4):
            here = jnp.logical_and(s == x, self_a)

            @pl.when(jnp.logical_not(here))
            def _(s=s, part=part, h=h):
                remote(
                    pa_hbm.at[rows(0, 0)], ra.at[s, part], a_send.at[0], a_recv.at[h * 4 + s], sib
                ).wait_recv()

        total = (
            ra[0, part].astype(F32)
            + ra[1, part].astype(F32)
            + ra[2, part].astype(F32)
            + ra[3, part].astype(F32)
        )
        tot[part] = total.astype(BF16)
        for d in range(1, NY):
            yt = (y + d) % NY

            @pl.when(yt * CHUNKS // NY == h)
            def _(d=d, yt=yt):
                remote(
                    tot.at[y_rows(yt)], ry.at[d], y_send.at[d], y_recv.at[d], dev(z, x, c, yt)
                ).start()

    y_cps = []
    for d in range(1, NY):
        yt = (y + d) % NY
        y_cps.append(
            remote(tot.at[y_rows(yt)], ry.at[d], y_send.at[d], y_recv.at[d], dev(z, x, c, yt))
        )
    mine = tot[y_rows(y), :].astype(F32)
    for d in range(1, NY):
        y_cps[d - 1].wait_recv()
        mine = mine + ry[d].astype(F32)
    for ys in range(NY):
        for zh in range(2):
            s = ys * 2 + zh
            here = jnp.logical_and(jnp.logical_and(self_b, ys == 0), z // 4 == zh)

            @pl.when(jnp.logical_not(here))
            def _(s=s):
                remote(
                    sb.at[0, pl.ds(0, SHARE)], rz.at[s], z_send.at[0], z_recv.at[s], sib
                ).wait_recv()

    for s in range(2 * NY):
        mine = mine + rz[s].astype(F32)
    out_ref[y_rows(y), :] = mine.astype(BF16)
    o_cps = []
    for d in range(1, NY):
        yt = (y + d) % NY
        piece = out_ref.at[y_rows(y)]
        cp = remote(piece, piece, o_send.at[d], o_recv.at[d], dev(z, x, c, yt))
        cp.start()
        o_cps.append(cp)
    for d in range(1, NY):
        piece = out_ref.at[y_rows((y - d + NY) % NY)]
        remote(piece, piece, o_send.at[d], o_recv.at[d], sib).wait_recv()

    for cp in list(sib_cps.values()) + y_cps + o_cps:
        cp.wait_send()
    for here, cp in a_cps + z_cps:

        @pl.when(jnp.logical_not(here))
        def _(cp=cp):
            cp.wait_send()


def reduce_back(pa, pb):
    width = pa.shape[1]
    dma = pltpu.SemaphoreType.DMA
    vmem = pl.BlockSpec(memory_space=pltpu.VMEM)
    return pl.pallas_call(
        reduce_kernel,
        out_shape=jax.ShapeDtypeStruct((BLK, width), BF16),
        in_specs=[pl.BlockSpec(memory_space=pltpu.HBM)] * 2,
        out_specs=vmem,
        scratch_shapes=[
            pltpu.VMEM((2, BLK, width), BF16),
            pltpu.VMEM((4, BLK, width), BF16),
            pltpu.VMEM((2, BLK, width), BF16),
            pltpu.VMEM((2, BLK, width), BF16),
            pltpu.VMEM((2 * NY, SHARE, width), BF16),
            pltpu.VMEM((BLK, width), BF16),
            pltpu.VMEM((NY, SHARE, width), BF16),
            dma((3,)),
            dma((4 * CHUNKS,)),
            dma((4 * CHUNKS,)),
            dma((2 * CHUNKS,)),
            dma((2 * CHUNKS,)),
            dma((2 * NY,)),
            dma((2 * NY,)),
            dma((4,)),
            dma((4,)),
            dma((4,)),
            dma((4,)),
        ],
        compiler_params=pltpu.CompilerParams(
            collective_id=1, has_side_effects=True, vmem_limit_bytes=32 * 1024 * 1024
        ),
        name="reduce_back",
    )(pa, pb)


def body(
    tokens,
    proj_in,
    attn_query,
    attn_keyval,
    attn_output,
    mlp_up,
    mlp_down,
    pair_list,
    conf_level,
    conf_table,
):
    img_dev, tok_count, enc_width = tokens.shape
    z, x, c, y = place()
    a_blk, b_blk, pairs = gather(
        tokens.reshape(img_dev * tok_count, enc_width),
        proj_in,
        pair_list.T,
        conf_level.reshape(1, PAIR_DEV),
    )
    ids = jnp.stack([z * 2 + c, x, (z + y) % 4, 0]).astype(jnp.int32)
    pa, pb = cell(
        ids, conf_table, pairs, a_blk, b_blk, attn_query, attn_keyval, attn_output, mlp_up, mlp_down
    )
    joined = reduce_back(pa, pb)
    return joined.reshape(img_dev, tok_count, joined.shape[1])


def solution(mesh):
    placed = (
        P("img", None, None),
        P(),
        P(),
        P(),
        P(),
        P(),
        P(),
        P(("img", "rep"), None),
        P(("img", "rep")),
        P(),
    )
    return jax.shard_map(
        body, mesh=mesh, in_specs=placed, out_specs=P("img", None, None), check_vma=False
    )
```

```python
import jax
import jax.numpy as jnp
from jax import lax
from jax.experimental import pallas as pl
from jax.experimental.pallas import tpu as pltpu
from jax.sharding import PartitionSpec as P

HEAD_DIM = 64
TOK = 24
IMG_DEV = 8
NX, NY, NZ = 4, 4, 8
BLK = IMG_DEV * TOK
SIDE = 4 * BLK
DEVS = NX * NY * NZ * 2
PAIR_DEV = 32
GROUP = 16
HALF = 8
SLOTS = 64
PARTS = 2
VMEM_ALL = 64 * 1024 * 1024
SHARE = BLK // NY
MESH = pl.DeviceIdType.MESH
F32 = jnp.float32
BF16 = jnp.bfloat16


def place():
    img = lax.axis_index("img")
    return img // 8, (img // 2) % 4, img % 2, lax.axis_index("rep")


def dev(z, x, c, y):
    return ((z * NX + x) * 2 + c, y)


def remote(src, dst, send, recv, to):
    return pltpu.make_async_remote_copy(
        src_ref=src,
        dst_ref=dst,
        send_sem=send,
        recv_sem=recv,
        device_id=to,
        device_id_type=MESH,
    )


def row_peers(z, x, c, y):
    ks = [(x * 2 + c + d) % 8 for d in range(1, 8)]
    return [dev(z, k // 2, k % 2, y) for k in ks]


def z_peers(z, x, c, y):
    return [dev((z + d) % NZ, x, c, y) for d in range(1, NZ)]


def y_peers(z, x, c, y):
    return [dev(z, x, c, (y + d) % NY) for d in range(1, NY)]


def barrier_all(z, x, c, y):
    barrier = pltpu.get_barrier_semaphore()
    peers = row_peers(z, x, c, y) + z_peers(z, x, c, y) + y_peers(z, x, c, y)
    for p in peers:
        pl.semaphore_signal(barrier, inc=1, device_id=p, device_id_type=MESH)
    return barrier, len(peers)


def gather_kernel(
    tok_hbm,
    proj_hbm,
    pair_hbm,
    level_hbm,
    a_out,
    b_out,
    list_out,
    tok,
    proj,
    pair_ref,
    level_ref,
    own,
    a_send,
    a_recv,
    b_send,
    b_recv,
    f_send,
    f_recv,
    loc,
    lx_send,
    lx_recv,
    lz_send,
    lz_recv,
    ly_send,
    ly_recv,
):
    z, x, c, y = place()
    tok_in = pltpu.make_async_copy(tok_hbm, tok, loc.at[2])
    proj_in = pltpu.make_async_copy(proj_hbm, proj, loc.at[3])
    pair_in = pltpu.make_async_copy(pair_hbm, pair_ref, loc.at[4])
    level_in = pltpu.make_async_copy(level_hbm, level_ref, loc.at[5])
    inputs = (pair_in, level_in, tok_in, proj_in)
    for cp in inputs:
        cp.start()
    barrier, n_peers = barrier_all(z, x, c, y)
    for cp in inputs:
        cp.wait()
    own[...] = jnp.dot(tok[...], proj[...], preferred_element_type=F32).astype(BF16)
    me8 = x * 2 + c
    row_me = y * 64 + me8 * 8 + z
    list_out[row_me, :, 0:PAIR_DEV] = pair_ref[0:1, :]
    list_out[row_me, :, PAIR_DEV : 2 * PAIR_DEV] = pair_ref[1:2, :]
    list_out[row_me, :, 2 * PAIR_DEV : 3 * PAIR_DEV] = level_ref[...]
    list_out[row_me, :, 3 * PAIR_DEV :] = jnp.zeros((1, 128 - 3 * PAIR_DEV), jnp.int32)
    pl.semaphore_wait(barrier, n_peers)

    lz = []
    for d in range(1, NZ):
        mine = list_out.at[pl.ds(row_me, 1)]
        cp = remote(mine, mine, lz_send.at[d], lz_recv.at[d], dev((z + d) % NZ, x, c, y))
        cp.start()
        lz.append(cp)

    s_b = (z // 4) * 2 + c
    b_dst = b_out.at[pl.ds(pl.multiple_of(s_b * BLK, BLK), BLK)]
    z0 = (z - y + NZ) % NZ
    z1 = (z - y + NZ + 4) % NZ
    self_b = y == 0
    b1 = remote(own, b_dst, b_send.at[1], b_recv.at[z // 4], dev(z1, x, c, y))
    b1.start()
    b0 = remote(own, b_dst, b_send.at[0], b_recv.at[z // 4], dev(z0, x, c, y))
    b0_local = pltpu.make_async_copy(own, b_dst, loc.at[0])

    @pl.when(jnp.logical_not(self_b))
    def _():
        b0.start()

    @pl.when(self_b)
    def _():
        b0_local.start()

    for cp in lz:
        cp.wait_recv()
    lx = []
    for d in range(1, 8):
        k = (me8 + d) % 8
        rows = list_out.at[pl.ds(y * 64 + me8 * 8, 8)]
        cp = remote(rows, rows, lx_send.at[d], lx_recv.at[d], dev(z, k // 2, k % 2, y))
        cp.start()
        lx.append(cp)

    s_a = (x % 2) * 2 + c
    a_dst = a_out.at[pl.ds(pl.multiple_of(s_a * BLK, BLK), BLK)]
    half = x // 2
    self_a = half == c
    a_cps = []
    for d in (2, 1, 3):
        cp = remote(own, a_dst, a_send.at[d], a_recv.at[s_a], dev(z, (x + d) % NX, half, y))
        cp.start()
        a_cps.append(cp)
    a0 = remote(own, a_dst, a_send.at[0], a_recv.at[s_a], dev(z, x, half, y))
    a0_local = pltpu.make_async_copy(own, a_dst, loc.at[1])

    @pl.when(jnp.logical_not(self_a))
    def _():
        a0.start()

    @pl.when(self_a)
    def _():
        a0_local.start()

    for cp in lx:
        cp.wait_recv()
    ly = []
    for d in range(1, NY):
        rows = list_out.at[pl.ds(y * 64, 64)]
        cp = remote(rows, rows, ly_send.at[d], ly_recv.at[d], dev(z, x, c, (y + d) % NY))
        cp.start()
        ly.append(cp)

    sib = dev(z, x, 1 - c, y)
    fwd = []
    for t in range(2):
        slot = b_out.at[pl.ds(pl.multiple_of((t * 2 + c) * BLK, BLK), BLK)]
        arrived = remote(own, slot, b_send.at[t], b_recv.at[t], sib)
        here = jnp.logical_and(self_b, z // 4 == t)

        @pl.when(jnp.logical_not(here))
        def _(arrived=arrived):
            arrived.wait_recv()

        @pl.when(here)
        def _():
            b0_local.wait()

        cp = remote(slot, slot, f_send.at[t], f_recv.at[t], sib)
        cp.start()
        fwd.append(cp)

    for s in range(4):
        slot = a_out.at[pl.ds(s * BLK, BLK)]
        arrived = remote(own, slot, a_send.at[0], a_recv.at[s], sib)
        here = jnp.logical_and(self_a, s_a == s)

        @pl.when(jnp.logical_not(here))
        def _(arrived=arrived):
            arrived.wait_recv()

        @pl.when(here)
        def _():
            a0_local.wait()

    for t in range(2):
        slot = b_out.at[pl.ds(pl.multiple_of((t * 2 + 1 - c) * BLK, BLK), BLK)]
        remote(slot, slot, f_send.at[t], f_recv.at[t], sib).wait_recv()
    for cp in ly:
        cp.wait_recv()

    for cp in lx + lz + ly + a_cps + fwd + [b1]:
        cp.wait_send()

    @pl.when(jnp.logical_not(self_b))
    def _():
        b0.wait_send()

    @pl.when(jnp.logical_not(self_a))
    def _():
        a0.wait_send()


def gather(tokens, proj_in, pairs_t, levels):
    width = proj_in.shape[1]
    dma = pltpu.SemaphoreType.DMA
    vmem = pl.BlockSpec(memory_space=pltpu.VMEM)
    anym = pl.BlockSpec(memory_space=pltpu.HBM)
    return pl.pallas_call(
        gather_kernel,
        out_shape=(
            jax.ShapeDtypeStruct((SIDE, width), BF16),
            jax.ShapeDtypeStruct((SIDE, width), BF16),
            jax.ShapeDtypeStruct((DEVS, 1, 128), jnp.int32),
        ),
        in_specs=[anym] * 4,
        out_specs=(anym, anym, vmem),
        scratch_shapes=[
            pltpu.VMEM(tokens.shape, BF16),
            pltpu.VMEM(proj_in.shape, BF16),
            pltpu.VMEM(pairs_t.shape, jnp.int32),
            pltpu.VMEM(levels.shape, jnp.int32),
            pltpu.VMEM((BLK, width), BF16),
            dma((4,)),
            dma((4,)),
            dma((2,)),
            dma((2,)),
            dma((2,)),
            dma((2,)),
            dma((6,)),
            dma((8,)),
            dma((8,)),
            dma((8,)),
            dma((8,)),
            dma((4,)),
            dma((4,)),
        ],
        compiler_params=pltpu.CompilerParams(
            collective_id=0, has_side_effects=True, vmem_limit_bytes=VMEM_ALL
        ),
        name="gather_blocks",
    )(tokens, proj_in, pairs_t, levels)


def norm(v):
    centred = v - jnp.mean(v, axis=-1, keepdims=True)
    spread = jnp.mean(centred * centred, axis=-1, keepdims=True)
    return centred * lax.rsqrt(spread + 1e-06)


def cell_kernel(
    ids_ref,
    table_ref,
    list_ref,
    a_hbm,
    b_hbm,
    wq_hbm,
    wkv_hbm,
    wo_hbm,
    up_hbm,
    down_hbm,
    pa_ref,
    pb_ref,
    a_ref,
    b_ref,
    wq,
    wkv,
    wo,
    up,
    down,
    side,
    qs,
    ks,
    vs,
    acc_a,
    acc_b,
    rank_t,
    val_t,
    slots_v,
    slots_s,
    att,
    ffn,
    sems,
):
    width = wq.shape[0]
    heads_quad = 4
    quad = heads_quad * HEAD_DIM
    copies = [
        pltpu.make_async_copy(h, v, sems.at[i])
        for i, (h, v) in enumerate(
            (
                (a_hbm, a_ref),
                (wq_hbm, wq),
                (b_hbm, b_ref),
                (wkv_hbm, wkv),
                (wo_hbm, wo),
                (up_hbm, up),
                (down_hbm, down),
            )
        )
    ]
    for cp in copies:
        cp.start()

    a_id, b_x, b_j = ids_ref[0], ids_ref[1], ids_ref[2]
    flat = list_ref[...].reshape(DEVS, 128)
    flat_t = flat.astype(F32).T.astype(jnp.int32)
    a_img = flat_t[:PAIR_DEV]
    b_img = flat_t[PAIR_DEV : 2 * PAIR_DEV]
    level = flat_t[2 * PAIR_DEV : 3 * PAIR_DEV]
    hit = (
        (lax.shift_right_logical(a_img, 5) == a_id)
        & ((lax.shift_right_logical(b_img, 4) & 3) == b_x)
        & ((lax.shift_right_logical(b_img, 6) & 3) == b_j)
    )
    hit_f = hit.astype(F32)
    r_i = lax.broadcasted_iota(jnp.int32, (DEVS, DEVS), 0)
    c_i = lax.broadcasted_iota(jnp.int32, (DEVS, DEVS), 1)
    upper = (r_i <= c_i).astype(BF16)
    across = jnp.dot(hit_f.astype(BF16), upper, preferred_element_type=F32)
    totals = across[:, DEVS - 1 : DEVS]
    k_r = lax.broadcasted_iota(jnp.int32, (PAIR_DEV, PAIR_DEV), 0)
    k_c = lax.broadcasted_iota(jnp.int32, (PAIR_DEV, PAIR_DEV), 1)
    lower = (k_c < k_r).astype(BF16)
    before = jnp.dot(
        lower,
        jnp.broadcast_to(totals, (PAIR_DEV, 128)).astype(BF16),
        preferred_element_type=F32,
    )[:, :1]
    rank = (across + before).astype(jnp.int32) - 1
    rank_t[...] = jnp.where(hit, rank, -1)
    val_t[...] = ((a_img & 31) * 32 + (lax.shift_right_logical(b_img, 8) * 16 + (b_img & 15))) * 16 + level
    count = jnp.sum(hit_f).astype(jnp.int32)

    def fetch_slots():
        return pltpu.make_async_copy(slots_v, slots_s, sems.at[7])

    def select(block):
        slot = lax.broadcasted_iota(jnp.int32, (SLOTS, DEVS), 0) + block * SLOTS
        found = jnp.zeros((SLOTS, DEVS), jnp.int32)
        for k in range(PAIR_DEV):
            found += jnp.where(rank_t[k : k + 1, :] == slot, val_t[k : k + 1, :], 0)
        col = jnp.sum(found.astype(F32), axis=1, keepdims=True).astype(jnp.int32)
        slots_v[...] = jnp.broadcast_to(col, (SLOTS, 128))
        fetch_slots().start()

    select(0)
    acc_a[...] = jnp.zeros_like(acc_a)
    acc_b[...] = jnp.zeros_like(acc_b)

    for cp in copies[:4]:
        cp.wait()
    for i in range(4):
        rows = pl.ds(i * BLK, BLK)
        q_side = a_ref[rows, :].astype(F32)
        side[pl.ds(i * IMG_DEV, IMG_DEV)] = q_side.reshape(IMG_DEV, TOK, width)
        qn = norm(q_side).astype(BF16)
        q = jnp.dot(qn, wq[...], preferred_element_type=F32).astype(BF16).astype(F32)
        qs[pl.ds(i * IMG_DEV, IMG_DEV)] = (q * (HEAD_DIM**-0.5)).reshape(IMG_DEV, TOK, width)
        mn = norm(b_ref[rows, :].astype(F32)).astype(BF16)
        k = jnp.dot(mn, wkv[:, :width], preferred_element_type=F32)
        ks[pl.ds(i * IMG_DEV, IMG_DEV)] = k.reshape(IMG_DEV, TOK, width)
        v = jnp.dot(mn, wkv[:, width:], preferred_element_type=F32)
        vs[pl.ds(i * IMG_DEV, IMG_DEV)] = v.reshape(IMG_DEV, TOK, width)
    for cp in copies[4:]:
        cp.wait()

    lane_head = lax.broadcasted_iota(jnp.int32, (TOK, quad), 1) // HEAD_DIM

    def attend(a_loc, b_loc):
        out = []
        for p in range(width // quad):
            cols = slice(p * quad, (p + 1) * quad)
            q = qs[a_loc, :, cols]
            k = ks[b_loc, :, cols].astype(BF16)
            v = vs[b_loc, :, cols].astype(BF16)
            q4 = jnp.concatenate(
                [jnp.where(lane_head == h, q, 0.0) for h in range(heads_quad)], axis=0
            ).astype(BF16)
            s = lax.dot_general(k, q4, (((1,), (1,)), ((), ())), preferred_element_type=F32)
            e = jnp.exp(s - jnp.max(s, axis=0, keepdims=True))
            probs = (e / jnp.sum(e, axis=0, keepdims=True)).astype(BF16)
            r = lax.dot_general(probs, v, (((0,), (0,)), ((), ())), preferred_element_type=F32)
            o = r[3 * TOK :]
            for h in (2, 1, 0):
                o = jnp.where(lane_head == h, r[h * TOK : (h + 1) * TOK], o)
            out.append(o)
        return jnp.concatenate(out, axis=1)

    def group(first, here, pairs_in):
        locs = []
        for i in range(pairs_in):
            word = slots_s[first + i, 0]
            a_loc = word // 512
            b_loc = (word // 16) % 32
            locs.append((a_loc, b_loc, word % 16))
            att[pl.ds(i * TOK, TOK), :] = attend(a_loc, b_loc)
        rows = pl.ds(0, pairs_in * TOK)
        query = jnp.concatenate([side[a_loc] for a_loc, _, _ in locs], axis=0)
        hidden = query + jnp.dot(att[rows, :].astype(BF16), wo[...], preferred_element_type=F32)
        hn = norm(hidden).astype(BF16)
        u = jnp.dot(hn, up[...], preferred_element_type=F32)
        ex = (0.5 * u) * (1.0 + lax.erf(u * (0.5**0.5)))
        ffn[rows, :] = hidden + jnp.dot(
            ex.astype(BF16), down[...], preferred_element_type=F32
        )
        for i in range(pairs_in):
            a_loc, b_loc, lev = locs[i]

            @pl.when(first + i < here)
            def _(i=i, a_loc=a_loc, b_loc=b_loc, lev=lev):
                feature = table_ref[lev] * ffn[pl.ds(i * TOK, TOK), :]
                feature = feature.astype(BF16).astype(F32)
                acc_a[a_loc] = acc_a[a_loc] + feature
                acc_b[b_loc] = acc_b[b_loc] + feature

    def slot_block(block, carry):
        here = jnp.minimum(count - block * SLOTS, SLOTS)
        wide = (here + GROUP - HALF - 1) // GROUP

        def wide_group(g, carry2):
            group(g * GROUP, here, GROUP)
            return carry2

        lax.fori_loop(0, wide, wide_group, 0)

        @pl.when(wide * GROUP < here)
        def _():
            group(wide * GROUP, here, HALF)

        @pl.when((block + 1) * SLOTS < count)
        def _():
            select(block + 1)
            fetch_slots().wait()

        return carry

    fetch_slots().wait()
    lax.fori_loop(0, (count + SLOTS - 1) // SLOTS, slot_block, 0)
    pa_ref[...] = acc_a[...].reshape(SIDE, width).astype(BF16)
    pb_ref[...] = acc_b[...].reshape(SIDE, width).astype(BF16)


def cell(ids, table, pairs, a_blk, b_blk, wq, wkv, wo, up, down, interpret=False):
    width, ff = up.shape
    vmem = pl.BlockSpec(memory_space=pltpu.VMEM)
    smem = pl.BlockSpec(memory_space=pltpu.SMEM)
    anym = pl.BlockSpec(memory_space=pltpu.HBM)
    images = 4 * IMG_DEV
    return pl.pallas_call(
        cell_kernel,
        out_shape=(
            jax.ShapeDtypeStruct((SIDE, width), BF16),
            jax.ShapeDtypeStruct((SIDE, width), BF16),
        ),
        in_specs=[smem, smem, vmem] + [anym] * 7,
        out_specs=(vmem, vmem),
        scratch_shapes=[
            pltpu.VMEM((SIDE, width), BF16),
            pltpu.VMEM((SIDE, width), BF16),
            pltpu.VMEM((width, width), BF16),
            pltpu.VMEM((width, 2 * width), BF16),
            pltpu.VMEM((width, width), BF16),
            pltpu.VMEM((width, ff), BF16),
            pltpu.VMEM((ff, width), BF16),
            pltpu.VMEM((images, TOK, width), F32),
            pltpu.VMEM((images, TOK, width), F32),
            pltpu.VMEM((images, TOK, width), F32),
            pltpu.VMEM((images, TOK, width), F32),
            pltpu.VMEM((images, TOK, width), F32),
            pltpu.VMEM((images, TOK, width), F32),
            pltpu.VMEM((PAIR_DEV, DEVS), jnp.int32),
            pltpu.VMEM((PAIR_DEV, DEVS), jnp.int32),
            pltpu.VMEM((SLOTS, 128), jnp.int32),
            pltpu.SMEM((SLOTS, 128), jnp.int32),
            pltpu.VMEM((GROUP * TOK, width), F32),
            pltpu.VMEM((GROUP * TOK, width), F32),
            pltpu.SemaphoreType.DMA((8,)),
        ],
        compiler_params=pltpu.CompilerParams(vmem_limit_bytes=VMEM_ALL),
        name="cell_pairs",
        interpret=interpret,
    )(ids, table, pairs, a_blk, b_blk, wq, wkv, wo, up, down)


def reduce_kernel(
    pa_hbm,
    pb_hbm,
    out_ref,
    pb,
    ra,
    rsib,
    sb,
    rz,
    tot,
    ry,
    loc,
    a_send,
    a_recv,
    s_send,
    s_recv,
    z_send,
    z_recv,
    y_send,
    y_recv,
    o_send,
    o_recv,
):
    z, x, c, y = place()
    self_a = x // 2 == c
    self_b = y == 0

    def block(s):
        return pl.ds(pl.multiple_of(s * BLK, BLK), BLK)

    def y_rows(yy):
        return pl.ds(pl.multiple_of(yy * SHARE, SHARE), SHARE)

    keep = []
    for t in range(2):
        cp = pltpu.make_async_copy(pb_hbm.at[block(t * 2 + c)], pb.at[t], loc.at[t])
        cp.start()
        keep.append(cp)
    own_a = pltpu.make_async_copy(pa_hbm.at[block((x % 2) * 2 + c)], ra.at[x], loc.at[2])

    @pl.when(self_a)
    def _():
        own_a.start()

    barrier = pltpu.get_barrier_semaphore()
    for p in row_peers(z, x, c, y) + y_peers(z, x, c, y):
        pl.semaphore_signal(barrier, inc=1, device_id=p, device_id_type=MESH)
    for ys in range(NY):
        for zh in range(2):
            zs = (z + NZ - ys) % 4 + 4 * zh
            here = jnp.logical_and(ys == y, zs == z)

            @pl.when(jnp.logical_not(here))
            def _(zs=zs, ys=ys):
                pl.semaphore_signal(
                    barrier, inc=1, device_id=dev(zs, x, c, ys), device_id_type=MESH
                )

    pl.semaphore_wait(barrier, 7 + NY - 1 + 2 * NY - jnp.where(self_b, 1, 0))
    sib = dev(z, x, 1 - c, y)

    width = out_ref.shape[1]

    def cols(n):
        return pl.ds(n * (width // PARTS), width // PARTS)

    sib_cps = {}
    for n in range(PARTS):
        for t in range(2):
            i = n * 2 + t
            sib_cps[i] = remote(
                pb_hbm.at[block(t * 2 + 1 - c), cols(n)],
                rsib.at[t, :, cols(n)],
                s_send.at[i],
                s_recv.at[i],
                sib,
            )
            sib_cps[i].start()

    a_cps = []
    for n in range(PARTS):
        for s in range(4):
            xt = 2 * c + s // 2
            here = jnp.logical_and(xt == x, c == s % 2)
            cp = remote(
                pa_hbm.at[block(s), cols(n)],
                ra.at[x, :, cols(n)],
                a_send.at[n * 4 + s],
                a_recv.at[n * 4 + x],
                dev(z, xt, s % 2, y),
            )
            a_cps.append((here, cp))

            @pl.when(jnp.logical_not(here))
            def _(cp=cp):
                cp.start()

    j = (z + y) % 4
    z_cps = []
    slot = y * 2 + z // 4
    for cp in keep:
        cp.wait()
    for n in range(PARTS):
        for t in range(2):
            sib_cps[n * 2 + t].wait_recv()
            total = pb[t, :, cols(n)].astype(F32) + rsib[t, :, cols(n)].astype(F32)
            sb[t, :, cols(n)] = total.astype(BF16)
            zt = j + 4 * t
            for q in range(NY):
                piece = pl.ds(q * SHARE, SHARE)
                here = jnp.logical_and(zt == z, q == y)
                cp = remote(
                    sb.at[t, piece, cols(n)],
                    rz.at[slot, :, cols(n)],
                    z_send.at[n * 8 + q * 2 + t],
                    z_recv.at[n * 8 + slot],
                    dev(zt, x, c, q),
                )
                z_cps.append((here, cp))

                @pl.when(jnp.logical_not(here))
                def _(cp=cp):
                    cp.start()

                @pl.when(here)
                def _(t=t, piece=piece, n=n):
                    rz[slot, :, cols(n)] = sb[t, piece, cols(n)]

    @pl.when(self_a)
    def _():
        own_a.wait()

    y_cps = {}
    for n in range(PARTS):
        for s in range(4):
            here = jnp.logical_and(s == x, self_a)

            @pl.when(jnp.logical_not(here))
            def _(s=s, n=n):
                remote(
                    pa_hbm.at[block(0), cols(n)],
                    ra.at[s, :, cols(n)],
                    a_send.at[0],
                    a_recv.at[n * 4 + s],
                    sib,
                ).wait_recv()

        total = (
            ra[0, :, cols(n)].astype(F32)
            + ra[1, :, cols(n)].astype(F32)
            + ra[2, :, cols(n)].astype(F32)
            + ra[3, :, cols(n)].astype(F32)
        )
        tot[:, cols(n)] = total.astype(BF16)
        for d in range(1, NY):
            yt = (y + d) % NY
            cp = remote(
                tot.at[y_rows(yt), cols(n)],
                ry.at[d, :, cols(n)],
                y_send.at[n * 4 + d],
                y_recv.at[n * 4 + d],
                dev(z, x, c, yt),
            )
            cp.start()
            y_cps[n * 4 + d] = cp

    o_cps = []
    for n in range(PARTS):
        mine = tot[y_rows(y), cols(n)].astype(F32)
        for d in range(1, NY):
            y_cps[n * 4 + d].wait_recv()
            mine = mine + ry[d, :, cols(n)].astype(F32)
        for ys in range(NY):
            for zh in range(2):
                s = ys * 2 + zh
                here = jnp.logical_and(jnp.logical_and(self_b, ys == 0), z // 4 == zh)

                @pl.when(jnp.logical_not(here))
                def _(s=s, n=n):
                    remote(
                        sb.at[0, pl.ds(0, SHARE), cols(n)],
                        rz.at[s, :, cols(n)],
                        z_send.at[0],
                        z_recv.at[n * 8 + s],
                        sib,
                    ).wait_recv()

        for s in range(2 * NY):
            mine = mine + rz[s, :, cols(n)].astype(F32)
        out_ref[y_rows(y), cols(n)] = mine.astype(BF16)
        for d in range(1, NY):
            piece = out_ref.at[y_rows(y), cols(n)]
            cp = remote(
                piece,
                piece,
                o_send.at[n * 4 + d],
                o_recv.at[n * 4 + d],
                dev(z, x, c, (y + d) % NY),
            )
            cp.start()
            o_cps.append(cp)
    for n in range(PARTS):
        for d in range(1, NY):
            piece = out_ref.at[y_rows((y - d + NY) % NY), cols(n)]
            remote(piece, piece, o_send.at[d], o_recv.at[n * 4 + d], sib).wait_recv()

    for cp in list(sib_cps.values()) + list(y_cps.values()) + o_cps:
        cp.wait_send()
    for here, cp in a_cps + z_cps:

        @pl.when(jnp.logical_not(here))
        def _(cp=cp):
            cp.wait_send()


def reduce_back(pa, pb):
    width = pa.shape[1]
    dma = pltpu.SemaphoreType.DMA
    vmem = pl.BlockSpec(memory_space=pltpu.VMEM)
    return pl.pallas_call(
        reduce_kernel,
        out_shape=jax.ShapeDtypeStruct((BLK, width), BF16),
        in_specs=[pl.BlockSpec(memory_space=pltpu.HBM)] * 2,
        out_specs=vmem,
        scratch_shapes=[
            pltpu.VMEM((2, BLK, width), BF16),
            pltpu.VMEM((4, BLK, width), BF16),
            pltpu.VMEM((2, BLK, width), BF16),
            pltpu.VMEM((2, BLK, width), BF16),
            pltpu.VMEM((2 * NY, SHARE, width), BF16),
            pltpu.VMEM((BLK, width), BF16),
            pltpu.VMEM((NY, SHARE, width), BF16),
            dma((3,)),
            dma((4 * PARTS,)),
            dma((4 * PARTS,)),
            dma((2 * PARTS,)),
            dma((2 * PARTS,)),
            dma((8 * PARTS,)),
            dma((8 * PARTS,)),
            dma((4 * PARTS,)),
            dma((4 * PARTS,)),
            dma((4 * PARTS,)),
            dma((4 * PARTS,)),
        ],
        compiler_params=pltpu.CompilerParams(
            collective_id=1, has_side_effects=True, vmem_limit_bytes=VMEM_ALL
        ),
        name="reduce_back",
    )(pa, pb)


def body(
    tokens,
    proj_in,
    attn_query,
    attn_keyval,
    attn_output,
    mlp_up,
    mlp_down,
    pair_list,
    conf_level,
    conf_table,
):
    img_dev, tok_count, enc_width = tokens.shape
    z, x, c, y = place()
    a_blk, b_blk, pairs = gather(
        tokens.reshape(img_dev * tok_count, enc_width),
        proj_in,
        pair_list.T,
        conf_level.reshape(1, PAIR_DEV),
    )
    ids = jnp.stack([z * 2 + c, x, (z + y) % 4, 0]).astype(jnp.int32)
    pa, pb = cell(
        ids, conf_table, pairs, a_blk, b_blk, attn_query, attn_keyval, attn_output, mlp_up, mlp_down
    )
    joined = reduce_back(pa, pb)
    return joined.reshape(img_dev, tok_count, joined.shape[1])


def solution(mesh):
    placed = (
        P("img", None, None),
        P(),
        P(),
        P(),
        P(),
        P(),
        P(),
        P(("img", "rep"), None),
        P(("img", "rep")),
        P(),
    )
    return jax.shard_map(
        body, mesh=mesh, in_specs=placed, out_specs=P("img", None, None), check_vma=False
    )
```

```python
import jax
import jax.numpy as jnp
from jax import lax
from jax.experimental import pallas as pl
from jax.experimental.pallas import tpu as pltpu
from jax.sharding import PartitionSpec as P

HEAD_DIM = 64
TOK = 24
IMG_DEV = 8
NX, NY, NZ = 4, 4, 8
BLK = IMG_DEV * TOK
SIDE = 4 * BLK
DEVS = NX * NY * NZ * 2
PAIR_DEV = 32
GROUP = 16
HALF = 8
SLOTS = 64
PARTS = 2
VMEM_ALL = 64 * 1024 * 1024
SHARE = BLK // NY
MESH = pl.DeviceIdType.MESH
F32 = jnp.float32
BF16 = jnp.bfloat16


def place():
    img = lax.axis_index("img")
    return img // 8, (img // 2) % 4, img % 2, lax.axis_index("rep")


def dev(z, x, c, y):
    return ((z * NX + x) * 2 + c, y)


def remote(src, dst, send, recv, to):
    return pltpu.make_async_remote_copy(
        src_ref=src,
        dst_ref=dst,
        send_sem=send,
        recv_sem=recv,
        device_id=to,
        device_id_type=MESH,
    )


def row_peers(z, x, c, y):
    ks = [(x * 2 + c + d) % 8 for d in range(1, 8)]
    return [dev(z, k // 2, k % 2, y) for k in ks]


def z_peers(z, x, c, y):
    return [dev((z + d) % NZ, x, c, y) for d in range(1, NZ)]


def y_peers(z, x, c, y):
    return [dev(z, x, c, (y + d) % NY) for d in range(1, NY)]


def barrier_all(z, x, c, y):
    barrier = pltpu.get_barrier_semaphore()
    peers = row_peers(z, x, c, y) + z_peers(z, x, c, y) + y_peers(z, x, c, y)
    for p in peers:
        pl.semaphore_signal(barrier, inc=1, device_id=p, device_id_type=MESH)
    return barrier, len(peers)


def gather_kernel(
    tok_hbm,
    proj_hbm,
    pair_hbm,
    level_hbm,
    wq_hbm,
    wkv_hbm,
    side_out,
    q_out,
    k_out,
    v_out,
    list_out,
    tok,
    proj,
    pair_ref,
    level_ref,
    wq,
    wkv,
    a_out,
    b_out,
    q_buf,
    k_buf,
    v_buf,
    own,
    own_n,
    a_send,
    a_recv,
    b_send,
    b_recv,
    f_send,
    f_recv,
    out_sem,
    loc,
    lx_send,
    lx_recv,
    lz_send,
    lz_recv,
    ly_send,
    ly_recv,
):
    z, x, c, y = place()
    tok_in = pltpu.make_async_copy(tok_hbm, tok, loc.at[2])
    proj_in = pltpu.make_async_copy(proj_hbm, proj, loc.at[3])
    pair_in = pltpu.make_async_copy(pair_hbm, pair_ref, loc.at[4])
    level_in = pltpu.make_async_copy(level_hbm, level_ref, loc.at[5])
    inputs = (pair_in, level_in, tok_in, proj_in)
    for cp in inputs:
        cp.start()
    weights = (
        pltpu.make_async_copy(wq_hbm, wq, loc.at[6]),
        pltpu.make_async_copy(wkv_hbm, wkv, loc.at[7]),
    )
    for cp in weights:
        cp.start()
    barrier, n_peers = barrier_all(z, x, c, y)
    for cp in inputs:
        cp.wait()
    projected = jnp.dot(tok[...], proj[...], preferred_element_type=F32).astype(BF16)
    own[...] = projected
    own_n[...] = norm(projected.astype(F32)).astype(BF16)
    me8 = x * 2 + c
    row_me = y * 64 + me8 * 8 + z
    list_out[row_me, :, 0:PAIR_DEV] = pair_ref[0:1, :]
    list_out[row_me, :, PAIR_DEV : 2 * PAIR_DEV] = pair_ref[1:2, :]
    list_out[row_me, :, 2 * PAIR_DEV : 3 * PAIR_DEV] = level_ref[...]
    list_out[row_me, :, 3 * PAIR_DEV :] = jnp.zeros((1, 128 - 3 * PAIR_DEV), jnp.int32)
    pl.semaphore_wait(barrier, n_peers)

    lz = []
    for d in range(1, NZ):
        mine = list_out.at[pl.ds(row_me, 1)]
        cp = remote(mine, mine, lz_send.at[d], lz_recv.at[d], dev((z + d) % NZ, x, c, y))
        cp.start()
        lz.append(cp)

    s_b = (z // 4) * 2 + c
    b_dst = b_out.at[pl.ds(pl.multiple_of(s_b * BLK, BLK), BLK)]
    z0 = (z - y + NZ) % NZ
    z1 = (z - y + NZ + 4) % NZ
    self_b = y == 0
    b1 = remote(own_n, b_dst, b_send.at[1], b_recv.at[z // 4], dev(z1, x, c, y))
    b1.start()
    b0 = remote(own_n, b_dst, b_send.at[0], b_recv.at[z // 4], dev(z0, x, c, y))
    b0_local = pltpu.make_async_copy(own_n, b_dst, loc.at[0])

    @pl.when(jnp.logical_not(self_b))
    def _():
        b0.start()

    @pl.when(self_b)
    def _():
        b0_local.start()

    for cp in lz:
        cp.wait_recv()
    lx = []
    for d in range(1, 8):
        k = (me8 + d) % 8
        rows = list_out.at[pl.ds(y * 64 + me8 * 8, 8)]
        cp = remote(rows, rows, lx_send.at[d], lx_recv.at[d], dev(z, k // 2, k % 2, y))
        cp.start()
        lx.append(cp)

    s_a = (x % 2) * 2 + c
    a_dst = a_out.at[pl.ds(pl.multiple_of(s_a * BLK, BLK), BLK)]
    half = x // 2
    self_a = half == c
    a_cps = []
    for d in (2, 1, 3):
        cp = remote(own, a_dst, a_send.at[d], a_recv.at[s_a], dev(z, (x + d) % NX, half, y))
        cp.start()
        a_cps.append(cp)
    a0 = remote(own, a_dst, a_send.at[0], a_recv.at[s_a], dev(z, x, half, y))
    a0_local = pltpu.make_async_copy(own, a_dst, loc.at[1])

    @pl.when(jnp.logical_not(self_a))
    def _():
        a0.start()

    @pl.when(self_a)
    def _():
        a0_local.start()

    for cp in lx:
        cp.wait_recv()
    ly = []
    for d in range(1, NY):
        rows = list_out.at[pl.ds(y * 64, 64)]
        cp = remote(rows, rows, ly_send.at[d], ly_recv.at[d], dev(z, x, c, (y + d) % NY))
        cp.start()
        ly.append(cp)

    for cp in weights:
        cp.wait()
    width = own.shape[1]
    sib = dev(z, x, 1 - c, y)
    outs = []

    def write(src, dst, rows, k):
        cp = pltpu.make_async_copy(src.at[rows], dst.at[rows], out_sem.at[k])
        cp.start()
        outs.append(cp)

    def query_block(s):
        rows = pl.ds(s * BLK, BLK)
        arrived = remote(own, a_out.at[rows], a_send.at[0], a_recv.at[s], sib)
        here = jnp.logical_and(self_a, s_a == s)

        @pl.when(jnp.logical_not(here))
        def _():
            arrived.wait_recv()

        @pl.when(here)
        def _():
            a0_local.wait()

        write(a_out, side_out, rows, s)
        qn = norm(a_out[rows, :].astype(F32)).astype(BF16)
        q = jnp.dot(qn, wq[...], preferred_element_type=F32).astype(BF16)
        q_buf[rows, :] = q * jnp.asarray(HEAD_DIM**-0.5, BF16)
        write(q_buf, q_out, rows, 4 + s)

    fwd = []

    def forward(t):
        slot = b_out.at[pl.ds(pl.multiple_of((t * 2 + c) * BLK, BLK), BLK)]
        arrived = remote(own_n, slot, b_send.at[t], b_recv.at[t], sib)
        here = jnp.logical_and(self_b, z // 4 == t)

        @pl.when(jnp.logical_not(here))
        def _():
            arrived.wait_recv()

        @pl.when(here)
        def _():
            b0_local.wait()

        cp = remote(slot, slot, f_send.at[t], f_recv.at[t], sib)
        cp.start()
        fwd.append(cp)

    def memory_block(s, k):
        rows = pl.ds(pl.multiple_of(s * BLK, BLK), BLK)
        mn = b_out[rows, :]
        k_buf[rows, :] = jnp.dot(mn, wkv[:, :width], preferred_element_type=F32).astype(BF16)
        write(k_buf, k_out, rows, 8 + k)
        v_buf[rows, :] = jnp.dot(mn, wkv[:, width:], preferred_element_type=F32).astype(BF16)
        write(v_buf, v_out, rows, 12 + k)

    query_block(0)
    query_block(1)
    forward(0)
    query_block(2)
    query_block(3)
    forward(1)
    memory_block(c, 0)
    memory_block(2 + c, 1)
    for t in range(2):
        slot = b_out.at[pl.ds(pl.multiple_of((t * 2 + 1 - c) * BLK, BLK), BLK)]
        remote(slot, slot, f_send.at[t], f_recv.at[t], sib).wait_recv()
        memory_block(t * 2 + 1 - c, 2 + t)
    for cp in ly:
        cp.wait_recv()

    for cp in outs:
        cp.wait()
    for cp in lx + lz + ly + a_cps + fwd + [b1]:
        cp.wait_send()

    @pl.when(jnp.logical_not(self_b))
    def _():
        b0.wait_send()

    @pl.when(jnp.logical_not(self_a))
    def _():
        a0.wait_send()


def gather(tokens, proj_in, pairs_t, levels, wq, wkv):
    width = proj_in.shape[1]
    dma = pltpu.SemaphoreType.DMA
    vmem = pl.BlockSpec(memory_space=pltpu.VMEM)
    anym = pl.BlockSpec(memory_space=pltpu.HBM)
    return pl.pallas_call(
        gather_kernel,
        out_shape=(
            jax.ShapeDtypeStruct((SIDE, width), BF16),
            jax.ShapeDtypeStruct((SIDE, width), BF16),
            jax.ShapeDtypeStruct((SIDE, width), BF16),
            jax.ShapeDtypeStruct((SIDE, width), BF16),
            jax.ShapeDtypeStruct((DEVS, 1, 128), jnp.int32),
        ),
        in_specs=[anym] * 6,
        out_specs=(anym, anym, anym, anym, vmem),
        scratch_shapes=[
            pltpu.VMEM(tokens.shape, BF16),
            pltpu.VMEM(proj_in.shape, BF16),
            pltpu.VMEM(pairs_t.shape, jnp.int32),
            pltpu.VMEM(levels.shape, jnp.int32),
            pltpu.VMEM(wq.shape, BF16),
            pltpu.VMEM(wkv.shape, BF16),
            pltpu.VMEM((SIDE, width), BF16),
            pltpu.VMEM((SIDE, width), BF16),
            pltpu.VMEM((SIDE, width), BF16),
            pltpu.VMEM((SIDE, width), BF16),
            pltpu.VMEM((SIDE, width), BF16),
            pltpu.VMEM((BLK, width), BF16),
            pltpu.VMEM((BLK, width), BF16),
            dma((4,)),
            dma((4,)),
            dma((2,)),
            dma((2,)),
            dma((2,)),
            dma((2,)),
            dma((16,)),
            dma((8,)),
            dma((8,)),
            dma((8,)),
            dma((8,)),
            dma((8,)),
            dma((4,)),
            dma((4,)),
        ],
        compiler_params=pltpu.CompilerParams(
            collective_id=0, has_side_effects=True, vmem_limit_bytes=VMEM_ALL
        ),
        name="gather_blocks",
    )(tokens, proj_in, pairs_t, levels, wq, wkv)


def norm(v):
    centred = v - jnp.mean(v, axis=-1, keepdims=True)
    spread = jnp.mean(centred * centred, axis=-1, keepdims=True)
    return centred * lax.rsqrt(spread + 1e-06)


def cell_kernel(
    table_ref,
    list_ref,
    side_hbm,
    q_hbm,
    k_hbm,
    v_hbm,
    wo_hbm,
    up_hbm,
    down_hbm,
    pa_ref,
    pb_ref,
    side_in,
    q_in,
    k_in,
    v_in,
    wo,
    up,
    down,
    side,
    qs,
    ks,
    vs,
    acc_a,
    acc_b,
    rank_t,
    val_t,
    slots_v,
    slots_s,
    att,
    ffn,
    sems,
):
    width = wo.shape[0]
    heads_quad = 4
    quad = heads_quad * HEAD_DIM
    copies = [
        pltpu.make_async_copy(h, v, sems.at[i])
        for i, (h, v) in enumerate(
            (
                (q_hbm, q_in),
                (k_hbm, k_in),
                (v_hbm, v_in),
                (side_hbm, side_in),
                (wo_hbm, wo),
                (up_hbm, up),
                (down_hbm, down),
            )
        )
    ]
    for cp in copies:
        cp.start()

    z, x, c, y = place()
    a_id, b_x, b_j = z * 2 + c, x, (z + y) % 4
    flat = list_ref[...].reshape(DEVS, 128)
    flat_t = flat.astype(F32).T.astype(jnp.int32)
    a_img = flat_t[:PAIR_DEV]
    b_img = flat_t[PAIR_DEV : 2 * PAIR_DEV]
    level = flat_t[2 * PAIR_DEV : 3 * PAIR_DEV]
    hit = (
        (lax.shift_right_logical(a_img, 5) == a_id)
        & ((lax.shift_right_logical(b_img, 4) & 3) == b_x)
        & ((lax.shift_right_logical(b_img, 6) & 3) == b_j)
    )
    hit_f = hit.astype(F32)
    r_i = lax.broadcasted_iota(jnp.int32, (DEVS, DEVS), 0)
    c_i = lax.broadcasted_iota(jnp.int32, (DEVS, DEVS), 1)
    upper = (r_i <= c_i).astype(BF16)
    across = jnp.dot(hit_f.astype(BF16), upper, preferred_element_type=F32)
    totals = across[:, DEVS - 1 : DEVS]
    k_r = lax.broadcasted_iota(jnp.int32, (PAIR_DEV, PAIR_DEV), 0)
    k_c = lax.broadcasted_iota(jnp.int32, (PAIR_DEV, PAIR_DEV), 1)
    lower = (k_c < k_r).astype(BF16)
    before = jnp.dot(
        lower,
        jnp.broadcast_to(totals, (PAIR_DEV, 128)).astype(BF16),
        preferred_element_type=F32,
    )[:, :1]
    rank = (across + before).astype(jnp.int32) - 1
    rank_t[...] = jnp.where(hit, rank, -1)
    val_t[...] = ((a_img & 31) * 32 + (lax.shift_right_logical(b_img, 8) * 16 + (b_img & 15))) * 16 + level
    count = jnp.sum(hit_f).astype(jnp.int32)

    def fetch_slots():
        return pltpu.make_async_copy(slots_v, slots_s, sems.at[7])

    def select(block):
        slot = lax.broadcasted_iota(jnp.int32, (SLOTS, DEVS), 0) + block * SLOTS
        found = jnp.zeros((SLOTS, DEVS), jnp.int32)
        for k in range(PAIR_DEV):
            found += jnp.where(rank_t[k : k + 1, :] == slot, val_t[k : k + 1, :], 0)
        col = jnp.sum(found.astype(F32), axis=1, keepdims=True).astype(jnp.int32)
        slots_v[...] = jnp.broadcast_to(col, (SLOTS, 128))
        fetch_slots().start()

    select(0)
    acc_a[...] = jnp.zeros_like(acc_a)
    acc_b[...] = jnp.zeros_like(acc_b)

    for cp, src, dst in zip(copies, (q_in, k_in, v_in, side_in), (qs, ks, vs, side)):
        cp.wait()
        dst[...] = src[...].astype(F32).reshape(dst.shape)
    for cp in copies[4:]:
        cp.wait()

    lane_head = lax.broadcasted_iota(jnp.int32, (TOK, quad), 1) // HEAD_DIM

    def attend(a_loc, b_loc):
        out = []
        for p in range(width // quad):
            cols = slice(p * quad, (p + 1) * quad)
            q = qs[a_loc, :, cols]
            k = ks[b_loc, :, cols].astype(BF16)
            v = vs[b_loc, :, cols].astype(BF16)
            q4 = jnp.concatenate(
                [jnp.where(lane_head == h, q, 0.0) for h in range(heads_quad)], axis=0
            ).astype(BF16)
            s = lax.dot_general(k, q4, (((1,), (1,)), ((), ())), preferred_element_type=F32)
            e = jnp.exp(s - jnp.max(s, axis=0, keepdims=True))
            probs = (e / jnp.sum(e, axis=0, keepdims=True)).astype(BF16)
            r = lax.dot_general(probs, v, (((0,), (0,)), ((), ())), preferred_element_type=F32)
            o = r[3 * TOK :]
            for h in (2, 1, 0):
                o = jnp.where(lane_head == h, r[h * TOK : (h + 1) * TOK], o)
            out.append(o)
        return jnp.concatenate(out, axis=1)

    def group(first, here, pairs_in):
        locs = []
        for i in range(pairs_in):
            word = slots_s[first + i, 0]
            a_loc = word // 512
            b_loc = (word // 16) % 32
            locs.append((a_loc, b_loc, word % 16))
            att[pl.ds(i * TOK, TOK), :] = attend(a_loc, b_loc)
        rows = pl.ds(0, pairs_in * TOK)
        query = jnp.concatenate([side[a_loc] for a_loc, _, _ in locs], axis=0)
        hidden = query + jnp.dot(att[rows, :].astype(BF16), wo[...], preferred_element_type=F32)
        hn = norm(hidden).astype(BF16)
        u = jnp.dot(hn, up[...], preferred_element_type=F32)
        ex = (0.5 * u) * (1.0 + lax.erf(u * (0.5**0.5)))
        ffn[rows, :] = hidden + jnp.dot(
            ex.astype(BF16), down[...], preferred_element_type=F32
        )
        for i in range(pairs_in):
            a_loc, b_loc, lev = locs[i]

            @pl.when(first + i < here)
            def _(i=i, a_loc=a_loc, b_loc=b_loc, lev=lev):
                feature = table_ref[lev] * ffn[pl.ds(i * TOK, TOK), :]
                feature = feature.astype(BF16).astype(F32)
                acc_a[a_loc] = acc_a[a_loc] + feature
                acc_b[b_loc] = acc_b[b_loc] + feature

    def slot_block(block, carry):
        here = jnp.minimum(count - block * SLOTS, SLOTS)
        wide = (here + GROUP - HALF - 1) // GROUP

        def wide_group(g, carry2):
            group(g * GROUP, here, GROUP)
            return carry2

        lax.fori_loop(0, wide, wide_group, 0)

        @pl.when(wide * GROUP < here)
        def _():
            group(wide * GROUP, here, HALF)

        @pl.when((block + 1) * SLOTS < count)
        def _():
            select(block + 1)
            fetch_slots().wait()

        return carry

    fetch_slots().wait()
    lax.fori_loop(0, (count + SLOTS - 1) // SLOTS, slot_block, 0)
    pa_ref[...] = acc_a[...].reshape(SIDE, width).astype(BF16)
    pb_ref[...] = acc_b[...].reshape(SIDE, width).astype(BF16)


def cell(table, pairs, side, q, k, v, wo, up, down):
    width, ff = up.shape
    vmem = pl.BlockSpec(memory_space=pltpu.VMEM)
    smem = pl.BlockSpec(memory_space=pltpu.SMEM)
    anym = pl.BlockSpec(memory_space=pltpu.HBM)
    images = 4 * IMG_DEV
    return pl.pallas_call(
        cell_kernel,
        out_shape=(
            jax.ShapeDtypeStruct((SIDE, width), BF16),
            jax.ShapeDtypeStruct((SIDE, width), BF16),
        ),
        in_specs=[smem, vmem] + [anym] * 7,
        out_specs=(vmem, vmem),
        scratch_shapes=[
            pltpu.VMEM((SIDE, width), BF16),
            pltpu.VMEM((SIDE, width), BF16),
            pltpu.VMEM((SIDE, width), BF16),
            pltpu.VMEM((SIDE, width), BF16),
            pltpu.VMEM((width, width), BF16),
            pltpu.VMEM((width, ff), BF16),
            pltpu.VMEM((ff, width), BF16),
            pltpu.VMEM((images, TOK, width), F32),
            pltpu.VMEM((images, TOK, width), F32),
            pltpu.VMEM((images, TOK, width), F32),
            pltpu.VMEM((images, TOK, width), F32),
            pltpu.VMEM((images, TOK, width), F32),
            pltpu.VMEM((images, TOK, width), F32),
            pltpu.VMEM((PAIR_DEV, DEVS), jnp.int32),
            pltpu.VMEM((PAIR_DEV, DEVS), jnp.int32),
            pltpu.VMEM((SLOTS, 128), jnp.int32),
            pltpu.SMEM((SLOTS, 128), jnp.int32),
            pltpu.VMEM((GROUP * TOK, width), F32),
            pltpu.VMEM((GROUP * TOK, width), F32),
            pltpu.SemaphoreType.DMA((8,)),
        ],
        compiler_params=pltpu.CompilerParams(vmem_limit_bytes=VMEM_ALL),
        name="cell_pairs",
    )(table, pairs, side, q, k, v, wo, up, down)


def reduce_kernel(
    pa_hbm,
    pb_hbm,
    out_ref,
    pb,
    ra,
    rsib,
    sb,
    rz,
    tot,
    ry,
    loc,
    a_send,
    a_recv,
    s_send,
    s_recv,
    z_send,
    z_recv,
    y_send,
    y_recv,
    o_send,
    o_recv,
):
    z, x, c, y = place()
    self_a = x // 2 == c
    self_b = y == 0

    def block(s):
        return pl.ds(pl.multiple_of(s * BLK, BLK), BLK)

    def y_rows(yy):
        return pl.ds(pl.multiple_of(yy * SHARE, SHARE), SHARE)

    keep = []
    for t in range(2):
        cp = pltpu.make_async_copy(pb_hbm.at[block(t * 2 + c)], pb.at[t], loc.at[t])
        cp.start()
        keep.append(cp)
    own_a = pltpu.make_async_copy(pa_hbm.at[block((x % 2) * 2 + c)], ra.at[x], loc.at[2])

    @pl.when(self_a)
    def _():
        own_a.start()

    barrier = pltpu.get_barrier_semaphore()
    for p in row_peers(z, x, c, y) + y_peers(z, x, c, y):
        pl.semaphore_signal(barrier, inc=1, device_id=p, device_id_type=MESH)
    for ys in range(NY):
        for zh in range(2):
            zs = (z + NZ - ys) % 4 + 4 * zh
            here = jnp.logical_and(ys == y, zs == z)

            @pl.when(jnp.logical_not(here))
            def _(zs=zs, ys=ys):
                pl.semaphore_signal(
                    barrier, inc=1, device_id=dev(zs, x, c, ys), device_id_type=MESH
                )

    pl.semaphore_wait(barrier, 7 + NY - 1 + 2 * NY - jnp.where(self_b, 1, 0))
    sib = dev(z, x, 1 - c, y)

    width = out_ref.shape[1]

    def cols(n):
        return pl.ds(n * (width // PARTS), width // PARTS)

    sib_cps = {}
    for n in range(PARTS):
        for t in range(2):
            i = n * 2 + t
            sib_cps[i] = remote(
                pb_hbm.at[block(t * 2 + 1 - c), cols(n)],
                rsib.at[t, :, cols(n)],
                s_send.at[i],
                s_recv.at[i],
                sib,
            )
            sib_cps[i].start()

    a_cps = []
    for n in range(PARTS):
        for s in range(4):
            xt = 2 * c + s // 2
            here = jnp.logical_and(xt == x, c == s % 2)
            cp = remote(
                pa_hbm.at[block(s), cols(n)],
                ra.at[x, :, cols(n)],
                a_send.at[n * 4 + s],
                a_recv.at[n * 4 + x],
                dev(z, xt, s % 2, y),
            )
            a_cps.append((here, cp))

            @pl.when(jnp.logical_not(here))
            def _(cp=cp):
                cp.start()

    j = (z + y) % 4
    z_cps = []
    slot = y * 2 + z // 4
    for cp in keep:
        cp.wait()
    for n in range(PARTS):
        for t in range(2):
            sib_cps[n * 2 + t].wait_recv()
            total = pb[t, :, cols(n)].astype(F32) + rsib[t, :, cols(n)].astype(F32)
            sb[t, :, cols(n)] = total.astype(BF16)
            zt = j + 4 * t
            for q in range(NY):
                piece = pl.ds(q * SHARE, SHARE)
                here = jnp.logical_and(zt == z, q == y)
                cp = remote(
                    sb.at[t, piece, cols(n)],
                    rz.at[slot, :, cols(n)],
                    z_send.at[n * 8 + q * 2 + t],
                    z_recv.at[n * 8 + slot],
                    dev(zt, x, c, q),
                )
                z_cps.append((here, cp))

                @pl.when(jnp.logical_not(here))
                def _(cp=cp):
                    cp.start()

                @pl.when(here)
                def _(t=t, piece=piece, n=n):
                    rz[slot, :, cols(n)] = sb[t, piece, cols(n)]

    @pl.when(self_a)
    def _():
        own_a.wait()

    y_cps = {}
    for n in range(PARTS):
        for s in range(4):
            here = jnp.logical_and(s == x, self_a)

            @pl.when(jnp.logical_not(here))
            def _(s=s, n=n):
                remote(
                    pa_hbm.at[block(0), cols(n)],
                    ra.at[s, :, cols(n)],
                    a_send.at[0],
                    a_recv.at[n * 4 + s],
                    sib,
                ).wait_recv()

        total = (
            ra[0, :, cols(n)].astype(F32)
            + ra[1, :, cols(n)].astype(F32)
            + ra[2, :, cols(n)].astype(F32)
            + ra[3, :, cols(n)].astype(F32)
        )
        tot[:, cols(n)] = total.astype(BF16)
        for d in range(1, NY):
            yt = (y + d) % NY
            cp = remote(
                tot.at[y_rows(yt), cols(n)],
                ry.at[d, :, cols(n)],
                y_send.at[n * 4 + d],
                y_recv.at[n * 4 + d],
                dev(z, x, c, yt),
            )
            cp.start()
            y_cps[n * 4 + d] = cp

    o_cps = []
    for n in range(PARTS):
        mine = tot[y_rows(y), cols(n)].astype(F32)
        for d in range(1, NY):
            y_cps[n * 4 + d].wait_recv()
            mine = mine + ry[d, :, cols(n)].astype(F32)
        for ys in range(NY):
            for zh in range(2):
                s = ys * 2 + zh
                here = jnp.logical_and(jnp.logical_and(self_b, ys == 0), z // 4 == zh)

                @pl.when(jnp.logical_not(here))
                def _(s=s, n=n):
                    remote(
                        sb.at[0, pl.ds(0, SHARE), cols(n)],
                        rz.at[s, :, cols(n)],
                        z_send.at[0],
                        z_recv.at[n * 8 + s],
                        sib,
                    ).wait_recv()

        for s in range(2 * NY):
            mine = mine + rz[s, :, cols(n)].astype(F32)
        out_ref[y_rows(y), cols(n)] = mine.astype(BF16)
        for d in range(1, NY):
            piece = out_ref.at[y_rows(y), cols(n)]
            cp = remote(
                piece,
                piece,
                o_send.at[n * 4 + d],
                o_recv.at[n * 4 + d],
                dev(z, x, c, (y + d) % NY),
            )
            cp.start()
            o_cps.append(cp)
    for n in range(PARTS):
        for d in range(1, NY):
            piece = out_ref.at[y_rows((y - d + NY) % NY), cols(n)]
            remote(piece, piece, o_send.at[d], o_recv.at[n * 4 + d], sib).wait_recv()

    for cp in list(sib_cps.values()) + list(y_cps.values()) + o_cps:
        cp.wait_send()
    for here, cp in a_cps + z_cps:

        @pl.when(jnp.logical_not(here))
        def _(cp=cp):
            cp.wait_send()


def reduce_back(pa, pb):
    width = pa.shape[1]
    dma = pltpu.SemaphoreType.DMA
    vmem = pl.BlockSpec(memory_space=pltpu.VMEM)
    return pl.pallas_call(
        reduce_kernel,
        out_shape=jax.ShapeDtypeStruct((BLK, width), BF16),
        in_specs=[pl.BlockSpec(memory_space=pltpu.HBM)] * 2,
        out_specs=vmem,
        scratch_shapes=[
            pltpu.VMEM((2, BLK, width), BF16),
            pltpu.VMEM((4, BLK, width), BF16),
            pltpu.VMEM((2, BLK, width), BF16),
            pltpu.VMEM((2, BLK, width), BF16),
            pltpu.VMEM((2 * NY, SHARE, width), BF16),
            pltpu.VMEM((BLK, width), BF16),
            pltpu.VMEM((NY, SHARE, width), BF16),
            dma((3,)),
            dma((4 * PARTS,)),
            dma((4 * PARTS,)),
            dma((2 * PARTS,)),
            dma((2 * PARTS,)),
            dma((8 * PARTS,)),
            dma((8 * PARTS,)),
            dma((4 * PARTS,)),
            dma((4 * PARTS,)),
            dma((4 * PARTS,)),
            dma((4 * PARTS,)),
        ],
        compiler_params=pltpu.CompilerParams(
            collective_id=1, has_side_effects=True, vmem_limit_bytes=VMEM_ALL - 640 * 1024
        ),
        name="reduce_back",
    )(pa, pb)


def body(
    tokens,
    proj_in,
    attn_query,
    attn_keyval,
    attn_output,
    mlp_up,
    mlp_down,
    pair_list,
    conf_level,
    conf_table,
):
    img_dev, tok_count, enc_width = tokens.shape
    side, q, k, v, pairs = gather(
        tokens.reshape(img_dev * tok_count, enc_width),
        proj_in,
        pair_list.T,
        conf_level.reshape(1, PAIR_DEV),
        attn_query,
        attn_keyval,
    )
    pa, pb = cell(conf_table, pairs, side, q, k, v, attn_output, mlp_up, mlp_down)
    joined = reduce_back(pa, pb)
    return joined.reshape(img_dev, tok_count, joined.shape[1])


def solution(mesh):
    placed = (
        P("img", None, None),
        P(),
        P(),
        P(),
        P(),
        P(),
        P(),
        P(("img", "rep"), None),
        P(("img", "rep")),
        P(),
    )
    return jax.shard_map(
        body, mesh=mesh, in_specs=placed, out_specs=P("img", None, None), check_vma=False
    )
```

```python
import jax
import jax.numpy as jnp
from jax import lax
from jax.experimental import pallas as pl
from jax.experimental.pallas import tpu as pltpu
from jax.sharding import PartitionSpec as P

HEAD_DIM = 64
TOK = 24
IMG_DEV = 8
NX, NY, NZ = 4, 4, 8
BLK = IMG_DEV * TOK
SIDE = 4 * BLK
DEVS = NX * NY * NZ * 2
PAIR_DEV = 32
GROUP = 16
HALF = 8
SLOTS = 64
PARTS = 2
VMEM_ALL = 64 * 1024 * 1024
SHARE = BLK // NY
FAR = 128
MESH = pl.DeviceIdType.MESH
F32 = jnp.float32
BF16 = jnp.bfloat16


def place():
    img = lax.axis_index("img")
    return img // 8, (img // 2) % 4, img % 2, lax.axis_index("rep")


def dev(z, x, c, y):
    return ((z * NX + x) * 2 + c, y)


def remote(src, dst, send, recv, to):
    return pltpu.make_async_remote_copy(
        src_ref=src,
        dst_ref=dst,
        send_sem=send,
        recv_sem=recv,
        device_id=to,
        device_id_type=MESH,
    )


def row_peers(z, x, c, y):
    ks = [(x * 2 + c + d) % 8 for d in range(1, 8)]
    return [dev(z, k // 2, k % 2, y) for k in ks]


def z_peers(z, x, c, y):
    return [dev((z + d) % NZ, x, c, y) for d in range(1, NZ)]


def y_peers(z, x, c, y):
    return [dev(z, x, c, (y + d) % NY) for d in range(1, NY)]


def barrier_all(z, x, c, y):
    barrier = pltpu.get_barrier_semaphore()
    peers = row_peers(z, x, c, y) + z_peers(z, x, c, y) + y_peers(z, x, c, y)
    for p in peers:
        pl.semaphore_signal(barrier, inc=1, device_id=p, device_id_type=MESH)
    return barrier, len(peers)


def far_target(z, y):
    return (z + jnp.where(y == 1, 3, 5)) % NZ


def far_source(z, y):
    return (z + jnp.where(y == 1, 5, 3)) % NZ


def gather_kernel(
    tok_hbm,
    proj_hbm,
    pair_hbm,
    level_hbm,
    a_out,
    b_out,
    list_out,
    tok,
    proj,
    pair_ref,
    level_ref,
    own,
    a_send,
    a_recv,
    b_send,
    b_recv,
    f_send,
    f_recv,
    loc,
    lx_send,
    lx_recv,
    lz_send,
    lz_recv,
    ly_send,
    ly_recv,
):
    z, x, c, y = place()
    tok_in = pltpu.make_async_copy(tok_hbm, tok, loc.at[2])
    proj_in = pltpu.make_async_copy(proj_hbm, proj, loc.at[3])
    pair_in = pltpu.make_async_copy(pair_hbm, pair_ref, loc.at[4])
    level_in = pltpu.make_async_copy(level_hbm, level_ref, loc.at[5])
    inputs = (pair_in, level_in, tok_in, proj_in)
    for cp in inputs:
        cp.start()
    barrier, n_peers = barrier_all(z, x, c, y)
    odd = y % 2 == 1
    other = (y + 2) % NY

    @pl.when(odd)
    def _():
        source = dev(far_source(z, y), x, c, other)
        pl.semaphore_signal(barrier, inc=1, device_id=source, device_id_type=MESH)

    for cp in inputs:
        cp.wait()
    own[...] = jnp.dot(tok[...], proj[...], preferred_element_type=F32).astype(BF16)
    me8 = x * 2 + c
    row_me = y * 64 + me8 * 8 + z
    list_out[row_me, :, 0:PAIR_DEV] = pair_ref[0:1, :]
    list_out[row_me, :, PAIR_DEV : 2 * PAIR_DEV] = pair_ref[1:2, :]
    list_out[row_me, :, 2 * PAIR_DEV : 3 * PAIR_DEV] = level_ref[...]
    list_out[row_me, :, 3 * PAIR_DEV :] = jnp.zeros((1, 128 - 3 * PAIR_DEV), jnp.int32)
    pl.semaphore_wait(barrier, n_peers + jnp.where(odd, 1, 0))

    lz = []
    for d in range(1, NZ):
        mine = list_out.at[pl.ds(row_me, 1)]
        cp = remote(mine, mine, lz_send.at[d], lz_recv.at[d], dev((z + d) % NZ, x, c, y))
        cp.start()
        lz.append(cp)

    s_b = (z // 4) * 2 + c
    b_dst = b_out.at[pl.ds(pl.multiple_of(s_b * BLK, BLK), BLK)]
    z0 = (z - y + NZ) % NZ
    z1 = (z - y + NZ + 4) % NZ
    self_b = y == 0
    b0_local = pltpu.make_async_copy(own, b_dst, loc.at[0])

    @pl.when(self_b)
    def _():
        b0_local.start()

    near_dst = b_out.at[pl.ds(pl.multiple_of(s_b * BLK, BLK), FAR)]
    far_dst = b_out.at[pl.ds(pl.multiple_of(s_b * BLK + FAR, BLK - FAR), BLK - FAR)]
    over = dev(far_target(z, other), x, c, other)
    cross = remote(own.at[pl.ds(FAR, BLK - FAR)], far_dst, b_send.at[2], b_recv.at[2], over)
    b_cps = [(odd, cross)]
    for t, zt in ((1, z1), (0, z0)):
        far = y == (1 if t == 1 else 3)
        whole = remote(own, b_dst, b_send.at[t], b_recv.at[z // 4], dev(zt, x, c, y))
        most = remote(
            own.at[pl.ds(0, FAR)], near_dst, b_send.at[t], b_recv.at[z // 4], dev(zt, x, c, y)
        )
        b_cps.append((far, most))
        full = jnp.logical_not(far)
        b_cps.append((jnp.logical_and(full, jnp.logical_not(self_b)) if t == 0 else full, whole))
    for go, cp in b_cps:

        @pl.when(go)
        def _(cp=cp):
            cp.start()

    for cp in lz:
        cp.wait_recv()
    lx = []
    for d in range(1, 8):
        k = (me8 + d) % 8
        rows = list_out.at[pl.ds(y * 64 + me8 * 8, 8)]
        cp = remote(rows, rows, lx_send.at[d], lx_recv.at[d], dev(z, k // 2, k % 2, y))
        cp.start()
        lx.append(cp)

    s_a = (x % 2) * 2 + c
    a_dst = a_out.at[pl.ds(pl.multiple_of(s_a * BLK, BLK), BLK)]
    half = x // 2
    self_a = half == c
    a_cps = []
    for d in (2, 1, 3):
        cp = remote(own, a_dst, a_send.at[d], a_recv.at[s_a], dev(z, (x + d) % NX, half, y))
        cp.start()
        a_cps.append(cp)
    a0 = remote(own, a_dst, a_send.at[0], a_recv.at[s_a], dev(z, x, half, y))
    a0_local = pltpu.make_async_copy(own, a_dst, loc.at[1])

    @pl.when(jnp.logical_not(self_a))
    def _():
        a0.start()

    @pl.when(self_a)
    def _():
        a0_local.start()

    for cp in lx:
        cp.wait_recv()
    ly = []
    for d in range(1, NY):
        rows = list_out.at[pl.ds(y * 64, 64)]
        cp = remote(rows, rows, ly_send.at[d], ly_recv.at[d], dev(z, x, c, (y + d) % NY))
        cp.start()
        ly.append(cp)

    sib = dev(z, x, 1 - c, y)
    fwd = []
    for t in range(2):
        base = (t * 2 + c) * BLK
        slot = b_out.at[pl.ds(pl.multiple_of(base, BLK), BLK)]
        arrived = remote(own, slot, b_send.at[t], b_recv.at[t], sib)
        most = remote(
            own.at[pl.ds(0, FAR)],
            b_out.at[pl.ds(pl.multiple_of(base, BLK), FAR)],
            b_send.at[t],
            b_recv.at[t],
            sib,
        )
        rest = remote(
            own.at[pl.ds(FAR, BLK - FAR)],
            b_out.at[pl.ds(pl.multiple_of(base + FAR, BLK - FAR), BLK - FAR)],
            b_send.at[2],
            b_recv.at[2],
            sib,
        )
        here = jnp.logical_and(self_b, z // 4 == t)
        split = jnp.logical_and(odd, far_source(z, y) // 4 == t)

        @pl.when(jnp.logical_not(jnp.logical_or(here, split)))
        def _(arrived=arrived):
            arrived.wait_recv()

        @pl.when(split)
        def _(most=most, rest=rest):
            most.wait_recv()
            rest.wait_recv()

        @pl.when(here)
        def _():
            b0_local.wait()

        cp = remote(slot, slot, f_send.at[t], f_recv.at[t], sib)
        cp.start()
        fwd.append(cp)

    for s in range(4):
        slot = a_out.at[pl.ds(s * BLK, BLK)]
        arrived = remote(own, slot, a_send.at[0], a_recv.at[s], sib)
        here = jnp.logical_and(self_a, s_a == s)

        @pl.when(jnp.logical_not(here))
        def _(arrived=arrived):
            arrived.wait_recv()

        @pl.when(here)
        def _():
            a0_local.wait()

    for t in range(2):
        slot = b_out.at[pl.ds(pl.multiple_of((t * 2 + 1 - c) * BLK, BLK), BLK)]
        remote(slot, slot, f_send.at[t], f_recv.at[t], sib).wait_recv()
    for cp in ly:
        cp.wait_recv()

    for cp in lx + lz + ly + a_cps + fwd:
        cp.wait_send()

    for go, cp in b_cps:

        @pl.when(go)
        def _(cp=cp):
            cp.wait_send()

    @pl.when(jnp.logical_not(self_a))
    def _():
        a0.wait_send()


def gather(tokens, proj_in, pairs_t, levels):
    width = proj_in.shape[1]
    dma = pltpu.SemaphoreType.DMA
    vmem = pl.BlockSpec(memory_space=pltpu.VMEM)
    anym = pl.BlockSpec(memory_space=pltpu.HBM)
    return pl.pallas_call(
        gather_kernel,
        out_shape=(
            jax.ShapeDtypeStruct((SIDE, width), BF16),
            jax.ShapeDtypeStruct((SIDE, width), BF16),
            jax.ShapeDtypeStruct((DEVS, 1, 128), jnp.int32),
        ),
        in_specs=[anym] * 4,
        out_specs=(anym, anym, vmem),
        scratch_shapes=[
            pltpu.VMEM(tokens.shape, BF16),
            pltpu.VMEM(proj_in.shape, BF16),
            pltpu.VMEM(pairs_t.shape, jnp.int32),
            pltpu.VMEM(levels.shape, jnp.int32),
            pltpu.VMEM((BLK, width), BF16),
            dma((4,)),
            dma((4,)),
            dma((3,)),
            dma((3,)),
            dma((2,)),
            dma((2,)),
            dma((6,)),
            dma((8,)),
            dma((8,)),
            dma((8,)),
            dma((8,)),
            dma((4,)),
            dma((4,)),
        ],
        compiler_params=pltpu.CompilerParams(
            collective_id=0, has_side_effects=True, vmem_limit_bytes=VMEM_ALL
        ),
        name="gather_blocks",
    )(tokens, proj_in, pairs_t, levels)


def norm(v):
    centred = v - jnp.mean(v, axis=-1, keepdims=True)
    spread = jnp.mean(centred * centred, axis=-1, keepdims=True)
    return centred * lax.rsqrt(spread + 1e-06)


def cell_kernel(
    table_ref,
    list_ref,
    a_hbm,
    b_hbm,
    wq_hbm,
    wkv_hbm,
    wo_hbm,
    up_hbm,
    down_hbm,
    pa_ref,
    pb_ref,
    a_ref,
    b_ref,
    wq,
    wkv,
    wo,
    up,
    down,
    side,
    qs,
    ks,
    vs,
    acc_a,
    acc_b,
    rank_t,
    val_t,
    slots_v,
    slots_s,
    att,
    ffn,
    sems,
):
    width = wq.shape[0]
    heads_quad = 4
    quad = heads_quad * HEAD_DIM
    copies = [
        pltpu.make_async_copy(h, v, sems.at[i])
        for i, (h, v) in enumerate(
            (
                (a_hbm, a_ref),
                (wq_hbm, wq),
                (b_hbm, b_ref),
                (wkv_hbm, wkv),
                (wo_hbm, wo),
                (up_hbm, up),
                (down_hbm, down),
            )
        )
    ]
    for cp in copies:
        cp.start()

    z, x, c, y = place()
    a_id, b_x, b_j = z * 2 + c, x, (z + y) % 4
    flat = list_ref[...].reshape(DEVS, 128)
    flat_t = flat.astype(F32).T.astype(jnp.int32)
    a_img = flat_t[:PAIR_DEV]
    b_img = flat_t[PAIR_DEV : 2 * PAIR_DEV]
    level = flat_t[2 * PAIR_DEV : 3 * PAIR_DEV]
    hit = (
        (lax.shift_right_logical(a_img, 5) == a_id)
        & ((lax.shift_right_logical(b_img, 4) & 3) == b_x)
        & ((lax.shift_right_logical(b_img, 6) & 3) == b_j)
    )
    hit_f = hit.astype(F32)
    r_i = lax.broadcasted_iota(jnp.int32, (DEVS, DEVS), 0)
    c_i = lax.broadcasted_iota(jnp.int32, (DEVS, DEVS), 1)
    upper = (r_i <= c_i).astype(BF16)
    across = jnp.dot(hit_f.astype(BF16), upper, preferred_element_type=F32)
    totals = across[:, DEVS - 1 : DEVS]
    k_r = lax.broadcasted_iota(jnp.int32, (PAIR_DEV, PAIR_DEV), 0)
    k_c = lax.broadcasted_iota(jnp.int32, (PAIR_DEV, PAIR_DEV), 1)
    lower = (k_c < k_r).astype(BF16)
    before = jnp.dot(
        lower,
        jnp.broadcast_to(totals, (PAIR_DEV, 128)).astype(BF16),
        preferred_element_type=F32,
    )[:, :1]
    rank = (across + before).astype(jnp.int32) - 1
    rank_t[...] = jnp.where(hit, rank, -1)
    val_t[...] = ((a_img & 31) * 32 + (lax.shift_right_logical(b_img, 8) * 16 + (b_img & 15))) * 16 + level
    count = jnp.sum(hit_f).astype(jnp.int32)

    def fetch_slots():
        return pltpu.make_async_copy(slots_v, slots_s, sems.at[7])

    def select(block):
        slot = lax.broadcasted_iota(jnp.int32, (SLOTS, DEVS), 0) + block * SLOTS
        found = jnp.zeros((SLOTS, DEVS), jnp.int32)
        for k in range(PAIR_DEV):
            found += jnp.where(rank_t[k : k + 1, :] == slot, val_t[k : k + 1, :], 0)
        col = jnp.sum(found.astype(F32), axis=1, keepdims=True).astype(jnp.int32)
        slots_v[...] = jnp.broadcast_to(col, (SLOTS, 128))
        fetch_slots().start()

    select(0)
    acc_a[...] = jnp.zeros_like(acc_a)
    acc_b[...] = jnp.zeros_like(acc_b)

    for cp in copies[:4]:
        cp.wait()
    for i in range(4):
        rows = pl.ds(i * BLK, BLK)
        q_side = a_ref[rows, :].astype(F32)
        side[pl.ds(i * IMG_DEV, IMG_DEV)] = q_side.reshape(IMG_DEV, TOK, width)
        qn = norm(q_side).astype(BF16)
        q = jnp.dot(qn, wq[...], preferred_element_type=F32).astype(BF16).astype(F32)
        qs[pl.ds(i * IMG_DEV, IMG_DEV)] = (q * (HEAD_DIM**-0.5)).reshape(IMG_DEV, TOK, width)
        mn = norm(b_ref[rows, :].astype(F32)).astype(BF16)
        k = jnp.dot(mn, wkv[:, :width], preferred_element_type=F32)
        ks[pl.ds(i * IMG_DEV, IMG_DEV)] = k.reshape(IMG_DEV, TOK, width)
        v = jnp.dot(mn, wkv[:, width:], preferred_element_type=F32)
        vs[pl.ds(i * IMG_DEV, IMG_DEV)] = v.reshape(IMG_DEV, TOK, width)
    for cp in copies[4:]:
        cp.wait()

    lane_head = lax.broadcasted_iota(jnp.int32, (TOK, quad), 1) // HEAD_DIM

    def attend(a_loc, b_loc):
        out = []
        for p in range(width // quad):
            cols = slice(p * quad, (p + 1) * quad)
            q = qs[a_loc, :, cols]
            k = ks[b_loc, :, cols].astype(BF16)
            v = vs[b_loc, :, cols].astype(BF16)
            q4 = jnp.concatenate(
                [jnp.where(lane_head == h, q, 0.0) for h in range(heads_quad)], axis=0
            ).astype(BF16)
            s = lax.dot_general(k, q4, (((1,), (1,)), ((), ())), preferred_element_type=F32)
            e = jnp.exp(s - jnp.max(s, axis=0, keepdims=True))
            probs = (e / jnp.sum(e, axis=0, keepdims=True)).astype(BF16)
            r = lax.dot_general(probs, v, (((0,), (0,)), ((), ())), preferred_element_type=F32)
            o = r[3 * TOK :]
            for h in (2, 1, 0):
                o = jnp.where(lane_head == h, r[h * TOK : (h + 1) * TOK], o)
            out.append(o)
        return jnp.concatenate(out, axis=1)

    def group(first, here, pairs_in):
        locs = []
        for i in range(pairs_in):
            word = slots_s[first + i, 0]
            a_loc = word // 512
            b_loc = (word // 16) % 32
            locs.append((a_loc, b_loc, word % 16))
            att[pl.ds(i * TOK, TOK), :] = attend(a_loc, b_loc)
        rows = pl.ds(0, pairs_in * TOK)
        query = jnp.concatenate([side[a_loc] for a_loc, _, _ in locs], axis=0)
        hidden = query + jnp.dot(att[rows, :].astype(BF16), wo[...], preferred_element_type=F32)
        hn = norm(hidden).astype(BF16)
        u = jnp.dot(hn, up[...], preferred_element_type=F32)
        ex = (0.5 * u) * (1.0 + lax.erf(u * (0.5**0.5)))
        ffn[rows, :] = hidden + jnp.dot(
            ex.astype(BF16), down[...], preferred_element_type=F32
        )
        for i in range(pairs_in):
            a_loc, b_loc, lev = locs[i]

            @pl.when(first + i < here)
            def _(i=i, a_loc=a_loc, b_loc=b_loc, lev=lev):
                feature = table_ref[lev] * ffn[pl.ds(i * TOK, TOK), :]
                feature = feature.astype(BF16).astype(F32)
                acc_a[a_loc] = acc_a[a_loc] + feature
                acc_b[b_loc] = acc_b[b_loc] + feature

    def slot_block(block, carry):
        here = jnp.minimum(count - block * SLOTS, SLOTS)
        wide = (here + GROUP - HALF - 1) // GROUP

        def wide_group(g, carry2):
            group(g * GROUP, here, GROUP)
            return carry2

        lax.fori_loop(0, wide, wide_group, 0)

        @pl.when(wide * GROUP < here)
        def _():
            group(wide * GROUP, here, HALF)

        @pl.when((block + 1) * SLOTS < count)
        def _():
            select(block + 1)
            fetch_slots().wait()

        return carry

    fetch_slots().wait()
    lax.fori_loop(0, (count + SLOTS - 1) // SLOTS, slot_block, 0)
    pa_ref[...] = acc_a[...].reshape(SIDE, width).astype(BF16)
    pb_ref[...] = acc_b[...].reshape(SIDE, width).astype(BF16)


def cell(table, pairs, a_blk, b_blk, wq, wkv, wo, up, down):
    width, ff = up.shape
    vmem = pl.BlockSpec(memory_space=pltpu.VMEM)
    smem = pl.BlockSpec(memory_space=pltpu.SMEM)
    anym = pl.BlockSpec(memory_space=pltpu.HBM)
    images = 4 * IMG_DEV
    return pl.pallas_call(
        cell_kernel,
        out_shape=(
            jax.ShapeDtypeStruct((SIDE, width), BF16),
            jax.ShapeDtypeStruct((SIDE, width), BF16),
        ),
        in_specs=[smem, vmem] + [anym] * 7,
        out_specs=(vmem, vmem),
        scratch_shapes=[
            pltpu.VMEM((SIDE, width), BF16),
            pltpu.VMEM((SIDE, width), BF16),
            pltpu.VMEM((width, width), BF16),
            pltpu.VMEM((width, 2 * width), BF16),
            pltpu.VMEM((width, width), BF16),
            pltpu.VMEM((width, ff), BF16),
            pltpu.VMEM((ff, width), BF16),
            pltpu.VMEM((images, TOK, width), F32),
            pltpu.VMEM((images, TOK, width), F32),
            pltpu.VMEM((images, TOK, width), F32),
            pltpu.VMEM((images, TOK, width), F32),
            pltpu.VMEM((images, TOK, width), F32),
            pltpu.VMEM((images, TOK, width), F32),
            pltpu.VMEM((PAIR_DEV, DEVS), jnp.int32),
            pltpu.VMEM((PAIR_DEV, DEVS), jnp.int32),
            pltpu.VMEM((SLOTS, 128), jnp.int32),
            pltpu.SMEM((SLOTS, 128), jnp.int32),
            pltpu.VMEM((GROUP * TOK, width), F32),
            pltpu.VMEM((GROUP * TOK, width), F32),
            pltpu.SemaphoreType.DMA((8,)),
        ],
        compiler_params=pltpu.CompilerParams(vmem_limit_bytes=VMEM_ALL),
        name="cell_pairs",
    )(table, pairs, a_blk, b_blk, wq, wkv, wo, up, down)


def reduce_kernel(
    pa_hbm,
    pb_hbm,
    out_ref,
    pb,
    ra,
    rsib,
    sb,
    rz,
    tot,
    ry,
    loc,
    a_send,
    a_recv,
    s_send,
    s_recv,
    z_send,
    z_recv,
    y_send,
    y_recv,
    o_send,
    o_recv,
):
    z, x, c, y = place()
    self_a = x // 2 == c
    self_b = y == 0

    def block(s):
        return pl.ds(pl.multiple_of(s * BLK, BLK), BLK)

    def y_rows(yy):
        return pl.ds(pl.multiple_of(yy * SHARE, SHARE), SHARE)

    keep = []
    for t in range(2):
        cp = pltpu.make_async_copy(pb_hbm.at[block(t * 2 + c)], pb.at[t], loc.at[t])
        cp.start()
        keep.append(cp)
    own_a = pltpu.make_async_copy(pa_hbm.at[block((x % 2) * 2 + c)], ra.at[x], loc.at[2])

    @pl.when(self_a)
    def _():
        own_a.start()

    barrier = pltpu.get_barrier_semaphore()
    for p in row_peers(z, x, c, y) + y_peers(z, x, c, y):
        pl.semaphore_signal(barrier, inc=1, device_id=p, device_id_type=MESH)
    for ys in range(NY):
        for zh in range(2):
            zs = (z + NZ - ys) % 4 + 4 * zh
            here = jnp.logical_and(ys == y, zs == z)

            @pl.when(jnp.logical_not(here))
            def _(zs=zs, ys=ys):
                pl.semaphore_signal(
                    barrier, inc=1, device_id=dev(zs, x, c, ys), device_id_type=MESH
                )

    pl.semaphore_wait(barrier, 7 + NY - 1 + 2 * NY - jnp.where(self_b, 1, 0))
    sib = dev(z, x, 1 - c, y)

    width = out_ref.shape[1]

    def cols(n):
        return pl.ds(n * (width // PARTS), width // PARTS)

    sib_cps = {}
    for n in range(PARTS):
        for t in range(2):
            i = n * 2 + t
            sib_cps[i] = remote(
                pb_hbm.at[block(t * 2 + 1 - c), cols(n)],
                rsib.at[t, :, cols(n)],
                s_send.at[i],
                s_recv.at[i],
                sib,
            )
            sib_cps[i].start()

    a_cps = []
    for n in range(PARTS):
        for s in range(4):
            xt = 2 * c + s // 2
            here = jnp.logical_and(xt == x, c == s % 2)
            cp = remote(
                pa_hbm.at[block(s), cols(n)],
                ra.at[x, :, cols(n)],
                a_send.at[n * 4 + s],
                a_recv.at[n * 4 + x],
                dev(z, xt, s % 2, y),
            )
            a_cps.append((here, cp))

            @pl.when(jnp.logical_not(here))
            def _(cp=cp):
                cp.start()

    j = (z + y) % 4
    z_cps = []
    slot = y * 2 + z // 4
    for cp in keep:
        cp.wait()
    for n in range(PARTS):
        for t in range(2):
            sib_cps[n * 2 + t].wait_recv()
            total = pb[t, :, cols(n)].astype(F32) + rsib[t, :, cols(n)].astype(F32)
            sb[t, :, cols(n)] = total.astype(BF16)
            zt = j + 4 * t
            for q in range(NY):
                piece = pl.ds(q * SHARE, SHARE)
                here = jnp.logical_and(zt == z, q == y)
                cp = remote(
                    sb.at[t, piece, cols(n)],
                    rz.at[slot, :, cols(n)],
                    z_send.at[n * 8 + q * 2 + t],
                    z_recv.at[n * 8 + slot],
                    dev(zt, x, c, q),
                )
                z_cps.append((here, cp))

                @pl.when(jnp.logical_not(here))
                def _(cp=cp):
                    cp.start()

                @pl.when(here)
                def _(t=t, piece=piece, n=n):
                    rz[slot, :, cols(n)] = sb[t, piece, cols(n)]

    @pl.when(self_a)
    def _():
        own_a.wait()

    y_cps = {}
    for n in range(PARTS):
        for s in range(4):
            here = jnp.logical_and(s == x, self_a)

            @pl.when(jnp.logical_not(here))
            def _(s=s, n=n):
                remote(
                    pa_hbm.at[block(0), cols(n)],
                    ra.at[s, :, cols(n)],
                    a_send.at[0],
                    a_recv.at[n * 4 + s],
                    sib,
                ).wait_recv()

        total = (
            ra[0, :, cols(n)].astype(F32)
            + ra[1, :, cols(n)].astype(F32)
            + ra[2, :, cols(n)].astype(F32)
            + ra[3, :, cols(n)].astype(F32)
        )
        tot[:, cols(n)] = total.astype(BF16)
        for d in range(1, NY):
            yt = (y + d) % NY
            cp = remote(
                tot.at[y_rows(yt), cols(n)],
                ry.at[d, :, cols(n)],
                y_send.at[n * 4 + d],
                y_recv.at[n * 4 + d],
                dev(z, x, c, yt),
            )
            cp.start()
            y_cps[n * 4 + d] = cp

    o_cps = []
    for n in range(PARTS):
        mine = tot[y_rows(y), cols(n)].astype(F32)
        for d in range(1, NY):
            y_cps[n * 4 + d].wait_recv()
            mine = mine + ry[d, :, cols(n)].astype(F32)
        for ys in range(NY):
            for zh in range(2):
                s = ys * 2 + zh
                here = jnp.logical_and(jnp.logical_and(self_b, ys == 0), z // 4 == zh)

                @pl.when(jnp.logical_not(here))
                def _(s=s, n=n):
                    remote(
                        sb.at[0, pl.ds(0, SHARE), cols(n)],
                        rz.at[s, :, cols(n)],
                        z_send.at[0],
                        z_recv.at[n * 8 + s],
                        sib,
                    ).wait_recv()

        for s in range(2 * NY):
            mine = mine + rz[s, :, cols(n)].astype(F32)
        out_ref[y_rows(y), cols(n)] = mine.astype(BF16)
        for d in range(1, NY):
            piece = out_ref.at[y_rows(y), cols(n)]
            cp = remote(
                piece,
                piece,
                o_send.at[n * 4 + d],
                o_recv.at[n * 4 + d],
                dev(z, x, c, (y + d) % NY),
            )
            cp.start()
            o_cps.append(cp)
    for n in range(PARTS):
        for d in range(1, NY):
            piece = out_ref.at[y_rows((y - d + NY) % NY), cols(n)]
            remote(piece, piece, o_send.at[d], o_recv.at[n * 4 + d], sib).wait_recv()

    for cp in list(sib_cps.values()) + list(y_cps.values()) + o_cps:
        cp.wait_send()
    for here, cp in a_cps + z_cps:

        @pl.when(jnp.logical_not(here))
        def _(cp=cp):
            cp.wait_send()


def reduce_back(pa, pb):
    width = pa.shape[1]
    dma = pltpu.SemaphoreType.DMA
    vmem = pl.BlockSpec(memory_space=pltpu.VMEM)
    return pl.pallas_call(
        reduce_kernel,
        out_shape=jax.ShapeDtypeStruct((BLK, width), BF16),
        in_specs=[pl.BlockSpec(memory_space=pltpu.HBM)] * 2,
        out_specs=vmem,
        scratch_shapes=[
            pltpu.VMEM((2, BLK, width), BF16),
            pltpu.VMEM((4, BLK, width), BF16),
            pltpu.VMEM((2, BLK, width), BF16),
            pltpu.VMEM((2, BLK, width), BF16),
            pltpu.VMEM((2 * NY, SHARE, width), BF16),
            pltpu.VMEM((BLK, width), BF16),
            pltpu.VMEM((NY, SHARE, width), BF16),
            dma((3,)),
            dma((4 * PARTS,)),
            dma((4 * PARTS,)),
            dma((2 * PARTS,)),
            dma((2 * PARTS,)),
            dma((8 * PARTS,)),
            dma((8 * PARTS,)),
            dma((4 * PARTS,)),
            dma((4 * PARTS,)),
            dma((4 * PARTS,)),
            dma((4 * PARTS,)),
        ],
        compiler_params=pltpu.CompilerParams(
            collective_id=1, has_side_effects=True, vmem_limit_bytes=VMEM_ALL
        ),
        name="reduce_back",
    )(pa, pb)


def body(
    tokens,
    proj_in,
    attn_query,
    attn_keyval,
    attn_output,
    mlp_up,
    mlp_down,
    pair_list,
    conf_level,
    conf_table,
):
    img_dev, tok_count, enc_width = tokens.shape
    a_blk, b_blk, pairs = gather(
        tokens.reshape(img_dev * tok_count, enc_width),
        proj_in,
        pair_list.T,
        conf_level.reshape(1, PAIR_DEV),
    )
    pa, pb = cell(
        conf_table, pairs, a_blk, b_blk, attn_query, attn_keyval, attn_output, mlp_up, mlp_down
    )
    joined = reduce_back(pa, pb)
    return joined.reshape(img_dev, tok_count, joined.shape[1])


def solution(mesh):
    placed = (
        P("img", None, None),
        P(),
        P(),
        P(),
        P(),
        P(),
        P(),
        P(("img", "rep"), None),
        P(("img", "rep")),
        P(),
    )
    return jax.shard_map(
        body, mesh=mesh, in_specs=placed, out_specs=P("img", None, None), check_vma=False
    )
```

```python
import jax
import jax.numpy as jnp
from jax import lax
from jax.experimental import pallas as pl
from jax.experimental.pallas import tpu as pltpu
from jax.sharding import PartitionSpec as P

HEAD_DIM = 64
TOK = 24
IMG_DEV = 8
NX, NY, NZ = 4, 4, 8
BLK = IMG_DEV * TOK
SIDE = 4 * BLK
DEVS = NX * NY * NZ * 2
PAIR_DEV = 32
GROUP = 16
HALF = 8
SLOTS = 64
PARTS = 2
VMEM_ALL = 64 * 1024 * 1024
SHARE = BLK // NY
FAR = 128
MESH = pl.DeviceIdType.MESH
F32 = jnp.float32
BF16 = jnp.bfloat16


def place():
    img = lax.axis_index("img")
    return img // 8, (img // 2) % 4, img % 2, lax.axis_index("rep")


def dev(z, x, c, y):
    return ((z * NX + x) * 2 + c, y)


def remote(src, dst, send, recv, to):
    return pltpu.make_async_remote_copy(
        src_ref=src,
        dst_ref=dst,
        send_sem=send,
        recv_sem=recv,
        device_id=to,
        device_id_type=MESH,
    )


def row_peers(z, x, c, y):
    ks = [(x * 2 + c + d) % 8 for d in range(1, 8)]
    return [dev(z, k // 2, k % 2, y) for k in ks]


def z_peers(z, x, c, y):
    return [dev((z + d) % NZ, x, c, y) for d in range(1, NZ)]


def y_peers(z, x, c, y):
    return [dev(z, x, c, (y + d) % NY) for d in range(1, NY)]


def barrier_all(z, x, c, y):
    barrier = pltpu.get_barrier_semaphore()
    peers = row_peers(z, x, c, y) + z_peers(z, x, c, y) + y_peers(z, x, c, y)
    for p in peers:
        pl.semaphore_signal(barrier, inc=1, device_id=p, device_id_type=MESH)
    return barrier, len(peers)


def far_target(z, y):
    return (z + jnp.where(y == 1, 3, 5)) % NZ


def far_source(z, y):
    return (z + jnp.where(y == 1, 5, 3)) % NZ


def gather_kernel(
    tok_hbm,
    proj_hbm,
    pair_hbm,
    level_hbm,
    a_out,
    b_out,
    list_out,
    tok,
    proj,
    pair_ref,
    level_ref,
    own,
    a_send,
    a_recv,
    b_send,
    b_recv,
    f_send,
    f_recv,
    loc,
    lx_send,
    lx_recv,
    lz_send,
    lz_recv,
    ly_send,
    ly_recv,
):
    z, x, c, y = place()
    tok_in = pltpu.make_async_copy(tok_hbm, tok, loc.at[2])
    proj_in = pltpu.make_async_copy(proj_hbm, proj, loc.at[3])
    pair_in = pltpu.make_async_copy(pair_hbm, pair_ref, loc.at[4])
    level_in = pltpu.make_async_copy(level_hbm, level_ref, loc.at[5])
    inputs = (pair_in, level_in, tok_in, proj_in)
    for cp in inputs:
        cp.start()
    barrier, n_peers = barrier_all(z, x, c, y)
    odd = y % 2 == 1
    other = (y + 2) % NY

    @pl.when(odd)
    def _():
        source = dev(far_source(z, y), x, c, other)
        pl.semaphore_signal(barrier, inc=1, device_id=source, device_id_type=MESH)

    for cp in inputs:
        cp.wait()
    own[...] = jnp.dot(tok[...], proj[...], preferred_element_type=F32).astype(BF16)
    me8 = x * 2 + c
    row_me = y * 64 + me8 * 8 + z
    list_out[row_me, :, 0:PAIR_DEV] = pair_ref[0:1, :]
    list_out[row_me, :, PAIR_DEV : 2 * PAIR_DEV] = pair_ref[1:2, :]
    list_out[row_me, :, 2 * PAIR_DEV : 3 * PAIR_DEV] = level_ref[...]
    list_out[row_me, :, 3 * PAIR_DEV :] = jnp.zeros((1, 128 - 3 * PAIR_DEV), jnp.int32)
    pl.semaphore_wait(barrier, n_peers + jnp.where(odd, 1, 0))

    lz = []
    for d in range(1, NZ):
        mine = list_out.at[pl.ds(row_me, 1)]
        cp = remote(mine, mine, lz_send.at[d], lz_recv.at[d], dev((z + d) % NZ, x, c, y))
        cp.start()
        lz.append(cp)

    s_b = (z // 4) * 2 + c
    b_dst = b_out.at[pl.ds(pl.multiple_of(s_b * BLK, BLK), BLK)]
    z0 = (z - y + NZ) % NZ
    z1 = (z - y + NZ + 4) % NZ
    self_b = y == 0
    b0_local = pltpu.make_async_copy(own, b_dst, loc.at[0])

    @pl.when(self_b)
    def _():
        b0_local.start()

    near_dst = b_out.at[pl.ds(pl.multiple_of(s_b * BLK, BLK), FAR)]
    far_dst = b_out.at[pl.ds(pl.multiple_of(s_b * BLK + FAR, BLK - FAR), BLK - FAR)]
    over = dev(far_target(z, other), x, c, other)
    cross = remote(own.at[pl.ds(FAR, BLK - FAR)], far_dst, b_send.at[2], b_recv.at[2], over)
    b_cps = [(odd, cross)]
    for t, zt in ((1, z1), (0, z0)):
        far = y == (1 if t == 1 else 3)
        whole = remote(own, b_dst, b_send.at[t], b_recv.at[z // 4], dev(zt, x, c, y))
        most = remote(
            own.at[pl.ds(0, FAR)], near_dst, b_send.at[t], b_recv.at[z // 4], dev(zt, x, c, y)
        )
        b_cps.append((far, most))
        full = jnp.logical_not(far)
        b_cps.append((jnp.logical_and(full, jnp.logical_not(self_b)) if t == 0 else full, whole))
    for go, cp in b_cps:

        @pl.when(go)
        def _(cp=cp):
            cp.start()

    for cp in lz:
        cp.wait_recv()
    lx = []
    for d in range(1, 8):
        k = (me8 + d) % 8
        rows = list_out.at[pl.ds(y * 64 + me8 * 8, 8)]
        cp = remote(rows, rows, lx_send.at[d], lx_recv.at[d], dev(z, k // 2, k % 2, y))
        cp.start()
        lx.append(cp)

    s_a = (x % 2) * 2 + c
    a_dst = a_out.at[pl.ds(pl.multiple_of(s_a * BLK, BLK), BLK)]
    half = x // 2
    self_a = half == c
    a_cps = []
    for d in (2, 1, 3):
        cp = remote(own, a_dst, a_send.at[d], a_recv.at[s_a], dev(z, (x + d) % NX, half, y))
        cp.start()
        a_cps.append(cp)
    a0 = remote(own, a_dst, a_send.at[0], a_recv.at[s_a], dev(z, x, half, y))
    a0_local = pltpu.make_async_copy(own, a_dst, loc.at[1])

    @pl.when(jnp.logical_not(self_a))
    def _():
        a0.start()

    @pl.when(self_a)
    def _():
        a0_local.start()

    for cp in lx:
        cp.wait_recv()
    ly = []
    for d in range(1, NY):
        rows = list_out.at[pl.ds(y * 64, 64)]
        cp = remote(rows, rows, ly_send.at[d], ly_recv.at[d], dev(z, x, c, (y + d) % NY))
        cp.start()
        ly.append(cp)

    sib = dev(z, x, 1 - c, y)
    fwd = []
    for t in range(2):
        base = (t * 2 + c) * BLK
        slot = b_out.at[pl.ds(pl.multiple_of(base, BLK), BLK)]
        arrived = remote(own, slot, b_send.at[t], b_recv.at[t], sib)
        most = remote(
            own.at[pl.ds(0, FAR)],
            b_out.at[pl.ds(pl.multiple_of(base, BLK), FAR)],
            b_send.at[t],
            b_recv.at[t],
            sib,
        )
        rest = remote(
            own.at[pl.ds(FAR, BLK - FAR)],
            b_out.at[pl.ds(pl.multiple_of(base + FAR, BLK - FAR), BLK - FAR)],
            b_send.at[2],
            b_recv.at[2],
            sib,
        )
        here = jnp.logical_and(self_b, z // 4 == t)
        split = jnp.logical_and(odd, far_source(z, y) // 4 == t)

        @pl.when(jnp.logical_not(jnp.logical_or(here, split)))
        def _(arrived=arrived):
            arrived.wait_recv()

        @pl.when(split)
        def _(most=most, rest=rest):
            most.wait_recv()
            rest.wait_recv()

        @pl.when(here)
        def _():
            b0_local.wait()

        cp = remote(slot, slot, f_send.at[t], f_recv.at[t], sib)
        cp.start()
        fwd.append(cp)

    for s in range(4):
        slot = a_out.at[pl.ds(s * BLK, BLK)]
        arrived = remote(own, slot, a_send.at[0], a_recv.at[s], sib)
        here = jnp.logical_and(self_a, s_a == s)

        @pl.when(jnp.logical_not(here))
        def _(arrived=arrived):
            arrived.wait_recv()

        @pl.when(here)
        def _():
            a0_local.wait()

    for t in range(2):
        slot = b_out.at[pl.ds(pl.multiple_of((t * 2 + 1 - c) * BLK, BLK), BLK)]
        remote(slot, slot, f_send.at[t], f_recv.at[t], sib).wait_recv()
    for cp in ly:
        cp.wait_recv()

    for cp in lx + lz + ly + a_cps + fwd:
        cp.wait_send()

    for go, cp in b_cps:

        @pl.when(go)
        def _(cp=cp):
            cp.wait_send()

    @pl.when(jnp.logical_not(self_a))
    def _():
        a0.wait_send()


def gather(tokens, proj_in, pairs_t, levels):
    width = proj_in.shape[1]
    dma = pltpu.SemaphoreType.DMA
    vmem = pl.BlockSpec(memory_space=pltpu.VMEM)
    anym = pl.BlockSpec(memory_space=pltpu.HBM)
    return pl.pallas_call(
        gather_kernel,
        out_shape=(
            jax.ShapeDtypeStruct((SIDE, width), BF16),
            jax.ShapeDtypeStruct((SIDE, width), BF16),
            jax.ShapeDtypeStruct((DEVS, 1, 128), jnp.int32),
        ),
        in_specs=[anym] * 4,
        out_specs=(anym, anym, vmem),
        scratch_shapes=[
            pltpu.VMEM(tokens.shape, BF16),
            pltpu.VMEM(proj_in.shape, BF16),
            pltpu.VMEM(pairs_t.shape, jnp.int32),
            pltpu.VMEM(levels.shape, jnp.int32),
            pltpu.VMEM((BLK, width), BF16),
            dma((4,)),
            dma((4,)),
            dma((3,)),
            dma((3,)),
            dma((2,)),
            dma((2,)),
            dma((6,)),
            dma((8,)),
            dma((8,)),
            dma((8,)),
            dma((8,)),
            dma((4,)),
            dma((4,)),
        ],
        compiler_params=pltpu.CompilerParams(
            collective_id=0, has_side_effects=True, vmem_limit_bytes=VMEM_ALL
        ),
        name="gather_blocks",
    )(tokens, proj_in, pairs_t, levels)


def norm(v):
    centred = v - jnp.mean(v, axis=-1, keepdims=True)
    spread = jnp.mean(centred * centred, axis=-1, keepdims=True)
    return centred * lax.rsqrt(spread + 1e-06)


def cell_kernel(
    table_ref,
    list_ref,
    a_hbm,
    b_hbm,
    wq_hbm,
    wkv_hbm,
    wo_hbm,
    up_hbm,
    down_hbm,
    pa_ref,
    pb_ref,
    a_ref,
    b_ref,
    wq,
    wkv,
    wo,
    up,
    down,
    side,
    qs,
    ks,
    vs,
    acc_a,
    acc_b,
    rank_t,
    val_t,
    slots_v,
    slots_s,
    att,
    ffn,
    sems,
):
    width = wq.shape[0]
    heads_quad = 4
    quad = heads_quad * HEAD_DIM
    copies = [
        pltpu.make_async_copy(h, v, sems.at[i])
        for i, (h, v) in enumerate(
            (
                (a_hbm, a_ref),
                (wq_hbm, wq),
                (b_hbm, b_ref),
                (wkv_hbm, wkv),
                (wo_hbm, wo),
                (up_hbm, up),
                (down_hbm, down),
            )
        )
    ]
    for cp in copies:
        cp.start()

    z, x, c, y = place()
    a_id, b_x, b_j = z * 2 + c, x, (z + y) % 4
    flat = list_ref[...].reshape(DEVS, 128)
    flat_t = flat.astype(F32).T.astype(jnp.int32)
    a_img = flat_t[:PAIR_DEV]
    b_img = flat_t[PAIR_DEV : 2 * PAIR_DEV]
    level = flat_t[2 * PAIR_DEV : 3 * PAIR_DEV]
    hit = (
        (lax.shift_right_logical(a_img, 5) == a_id)
        & ((lax.shift_right_logical(b_img, 4) & 3) == b_x)
        & ((lax.shift_right_logical(b_img, 6) & 3) == b_j)
    )
    hit_f = hit.astype(F32)
    r_i = lax.broadcasted_iota(jnp.int32, (DEVS, DEVS), 0)
    c_i = lax.broadcasted_iota(jnp.int32, (DEVS, DEVS), 1)
    upper = (r_i <= c_i).astype(BF16)
    across = jnp.dot(hit_f.astype(BF16), upper, preferred_element_type=F32)
    totals = across[:, DEVS - 1 : DEVS]
    k_r = lax.broadcasted_iota(jnp.int32, (PAIR_DEV, PAIR_DEV), 0)
    k_c = lax.broadcasted_iota(jnp.int32, (PAIR_DEV, PAIR_DEV), 1)
    lower = (k_c < k_r).astype(BF16)
    before = jnp.dot(
        lower,
        jnp.broadcast_to(totals, (PAIR_DEV, 128)).astype(BF16),
        preferred_element_type=F32,
    )[:, :1]
    rank = (across + before).astype(jnp.int32) - 1
    rank_t[...] = jnp.where(hit, rank, -1)
    val_t[...] = ((a_img & 31) * 32 + (lax.shift_right_logical(b_img, 8) * 16 + (b_img & 15))) * 16 + level
    count = jnp.sum(hit_f).astype(jnp.int32)

    def fetch_slots():
        return pltpu.make_async_copy(slots_v, slots_s, sems.at[7])

    def select(block):
        slot = lax.broadcasted_iota(jnp.int32, (SLOTS, DEVS), 0) + block * SLOTS
        found = jnp.zeros((SLOTS, DEVS), jnp.int32)
        for k in range(PAIR_DEV):
            found += jnp.where(rank_t[k : k + 1, :] == slot, val_t[k : k + 1, :], 0)
        col = jnp.sum(found.astype(F32), axis=1, keepdims=True).astype(jnp.int32)
        slots_v[...] = jnp.broadcast_to(col, (SLOTS, 128))
        fetch_slots().start()

    select(0)
    acc_a[...] = jnp.zeros_like(acc_a)
    acc_b[...] = jnp.zeros_like(acc_b)

    for cp in copies[:4]:
        cp.wait()
    for i in range(4):
        rows = pl.ds(i * BLK, BLK)
        q_side = a_ref[rows, :].astype(F32)
        side[pl.ds(i * IMG_DEV, IMG_DEV)] = q_side.reshape(IMG_DEV, TOK, width)
        qn = norm(q_side).astype(BF16)
        q = jnp.dot(qn, wq[...], preferred_element_type=F32).astype(BF16).astype(F32)
        qs[pl.ds(i * IMG_DEV, IMG_DEV)] = (q * (HEAD_DIM**-0.5)).reshape(IMG_DEV, TOK, width)
        mn = norm(b_ref[rows, :].astype(F32)).astype(BF16)
        k = jnp.dot(mn, wkv[:, :width], preferred_element_type=F32)
        ks[pl.ds(i * IMG_DEV, IMG_DEV)] = k.reshape(IMG_DEV, TOK, width)
        v = jnp.dot(mn, wkv[:, width:], preferred_element_type=F32)
        vs[pl.ds(i * IMG_DEV, IMG_DEV)] = v.reshape(IMG_DEV, TOK, width)
    for cp in copies[4:]:
        cp.wait()

    lane_head = lax.broadcasted_iota(jnp.int32, (TOK, quad), 1) // HEAD_DIM

    def attend(a_loc, b_loc):
        out = []
        for p in range(width // quad):
            cols = slice(p * quad, (p + 1) * quad)
            q = qs[a_loc, :, cols]
            k = ks[b_loc, :, cols].astype(BF16)
            v = vs[b_loc, :, cols].astype(BF16)
            q4 = jnp.concatenate(
                [jnp.where(lane_head == h, q, 0.0) for h in range(heads_quad)], axis=0
            ).astype(BF16)
            s = lax.dot_general(k, q4, (((1,), (1,)), ((), ())), preferred_element_type=F32)
            e = jnp.exp(s - jnp.max(s, axis=0, keepdims=True))
            probs = (e / jnp.sum(e, axis=0, keepdims=True)).astype(BF16)
            r = lax.dot_general(probs, v, (((0,), (0,)), ((), ())), preferred_element_type=F32)
            o = r[3 * TOK :]
            for h in (2, 1, 0):
                o = jnp.where(lane_head == h, r[h * TOK : (h + 1) * TOK], o)
            out.append(o)
        return jnp.concatenate(out, axis=1)

    def group(first, here, pairs_in):
        locs = []
        for i in range(pairs_in):
            word = slots_s[first + i, 0]
            a_loc = word // 512
            b_loc = (word // 16) % 32
            locs.append((a_loc, b_loc, word % 16))
            att[pl.ds(i * TOK, TOK), :] = attend(a_loc, b_loc)
        rows = pl.ds(0, pairs_in * TOK)
        query = jnp.concatenate([side[a_loc] for a_loc, _, _ in locs], axis=0)
        hidden = query + jnp.dot(att[rows, :].astype(BF16), wo[...], preferred_element_type=F32)
        hn = norm(hidden).astype(BF16)
        u = jnp.dot(hn, up[...], preferred_element_type=F32)
        ex = (0.5 * u) * (1.0 + lax.erf(u * (0.5**0.5)))
        ffn[rows, :] = hidden + jnp.dot(
            ex.astype(BF16), down[...], preferred_element_type=F32
        )
        for i in range(pairs_in):
            a_loc, b_loc, lev = locs[i]

            @pl.when(first + i < here)
            def _(i=i, a_loc=a_loc, b_loc=b_loc, lev=lev):
                feature = table_ref[lev] * ffn[pl.ds(i * TOK, TOK), :]
                feature = feature.astype(BF16).astype(F32)
                acc_a[a_loc] = acc_a[a_loc] + feature
                acc_b[b_loc] = acc_b[b_loc] + feature

    def slot_block(block, carry):
        here = jnp.minimum(count - block * SLOTS, SLOTS)
        wide = (here + GROUP - HALF - 1) // GROUP

        def wide_group(g, carry2):
            group(g * GROUP, here, GROUP)
            return carry2

        lax.fori_loop(0, wide, wide_group, 0)

        @pl.when(wide * GROUP < here)
        def _():
            group(wide * GROUP, here, HALF)

        @pl.when((block + 1) * SLOTS < count)
        def _():
            select(block + 1)
            fetch_slots().wait()

        return carry

    fetch_slots().wait()
    lax.fori_loop(0, (count + SLOTS - 1) // SLOTS, slot_block, 0)
    pa_ref[...] = acc_a[...].reshape(SIDE, width).astype(BF16)
    pb_ref[...] = acc_b[...].reshape(SIDE, width).astype(BF16)


def cell(table, pairs, a_blk, b_blk, wq, wkv, wo, up, down):
    width, ff = up.shape
    vmem = pl.BlockSpec(memory_space=pltpu.VMEM)
    smem = pl.BlockSpec(memory_space=pltpu.SMEM)
    anym = pl.BlockSpec(memory_space=pltpu.HBM)
    images = 4 * IMG_DEV
    return pl.pallas_call(
        cell_kernel,
        out_shape=(
            jax.ShapeDtypeStruct((SIDE, width), BF16),
            jax.ShapeDtypeStruct((SIDE, width), BF16),
        ),
        in_specs=[smem, vmem] + [anym] * 7,
        out_specs=(vmem, vmem),
        scratch_shapes=[
            pltpu.VMEM((SIDE, width), BF16),
            pltpu.VMEM((SIDE, width), BF16),
            pltpu.VMEM((width, width), BF16),
            pltpu.VMEM((width, 2 * width), BF16),
            pltpu.VMEM((width, width), BF16),
            pltpu.VMEM((width, ff), BF16),
            pltpu.VMEM((ff, width), BF16),
            pltpu.VMEM((images, TOK, width), F32),
            pltpu.VMEM((images, TOK, width), F32),
            pltpu.VMEM((images, TOK, width), F32),
            pltpu.VMEM((images, TOK, width), F32),
            pltpu.VMEM((images, TOK, width), F32),
            pltpu.VMEM((images, TOK, width), F32),
            pltpu.VMEM((PAIR_DEV, DEVS), jnp.int32),
            pltpu.VMEM((PAIR_DEV, DEVS), jnp.int32),
            pltpu.VMEM((SLOTS, 128), jnp.int32),
            pltpu.SMEM((SLOTS, 128), jnp.int32),
            pltpu.VMEM((GROUP * TOK, width), F32),
            pltpu.VMEM((GROUP * TOK, width), F32),
            pltpu.SemaphoreType.DMA((8,)),
        ],
        compiler_params=pltpu.CompilerParams(vmem_limit_bytes=VMEM_ALL),
        name="cell_pairs",
    )(table, pairs, a_blk, b_blk, wq, wkv, wo, up, down)


def reduce_kernel(
    pa_hbm,
    pb_hbm,
    out_ref,
    pb,
    ra,
    rsib,
    sb,
    rz,
    tot,
    ry,
    rx,
    relay,
    loc,
    a_send,
    a_recv,
    s_send,
    s_recv,
    z_send,
    z_recv,
    y_send,
    y_recv,
    o_send,
    o_recv,
    x_send,
    x_recv,
    h_send,
):
    z, x, c, y = place()
    self_a = x // 2 == c
    self_b = y == 0

    def block(s):
        return pl.ds(pl.multiple_of(s * BLK, BLK), BLK)

    def y_rows(yy):
        return pl.ds(pl.multiple_of(yy * SHARE, SHARE), SHARE)

    keep = []
    for t in range(2):
        cp = pltpu.make_async_copy(pb_hbm.at[block(t * 2 + c)], pb.at[t], loc.at[t])
        cp.start()
        keep.append(cp)
    own_a = pltpu.make_async_copy(pa_hbm.at[block((x % 2) * 2 + c)], ra.at[x], loc.at[2])

    @pl.when(self_a)
    def _():
        own_a.start()

    barrier = pltpu.get_barrier_semaphore()
    for p in row_peers(z, x, c, y) + y_peers(z, x, c, y):
        pl.semaphore_signal(barrier, inc=1, device_id=p, device_id_type=MESH)
    for ys in range(NY):
        for zh in range(2):
            zs = (z + NZ - ys) % 4 + 4 * zh
            here = jnp.logical_and(ys == y, zs == z)

            @pl.when(jnp.logical_not(here))
            def _(zs=zs, ys=ys):
                pl.semaphore_signal(
                    barrier, inc=1, device_id=dev(zs, x, c, ys), device_id_type=MESH
                )

    odd = y % 2 == 1
    other = (y + 2) % NY

    @pl.when(odd)
    def _():
        for p in (dev(z, x, 1 - c, other), dev(far_target(z, other), x, c, y)):
            pl.semaphore_signal(barrier, inc=1, device_id=p, device_id_type=MESH)

    extra = jnp.where(odd, 2, jnp.where(self_b, -1, 0))
    pl.semaphore_wait(barrier, 7 + NY - 1 + 2 * NY + extra)
    sib = dev(z, x, 1 - c, y)

    width = out_ref.shape[1]

    def cols(n):
        return pl.ds(n * (width // PARTS), width // PARTS)

    sib_cps = {}
    for n in range(PARTS):
        for t in range(2):
            i = n * 2 + t
            sib_cps[i] = remote(
                pb_hbm.at[block(t * 2 + 1 - c), cols(n)],
                rsib.at[t, :, cols(n)],
                s_send.at[i],
                s_recv.at[i],
                sib,
            )
            sib_cps[i].start()

    far = far_source(z, y)
    x_cps = []
    for n in range(PARTS):
        for cc in range(2):
            s = (far // 4) * 2 + cc
            piece = pl.ds(pl.multiple_of(s * BLK + other * SHARE, SHARE), SHARE)
            cp = remote(
                pb_hbm.at[piece, cols(n)],
                rx.at[c, :, cols(n)],
                x_send.at[n * 2 + cc],
                x_recv.at[n * 2 + c],
                dev(z, x, cc, other),
            )
            x_cps.append(cp)

            @pl.when(odd)
            def _(cp=cp):
                cp.start()

    a_cps = []
    for n in range(PARTS):
        for s in range(4):
            xt = 2 * c + s // 2
            here = jnp.logical_and(xt == x, c == s % 2)
            cp = remote(
                pa_hbm.at[block(s), cols(n)],
                ra.at[x, :, cols(n)],
                a_send.at[n * 4 + s],
                a_recv.at[n * 4 + x],
                dev(z, xt, s % 2, y),
            )
            a_cps.append((here, cp))

            @pl.when(jnp.logical_not(here))
            def _(cp=cp):
                cp.start()

    j = (z + y) % 4
    z_cps = []
    slot = y * 2 + z // 4
    for cp in keep:
        cp.wait()
    for n in range(PARTS):
        for t in range(2):
            sib_cps[n * 2 + t].wait_recv()
            total = pb[t, :, cols(n)].astype(F32) + rsib[t, :, cols(n)].astype(F32)
            sb[t, :, cols(n)] = total.astype(BF16)
            zt = j + 4 * t
            for q in range(NY):
                piece = pl.ds(q * SHARE, SHARE)
                here = jnp.logical_and(zt == z, q == y)
                cp = remote(
                    sb.at[t, piece, cols(n)],
                    rz.at[slot, :, cols(n)],
                    z_send.at[n * 8 + q * 2 + t],
                    z_recv.at[n * 8 + slot],
                    dev(zt, x, c, q),
                )
                turn = jnp.logical_and(odd, jnp.logical_and(far // 4 == t, q == other))
                kept = jnp.logical_or(here, turn)
                z_cps.append((kept, cp))

                @pl.when(jnp.logical_not(kept))
                def _(cp=cp):
                    cp.start()

                @pl.when(here)
                def _(t=t, piece=piece, n=n):
                    rz[slot, :, cols(n)] = sb[t, piece, cols(n)]

    h_slot = other * 2 + z // 4
    h_cps = []
    for n in range(PARTS):
        h_cps.append(
            remote(
                relay.at[:, cols(n)],
                rz.at[h_slot, :, cols(n)],
                h_send.at[n],
                z_recv.at[n * 8 + h_slot],
                dev(far_source(z, other), x, c, y),
            )
        )

        @pl.when(odd)
        def _(n=n):
            for cc in range(2):
                remote(
                    pb_hbm.at[pl.ds(0, SHARE), cols(n)],
                    rx.at[cc, :, cols(n)],
                    x_send.at[0],
                    x_recv.at[n * 2 + cc],
                    sib,
                ).wait_recv()
            both = rx[0, :, cols(n)].astype(F32) + rx[1, :, cols(n)].astype(F32)
            relay[:, cols(n)] = both.astype(BF16)
            h_cps[n].start()

    @pl.when(self_a)
    def _():
        own_a.wait()

    y_cps = {}
    for n in range(PARTS):
        for s in range(4):
            here = jnp.logical_and(s == x, self_a)

            @pl.when(jnp.logical_not(here))
            def _(s=s, n=n):
                remote(
                    pa_hbm.at[block(0), cols(n)],
                    ra.at[s, :, cols(n)],
                    a_send.at[0],
                    a_recv.at[n * 4 + s],
                    sib,
                ).wait_recv()

        total = (
            ra[0, :, cols(n)].astype(F32)
            + ra[1, :, cols(n)].astype(F32)
            + ra[2, :, cols(n)].astype(F32)
            + ra[3, :, cols(n)].astype(F32)
        )
        tot[:, cols(n)] = total.astype(BF16)
        for d in range(1, NY):
            yt = (y + d) % NY
            cp = remote(
                tot.at[y_rows(yt), cols(n)],
                ry.at[d, :, cols(n)],
                y_send.at[n * 4 + d],
                y_recv.at[n * 4 + d],
                dev(z, x, c, yt),
            )
            cp.start()
            y_cps[n * 4 + d] = cp

    o_cps = []
    for n in range(PARTS):
        mine = tot[y_rows(y), cols(n)].astype(F32)
        for d in range(1, NY):
            y_cps[n * 4 + d].wait_recv()
            mine = mine + ry[d, :, cols(n)].astype(F32)
        for ys in range(NY):
            for zh in range(2):
                s = ys * 2 + zh
                here = jnp.logical_and(jnp.logical_and(self_b, ys == 0), z // 4 == zh)

                @pl.when(jnp.logical_not(here))
                def _(s=s, n=n):
                    remote(
                        sb.at[0, pl.ds(0, SHARE), cols(n)],
                        rz.at[s, :, cols(n)],
                        z_send.at[0],
                        z_recv.at[n * 8 + s],
                        sib,
                    ).wait_recv()

        for s in range(2 * NY):
            mine = mine + rz[s, :, cols(n)].astype(F32)
        out_ref[y_rows(y), cols(n)] = mine.astype(BF16)
        for d in range(1, NY):
            piece = out_ref.at[y_rows(y), cols(n)]
            cp = remote(
                piece,
                piece,
                o_send.at[n * 4 + d],
                o_recv.at[n * 4 + d],
                dev(z, x, c, (y + d) % NY),
            )
            cp.start()
            o_cps.append(cp)
    for n in range(PARTS):
        for d in range(1, NY):
            piece = out_ref.at[y_rows((y - d + NY) % NY), cols(n)]
            remote(piece, piece, o_send.at[d], o_recv.at[n * 4 + d], sib).wait_recv()

    for cp in list(sib_cps.values()) + list(y_cps.values()) + o_cps:
        cp.wait_send()
    for here, cp in a_cps + z_cps:

        @pl.when(jnp.logical_not(here))
        def _(cp=cp):
            cp.wait_send()

    for cp in x_cps + h_cps:

        @pl.when(odd)
        def _(cp=cp):
            cp.wait_send()


def reduce_back(pa, pb):
    width = pa.shape[1]
    dma = pltpu.SemaphoreType.DMA
    vmem = pl.BlockSpec(memory_space=pltpu.VMEM)
    return pl.pallas_call(
        reduce_kernel,
        out_shape=jax.ShapeDtypeStruct((BLK, width), BF16),
        in_specs=[pl.BlockSpec(memory_space=pltpu.HBM)] * 2,
        out_specs=vmem,
        scratch_shapes=[
            pltpu.VMEM((2, BLK, width), BF16),
            pltpu.VMEM((4, BLK, width), BF16),
            pltpu.VMEM((2, BLK, width), BF16),
            pltpu.VMEM((2, BLK, width), BF16),
            pltpu.VMEM((2 * NY, SHARE, width), BF16),
            pltpu.VMEM((BLK, width), BF16),
            pltpu.VMEM((NY, SHARE, width), BF16),
            pltpu.VMEM((2, SHARE, width), BF16),
            pltpu.VMEM((SHARE, width), BF16),
            dma((3,)),
            dma((4 * PARTS,)),
            dma((4 * PARTS,)),
            dma((2 * PARTS,)),
            dma((2 * PARTS,)),
            dma((8 * PARTS,)),
            dma((8 * PARTS,)),
            dma((4 * PARTS,)),
            dma((4 * PARTS,)),
            dma((4 * PARTS,)),
            dma((4 * PARTS,)),
            dma((2 * PARTS,)),
            dma((2 * PARTS,)),
            dma((PARTS,)),
        ],
        compiler_params=pltpu.CompilerParams(
            collective_id=1, has_side_effects=True, vmem_limit_bytes=VMEM_ALL
        ),
        name="reduce_back",
    )(pa, pb)


def body(
    tokens,
    proj_in,
    attn_query,
    attn_keyval,
    attn_output,
    mlp_up,
    mlp_down,
    pair_list,
    conf_level,
    conf_table,
):
    img_dev, tok_count, enc_width = tokens.shape
    a_blk, b_blk, pairs = gather(
        tokens.reshape(img_dev * tok_count, enc_width),
        proj_in,
        pair_list.T,
        conf_level.reshape(1, PAIR_DEV),
    )
    pa, pb = cell(
        conf_table, pairs, a_blk, b_blk, attn_query, attn_keyval, attn_output, mlp_up, mlp_down
    )
    joined = reduce_back(pa, pb)
    return joined.reshape(img_dev, tok_count, joined.shape[1])


def solution(mesh):
    placed = (
        P("img", None, None),
        P(),
        P(),
        P(),
        P(),
        P(),
        P(),
        P(("img", "rep"), None),
        P(("img", "rep")),
        P(),
    )
    return jax.shard_map(
        body, mesh=mesh, in_specs=placed, out_specs=P("img", None, None), check_vma=False
    )
```

```python
import jax
import jax.numpy as jnp
from jax import lax
from jax.experimental import pallas as pl
from jax.experimental.pallas import tpu as pltpu
from jax.sharding import PartitionSpec as P

HEAD_DIM = 64
TOK = 24
IMG_DEV = 8
NX, NY, NZ = 4, 4, 8
BLK = IMG_DEV * TOK
SIDE = 4 * BLK
DEVS = NX * NY * NZ * 2
PAIR_DEV = 32
GROUP = 24
HALF = 8
SLOTS = 72
PARTS = 2
VMEM_ALL = 64 * 1024 * 1024
SHARE = BLK // NY
FAR = 128
MESH = pl.DeviceIdType.MESH
F32 = jnp.float32
BF16 = jnp.bfloat16


def place():
    img = lax.axis_index("img")
    return img // 8, (img // 2) % 4, img % 2, lax.axis_index("rep")


def dev(z, x, c, y):
    return ((z * NX + x) * 2 + c, y)


def remote(src, dst, send, recv, to):
    return pltpu.make_async_remote_copy(
        src_ref=src,
        dst_ref=dst,
        send_sem=send,
        recv_sem=recv,
        device_id=to,
        device_id_type=MESH,
    )


def row_peers(z, x, c, y):
    ks = [(x * 2 + c + d) % 8 for d in range(1, 8)]
    return [dev(z, k // 2, k % 2, y) for k in ks]


def z_peers(z, x, c, y):
    return [dev((z + d) % NZ, x, c, y) for d in range(1, NZ)]


def y_peers(z, x, c, y):
    return [dev(z, x, c, (y + d) % NY) for d in range(1, NY)]


def barrier_all(z, x, c, y):
    barrier = pltpu.get_barrier_semaphore()
    peers = row_peers(z, x, c, y) + z_peers(z, x, c, y) + y_peers(z, x, c, y)
    for p in peers:
        pl.semaphore_signal(barrier, inc=1, device_id=p, device_id_type=MESH)
    return barrier, len(peers)


def far_target(z, y):
    return (z + jnp.where(y == 1, 3, 5)) % NZ


def far_source(z, y):
    return (z + jnp.where(y == 1, 5, 3)) % NZ


def gather_kernel(
    tok_hbm,
    proj_hbm,
    pair_hbm,
    level_hbm,
    a_out,
    b_out,
    list_out,
    tok,
    proj,
    pair_ref,
    level_ref,
    own,
    a_send,
    a_recv,
    b_send,
    b_recv,
    f_send,
    f_recv,
    loc,
    lx_send,
    lx_recv,
    lz_send,
    lz_recv,
    ly_send,
    ly_recv,
):
    z, x, c, y = place()
    tok_in = pltpu.make_async_copy(tok_hbm, tok, loc.at[2])
    proj_in = pltpu.make_async_copy(proj_hbm, proj, loc.at[3])
    pair_in = pltpu.make_async_copy(pair_hbm, pair_ref, loc.at[4])
    level_in = pltpu.make_async_copy(level_hbm, level_ref, loc.at[5])
    inputs = (pair_in, level_in, tok_in, proj_in)
    for cp in inputs:
        cp.start()
    barrier, n_peers = barrier_all(z, x, c, y)
    odd = y % 2 == 1
    other = (y + 2) % NY

    @pl.when(odd)
    def _():
        source = dev(far_source(z, y), x, c, other)
        pl.semaphore_signal(barrier, inc=1, device_id=source, device_id_type=MESH)

    for cp in inputs:
        cp.wait()
    own[...] = jnp.dot(tok[...], proj[...], preferred_element_type=F32).astype(BF16)
    me8 = x * 2 + c
    row_me = y * 64 + me8 * 8 + z
    list_out[row_me, :, 0:PAIR_DEV] = pair_ref[0:1, :]
    list_out[row_me, :, PAIR_DEV : 2 * PAIR_DEV] = pair_ref[1:2, :]
    list_out[row_me, :, 2 * PAIR_DEV : 3 * PAIR_DEV] = level_ref[...]
    list_out[row_me, :, 3 * PAIR_DEV :] = jnp.zeros((1, 128 - 3 * PAIR_DEV), jnp.int32)
    pl.semaphore_wait(barrier, n_peers + jnp.where(odd, 1, 0))

    lz = []
    for d in range(1, NZ):
        mine = list_out.at[pl.ds(row_me, 1)]
        cp = remote(mine, mine, lz_send.at[d], lz_recv.at[d], dev((z + d) % NZ, x, c, y))
        cp.start()
        lz.append(cp)

    s_b = (z // 4) * 2 + c
    b_dst = b_out.at[pl.ds(pl.multiple_of(s_b * BLK, BLK), BLK)]
    z0 = (z - y + NZ) % NZ
    z1 = (z - y + NZ + 4) % NZ
    self_b = y == 0
    b0_local = pltpu.make_async_copy(own, b_dst, loc.at[0])

    @pl.when(self_b)
    def _():
        b0_local.start()

    near_dst = b_out.at[pl.ds(pl.multiple_of(s_b * BLK, BLK), FAR)]
    far_dst = b_out.at[pl.ds(pl.multiple_of(s_b * BLK + FAR, BLK - FAR), BLK - FAR)]
    over = dev(far_target(z, other), x, c, other)
    cross = remote(own.at[pl.ds(FAR, BLK - FAR)], far_dst, b_send.at[2], b_recv.at[2], over)
    b_cps = [(odd, cross)]
    for t, zt in ((1, z1), (0, z0)):
        far = y == (1 if t == 1 else 3)
        whole = remote(own, b_dst, b_send.at[t], b_recv.at[z // 4], dev(zt, x, c, y))
        most = remote(
            own.at[pl.ds(0, FAR)], near_dst, b_send.at[t], b_recv.at[z // 4], dev(zt, x, c, y)
        )
        b_cps.append((far, most))
        full = jnp.logical_not(far)
        b_cps.append((jnp.logical_and(full, jnp.logical_not(self_b)) if t == 0 else full, whole))
    for go, cp in b_cps:

        @pl.when(go)
        def _(cp=cp):
            cp.start()

    for cp in lz:
        cp.wait_recv()
    lx = []
    for d in range(1, 8):
        k = (me8 + d) % 8
        rows = list_out.at[pl.ds(y * 64 + me8 * 8, 8)]
        cp = remote(rows, rows, lx_send.at[d], lx_recv.at[d], dev(z, k // 2, k % 2, y))
        cp.start()
        lx.append(cp)

    s_a = (x % 2) * 2 + c
    a_dst = a_out.at[pl.ds(pl.multiple_of(s_a * BLK, BLK), BLK)]
    half = x // 2
    self_a = half == c
    a_cps = []
    for d in (2, 1, 3):
        cp = remote(own, a_dst, a_send.at[d], a_recv.at[s_a], dev(z, (x + d) % NX, half, y))
        cp.start()
        a_cps.append(cp)
    a0 = remote(own, a_dst, a_send.at[0], a_recv.at[s_a], dev(z, x, half, y))
    a0_local = pltpu.make_async_copy(own, a_dst, loc.at[1])

    @pl.when(jnp.logical_not(self_a))
    def _():
        a0.start()

    @pl.when(self_a)
    def _():
        a0_local.start()

    for cp in lx:
        cp.wait_recv()
    ly = []
    for d in range(1, NY):
        rows = list_out.at[pl.ds(y * 64, 64)]
        cp = remote(rows, rows, ly_send.at[d], ly_recv.at[d], dev(z, x, c, (y + d) % NY))
        cp.start()
        ly.append(cp)

    sib = dev(z, x, 1 - c, y)
    fwd = []
    for t in range(2):
        base = (t * 2 + c) * BLK
        slot = b_out.at[pl.ds(pl.multiple_of(base, BLK), BLK)]
        arrived = remote(own, slot, b_send.at[t], b_recv.at[t], sib)
        most = remote(
            own.at[pl.ds(0, FAR)],
            b_out.at[pl.ds(pl.multiple_of(base, BLK), FAR)],
            b_send.at[t],
            b_recv.at[t],
            sib,
        )
        rest = remote(
            own.at[pl.ds(FAR, BLK - FAR)],
            b_out.at[pl.ds(pl.multiple_of(base + FAR, BLK - FAR), BLK - FAR)],
            b_send.at[2],
            b_recv.at[2],
            sib,
        )
        here = jnp.logical_and(self_b, z // 4 == t)
        split = jnp.logical_and(odd, far_source(z, y) // 4 == t)

        @pl.when(jnp.logical_not(jnp.logical_or(here, split)))
        def _(arrived=arrived):
            arrived.wait_recv()

        @pl.when(split)
        def _(most=most, rest=rest):
            most.wait_recv()
            rest.wait_recv()

        @pl.when(here)
        def _():
            b0_local.wait()

        cp = remote(slot, slot, f_send.at[t], f_recv.at[t], sib)
        cp.start()
        fwd.append(cp)

    for s in range(4):
        slot = a_out.at[pl.ds(s * BLK, BLK)]
        arrived = remote(own, slot, a_send.at[0], a_recv.at[s], sib)
        here = jnp.logical_and(self_a, s_a == s)

        @pl.when(jnp.logical_not(here))
        def _(arrived=arrived):
            arrived.wait_recv()

        @pl.when(here)
        def _():
            a0_local.wait()

    for t in range(2):
        slot = b_out.at[pl.ds(pl.multiple_of((t * 2 + 1 - c) * BLK, BLK), BLK)]
        remote(slot, slot, f_send.at[t], f_recv.at[t], sib).wait_recv()
    for cp in ly:
        cp.wait_recv()

    for cp in lx + lz + ly + a_cps + fwd:
        cp.wait_send()

    for go, cp in b_cps:

        @pl.when(go)
        def _(cp=cp):
            cp.wait_send()

    @pl.when(jnp.logical_not(self_a))
    def _():
        a0.wait_send()


def gather(tokens, proj_in, pairs_t, levels):
    width = proj_in.shape[1]
    dma = pltpu.SemaphoreType.DMA
    vmem = pl.BlockSpec(memory_space=pltpu.VMEM)
    anym = pl.BlockSpec(memory_space=pltpu.HBM)
    return pl.pallas_call(
        gather_kernel,
        out_shape=(
            jax.ShapeDtypeStruct((SIDE, width), BF16),
            jax.ShapeDtypeStruct((SIDE, width), BF16),
            jax.ShapeDtypeStruct((DEVS, 1, 128), jnp.int32),
        ),
        in_specs=[anym] * 4,
        out_specs=(anym, anym, vmem),
        scratch_shapes=[
            pltpu.VMEM(tokens.shape, BF16),
            pltpu.VMEM(proj_in.shape, BF16),
            pltpu.VMEM(pairs_t.shape, jnp.int32),
            pltpu.VMEM(levels.shape, jnp.int32),
            pltpu.VMEM((BLK, width), BF16),
            dma((4,)),
            dma((4,)),
            dma((3,)),
            dma((3,)),
            dma((2,)),
            dma((2,)),
            dma((6,)),
            dma((8,)),
            dma((8,)),
            dma((8,)),
            dma((8,)),
            dma((4,)),
            dma((4,)),
        ],
        compiler_params=pltpu.CompilerParams(
            collective_id=0, has_side_effects=True, vmem_limit_bytes=VMEM_ALL
        ),
        name="gather_blocks",
    )(tokens, proj_in, pairs_t, levels)


def norm(v):
    centred = v - jnp.mean(v, axis=-1, keepdims=True)
    spread = jnp.mean(centred * centred, axis=-1, keepdims=True)
    return centred * lax.rsqrt(spread + 1e-06)


def cell_kernel(
    table_ref,
    list_hbm,
    a_hbm,
    b_hbm,
    wq_hbm,
    wkv_hbm,
    wo_hbm,
    up_hbm,
    down_hbm,
    pa_hbm,
    pb_hbm,
    list_ref,
    a_ref,
    b_ref,
    wq,
    wkv,
    wo,
    up,
    down,
    side,
    qs,
    ks,
    vs,
    acc_a,
    acc_b,
    rank_t,
    val_t,
    slots_v,
    slots_s,
    att,
    ffn,
    sems,
):
    width = wq.shape[0]
    heads_quad = 4
    quad = heads_quad * HEAD_DIM
    copies = [
        pltpu.make_async_copy(h, v, sems.at[i])
        for i, (h, v) in enumerate(
            (
                (a_hbm, a_ref),
                (wq_hbm, wq),
                (b_hbm, b_ref),
                (wkv_hbm, wkv),
                (wo_hbm, wo),
                (up_hbm, up),
                (down_hbm, down),
            )
        )
    ]
    list_in = pltpu.make_async_copy(list_hbm, list_ref, sems.at[8])
    list_in.start()
    for cp in copies[:4]:
        cp.start()
    acc_a[...] = jnp.zeros_like(acc_a)
    acc_b[...] = jnp.zeros_like(acc_b)
    list_in.wait()

    z, x, c, y = place()
    a_id, b_x, b_j = z * 2 + c, x, (z + y) % 4
    flat = list_ref[...].reshape(DEVS, 128)
    flat_t = flat.astype(F32).T.astype(jnp.int32)
    a_img = flat_t[:PAIR_DEV]
    b_img = flat_t[PAIR_DEV : 2 * PAIR_DEV]
    level = flat_t[2 * PAIR_DEV : 3 * PAIR_DEV]
    hit = (
        (lax.shift_right_logical(a_img, 5) == a_id)
        & ((lax.shift_right_logical(b_img, 4) & 3) == b_x)
        & ((lax.shift_right_logical(b_img, 6) & 3) == b_j)
    )
    hit_f = hit.astype(F32)
    r_i = lax.broadcasted_iota(jnp.int32, (DEVS, DEVS), 0)
    c_i = lax.broadcasted_iota(jnp.int32, (DEVS, DEVS), 1)
    upper = (r_i <= c_i).astype(BF16)
    across = jnp.dot(hit_f.astype(BF16), upper, preferred_element_type=F32)
    totals = across[:, DEVS - 1 : DEVS]
    k_r = lax.broadcasted_iota(jnp.int32, (PAIR_DEV, PAIR_DEV), 0)
    k_c = lax.broadcasted_iota(jnp.int32, (PAIR_DEV, PAIR_DEV), 1)
    lower = (k_c < k_r).astype(BF16)
    before = jnp.dot(
        lower,
        jnp.broadcast_to(totals, (PAIR_DEV, 128)).astype(BF16),
        preferred_element_type=F32,
    )[:, :1]
    rank = (across + before).astype(jnp.int32) - 1
    rank_t[...] = jnp.where(hit, rank, -1)
    val_t[...] = ((a_img & 31) * 32 + (lax.shift_right_logical(b_img, 8) * 16 + (b_img & 15))) * 16 + level
    count = jnp.sum(hit_f).astype(jnp.int32)

    def fetch_slots():
        return pltpu.make_async_copy(slots_v, slots_s, sems.at[7])

    def select(block):
        slot = lax.broadcasted_iota(jnp.int32, (SLOTS, DEVS), 0) + block * SLOTS
        found = jnp.zeros((SLOTS, DEVS), jnp.int32)
        for k in range(PAIR_DEV):
            found += jnp.where(rank_t[k : k + 1, :] == slot, val_t[k : k + 1, :], 0)
        col = jnp.sum(found.astype(F32), axis=1, keepdims=True).astype(jnp.int32)
        slots_v[...] = jnp.broadcast_to(col, (SLOTS, 128))
        fetch_slots().start()

    select(0)

    for cp in copies[:4]:
        cp.wait()
    for cp in copies[4:]:
        cp.start()
    for i in range(4):
        rows = pl.ds(i * BLK, BLK)
        q_side = a_ref[rows, :].astype(F32)
        side[pl.ds(i * IMG_DEV, IMG_DEV)] = q_side.reshape(IMG_DEV, TOK, width)
        qn = norm(q_side).astype(BF16)
        q = jnp.dot(qn, wq[...], preferred_element_type=F32).astype(BF16).astype(F32)
        qs[pl.ds(i * IMG_DEV, IMG_DEV)] = (q * (HEAD_DIM**-0.5)).reshape(IMG_DEV, TOK, width)
        mn = norm(b_ref[rows, :].astype(F32)).astype(BF16)
        k = jnp.dot(mn, wkv[:, :width], preferred_element_type=F32)
        ks[pl.ds(i * IMG_DEV, IMG_DEV)] = k.reshape(IMG_DEV, TOK, width)
        v = jnp.dot(mn, wkv[:, width:], preferred_element_type=F32)
        vs[pl.ds(i * IMG_DEV, IMG_DEV)] = v.reshape(IMG_DEV, TOK, width)
    for cp in copies[4:]:
        cp.wait()

    lane_head = lax.broadcasted_iota(jnp.int32, (TOK, quad), 1) // HEAD_DIM

    def attend(a_loc, b_loc):
        out = []
        for p in range(width // quad):
            cols = slice(p * quad, (p + 1) * quad)
            q = qs[a_loc, :, cols]
            k = ks[b_loc, :, cols].astype(BF16)
            v = vs[b_loc, :, cols].astype(BF16)
            q4 = jnp.concatenate(
                [jnp.where(lane_head == h, q, 0.0) for h in range(heads_quad)], axis=0
            ).astype(BF16)
            s = lax.dot_general(k, q4, (((1,), (1,)), ((), ())), preferred_element_type=F32)
            e = jnp.exp(s - jnp.max(s, axis=0, keepdims=True))
            probs = (e / jnp.sum(e, axis=0, keepdims=True)).astype(BF16)
            r = lax.dot_general(probs, v, (((0,), (0,)), ((), ())), preferred_element_type=F32)
            o = r[3 * TOK :]
            for h in (2, 1, 0):
                o = jnp.where(lane_head == h, r[h * TOK : (h + 1) * TOK], o)
            out.append(o)
        return jnp.concatenate(out, axis=1)

    def group(first, here, pairs_in):
        locs = []
        for i in range(pairs_in):
            word = slots_s[first + i, 0]
            a_loc = word // 512
            b_loc = (word // 16) % 32
            locs.append((a_loc, b_loc, word % 16))
            att[pl.ds(i * TOK, TOK), :] = attend(a_loc, b_loc)
        rows = pl.ds(0, pairs_in * TOK)
        query = jnp.concatenate([side[a_loc] for a_loc, _, _ in locs], axis=0)
        hidden = query + jnp.dot(att[rows, :].astype(BF16), wo[...], preferred_element_type=F32)
        hn = norm(hidden).astype(BF16)
        u = jnp.dot(hn, up[...], preferred_element_type=F32)
        ex = (0.5 * u) * (1.0 + lax.erf(u * (0.5**0.5)))
        ffn[rows, :] = hidden + jnp.dot(
            ex.astype(BF16), down[...], preferred_element_type=F32
        )
        for i in range(pairs_in):
            a_loc, b_loc, lev = locs[i]

            @pl.when(first + i < here)
            def _(i=i, a_loc=a_loc, b_loc=b_loc, lev=lev):
                feature = table_ref[lev] * ffn[pl.ds(i * TOK, TOK), :]
                feature = feature.astype(BF16).astype(F32)
                acc_a[a_loc] = acc_a[a_loc] + feature
                acc_b[b_loc] = acc_b[b_loc] + feature

    def slot_block(block, carry):
        here = jnp.minimum(count - block * SLOTS, SLOTS)
        wide = (here + GROUP - HALF - 1) // GROUP

        def wide_group(g, carry2):
            group(g * GROUP, here, GROUP)
            return carry2

        lax.fori_loop(0, wide, wide_group, 0)

        @pl.when(wide * GROUP < here)
        def _():
            group(wide * GROUP, here, HALF)

        @pl.when((block + 1) * SLOTS < count)
        def _():
            select(block + 1)
            fetch_slots().wait()

        return carry

    fetch_slots().wait()
    lax.fori_loop(0, (count + SLOTS - 1) // SLOTS, slot_block, 0)
    outs = []
    for i in range(4):
        rows = pl.ds(i * BLK, BLK)
        images = pl.ds(i * IMG_DEV, IMG_DEV)
        for k, (acc, buf, hbm) in enumerate(((acc_a, a_ref, pa_hbm), (acc_b, b_ref, pb_hbm))):
            buf[rows, :] = acc[images].reshape(BLK, width).astype(BF16)
            cp = pltpu.make_async_copy(buf.at[rows], hbm.at[rows], sems.at[9 + 2 * i + k])
            cp.start()
            outs.append(cp)
    for cp in outs:
        cp.wait()


def cell(table, pairs, a_blk, b_blk, wq, wkv, wo, up, down):
    width, ff = up.shape
    smem = pl.BlockSpec(memory_space=pltpu.SMEM)
    anym = pl.BlockSpec(memory_space=pltpu.HBM)
    images = 4 * IMG_DEV
    return pl.pallas_call(
        cell_kernel,
        out_shape=(
            jax.ShapeDtypeStruct((SIDE, width), BF16),
            jax.ShapeDtypeStruct((SIDE, width), BF16),
        ),
        in_specs=[smem] + [anym] * 8,
        out_specs=(anym, anym),
        scratch_shapes=[
            pltpu.VMEM((DEVS, 1, 128), jnp.int32),
            pltpu.VMEM((SIDE, width), BF16),
            pltpu.VMEM((SIDE, width), BF16),
            pltpu.VMEM((width, width), BF16),
            pltpu.VMEM((width, 2 * width), BF16),
            pltpu.VMEM((width, width), BF16),
            pltpu.VMEM((width, ff), BF16),
            pltpu.VMEM((ff, width), BF16),
            pltpu.VMEM((images, TOK, width), F32),
            pltpu.VMEM((images, TOK, width), F32),
            pltpu.VMEM((images, TOK, width), F32),
            pltpu.VMEM((images, TOK, width), F32),
            pltpu.VMEM((images, TOK, width), F32),
            pltpu.VMEM((images, TOK, width), F32),
            pltpu.VMEM((PAIR_DEV, DEVS), jnp.int32),
            pltpu.VMEM((PAIR_DEV, DEVS), jnp.int32),
            pltpu.VMEM((SLOTS, 128), jnp.int32),
            pltpu.SMEM((SLOTS, 128), jnp.int32),
            pltpu.VMEM((GROUP * TOK, width), F32),
            pltpu.VMEM((GROUP * TOK, width), F32),
            pltpu.SemaphoreType.DMA((17,)),
        ],
        compiler_params=pltpu.CompilerParams(vmem_limit_bytes=VMEM_ALL),
        name="cell_pairs",
    )(table, pairs, a_blk, b_blk, wq, wkv, wo, up, down)


def reduce_kernel(
    pa_hbm,
    pb_hbm,
    out_ref,
    pb,
    ra,
    rsib,
    sb,
    rz,
    tot,
    ry,
    rx,
    relay,
    loc,
    a_send,
    a_recv,
    s_send,
    s_recv,
    z_send,
    z_recv,
    y_send,
    y_recv,
    o_send,
    o_recv,
    x_send,
    x_recv,
    h_send,
):
    z, x, c, y = place()
    self_a = x // 2 == c
    self_b = y == 0

    def block(s):
        return pl.ds(pl.multiple_of(s * BLK, BLK), BLK)

    def y_rows(yy):
        return pl.ds(pl.multiple_of(yy * SHARE, SHARE), SHARE)

    keep = []
    for t in range(2):
        cp = pltpu.make_async_copy(pb_hbm.at[block(t * 2 + c)], pb.at[t], loc.at[t])
        cp.start()
        keep.append(cp)
    own_a = pltpu.make_async_copy(pa_hbm.at[block((x % 2) * 2 + c)], ra.at[x], loc.at[2])

    @pl.when(self_a)
    def _():
        own_a.start()

    barrier = pltpu.get_barrier_semaphore()
    for p in row_peers(z, x, c, y) + y_peers(z, x, c, y):
        pl.semaphore_signal(barrier, inc=1, device_id=p, device_id_type=MESH)
    for ys in range(NY):
        for zh in range(2):
            zs = (z + NZ - ys) % 4 + 4 * zh
            here = jnp.logical_and(ys == y, zs == z)

            @pl.when(jnp.logical_not(here))
            def _(zs=zs, ys=ys):
                pl.semaphore_signal(
                    barrier, inc=1, device_id=dev(zs, x, c, ys), device_id_type=MESH
                )

    odd = y % 2 == 1
    other = (y + 2) % NY

    @pl.when(odd)
    def _():
        for p in (dev(z, x, 1 - c, other), dev(far_target(z, other), x, c, y)):
            pl.semaphore_signal(barrier, inc=1, device_id=p, device_id_type=MESH)

    extra = jnp.where(odd, 2, jnp.where(self_b, -1, 0))
    pl.semaphore_wait(barrier, 7 + NY - 1 + 2 * NY + extra)
    sib = dev(z, x, 1 - c, y)

    width = out_ref.shape[1]

    def cols(n):
        return pl.ds(n * (width // PARTS), width // PARTS)

    sib_cps = {}
    for n in range(PARTS):
        for t in range(2):
            i = n * 2 + t
            sib_cps[i] = remote(
                pb_hbm.at[block(t * 2 + 1 - c), cols(n)],
                rsib.at[t, :, cols(n)],
                s_send.at[i],
                s_recv.at[i],
                sib,
            )
            sib_cps[i].start()

    far = far_source(z, y)
    x_cps = []
    for n in range(PARTS):
        for cc in range(2):
            s = (far // 4) * 2 + cc
            piece = pl.ds(pl.multiple_of(s * BLK + other * SHARE, SHARE), SHARE)
            cp = remote(
                pb_hbm.at[piece, cols(n)],
                rx.at[c, :, cols(n)],
                x_send.at[n * 2 + cc],
                x_recv.at[n * 2 + c],
                dev(z, x, cc, other),
            )
            x_cps.append(cp)

            @pl.when(odd)
            def _(cp=cp):
                cp.start()

    a_cps = []
    for n in range(PARTS):
        for s in range(4):
            xt = 2 * c + s // 2
            here = jnp.logical_and(xt == x, c == s % 2)
            cp = remote(
                pa_hbm.at[block(s), cols(n)],
                ra.at[x, :, cols(n)],
                a_send.at[n * 4 + s],
                a_recv.at[n * 4 + x],
                dev(z, xt, s % 2, y),
            )
            a_cps.append((here, cp))

            @pl.when(jnp.logical_not(here))
            def _(cp=cp):
                cp.start()

    j = (z + y) % 4
    z_cps = []
    slot = y * 2 + z // 4
    for cp in keep:
        cp.wait()
    for n in range(PARTS):
        for t in range(2):
            sib_cps[n * 2 + t].wait_recv()
            total = pb[t, :, cols(n)].astype(F32) + rsib[t, :, cols(n)].astype(F32)
            sb[t, :, cols(n)] = total.astype(BF16)
            zt = j + 4 * t
            for q in range(NY):
                piece = pl.ds(q * SHARE, SHARE)
                here = jnp.logical_and(zt == z, q == y)
                cp = remote(
                    sb.at[t, piece, cols(n)],
                    rz.at[slot, :, cols(n)],
                    z_send.at[n * 8 + q * 2 + t],
                    z_recv.at[n * 8 + slot],
                    dev(zt, x, c, q),
                )
                turn = jnp.logical_and(odd, jnp.logical_and(far // 4 == t, q == other))
                kept = jnp.logical_or(here, turn)
                z_cps.append((kept, cp))

                @pl.when(jnp.logical_not(kept))
                def _(cp=cp):
                    cp.start()

                @pl.when(here)
                def _(t=t, piece=piece, n=n):
                    rz[slot, :, cols(n)] = sb[t, piece, cols(n)]

    h_slot = other * 2 + z // 4
    h_cps = []
    for n in range(PARTS):
        h_cps.append(
            remote(
                relay.at[:, cols(n)],
                rz.at[h_slot, :, cols(n)],
                h_send.at[n],
                z_recv.at[n * 8 + h_slot],
                dev(far_source(z, other), x, c, y),
            )
        )

        @pl.when(odd)
        def _(n=n):
            for cc in range(2):
                remote(
                    pb_hbm.at[pl.ds(0, SHARE), cols(n)],
                    rx.at[cc, :, cols(n)],
                    x_send.at[0],
                    x_recv.at[n * 2 + cc],
                    sib,
                ).wait_recv()
            both = rx[0, :, cols(n)].astype(F32) + rx[1, :, cols(n)].astype(F32)
            relay[:, cols(n)] = both.astype(BF16)
            h_cps[n].start()

    @pl.when(self_a)
    def _():
        own_a.wait()

    y_cps = {}
    for n in range(PARTS):
        for s in range(4):
            here = jnp.logical_and(s == x, self_a)

            @pl.when(jnp.logical_not(here))
            def _(s=s, n=n):
                remote(
                    pa_hbm.at[block(0), cols(n)],
                    ra.at[s, :, cols(n)],
                    a_send.at[0],
                    a_recv.at[n * 4 + s],
                    sib,
                ).wait_recv()

        total = (
            ra[0, :, cols(n)].astype(F32)
            + ra[1, :, cols(n)].astype(F32)
            + ra[2, :, cols(n)].astype(F32)
            + ra[3, :, cols(n)].astype(F32)
        )
        tot[:, cols(n)] = total.astype(BF16)
        for d in range(1, NY):
            yt = (y + d) % NY
            cp = remote(
                tot.at[y_rows(yt), cols(n)],
                ry.at[d, :, cols(n)],
                y_send.at[n * 4 + d],
                y_recv.at[n * 4 + d],
                dev(z, x, c, yt),
            )
            cp.start()
            y_cps[n * 4 + d] = cp

    o_cps = []
    for n in range(PARTS):
        mine = tot[y_rows(y), cols(n)].astype(F32)
        for d in range(1, NY):
            y_cps[n * 4 + d].wait_recv()
            mine = mine + ry[d, :, cols(n)].astype(F32)
        for ys in range(NY):
            for zh in range(2):
                s = ys * 2 + zh
                here = jnp.logical_and(jnp.logical_and(self_b, ys == 0), z // 4 == zh)

                @pl.when(jnp.logical_not(here))
                def _(s=s, n=n):
                    remote(
                        sb.at[0, pl.ds(0, SHARE), cols(n)],
                        rz.at[s, :, cols(n)],
                        z_send.at[0],
                        z_recv.at[n * 8 + s],
                        sib,
                    ).wait_recv()

        for s in range(2 * NY):
            mine = mine + rz[s, :, cols(n)].astype(F32)
        out_ref[y_rows(y), cols(n)] = mine.astype(BF16)
        for d in range(1, NY):
            piece = out_ref.at[y_rows(y), cols(n)]
            cp = remote(
                piece,
                piece,
                o_send.at[n * 4 + d],
                o_recv.at[n * 4 + d],
                dev(z, x, c, (y + d) % NY),
            )
            cp.start()
            o_cps.append(cp)
    for n in range(PARTS):
        for d in range(1, NY):
            piece = out_ref.at[y_rows((y - d + NY) % NY), cols(n)]
            remote(piece, piece, o_send.at[d], o_recv.at[n * 4 + d], sib).wait_recv()

    for cp in list(sib_cps.values()) + list(y_cps.values()) + o_cps:
        cp.wait_send()
    for here, cp in a_cps + z_cps:

        @pl.when(jnp.logical_not(here))
        def _(cp=cp):
            cp.wait_send()

    for cp in x_cps + h_cps:

        @pl.when(odd)
        def _(cp=cp):
            cp.wait_send()


def reduce_back(pa, pb):
    width = pa.shape[1]
    dma = pltpu.SemaphoreType.DMA
    vmem = pl.BlockSpec(memory_space=pltpu.VMEM)
    return pl.pallas_call(
        reduce_kernel,
        out_shape=jax.ShapeDtypeStruct((BLK, width), BF16),
        in_specs=[pl.BlockSpec(memory_space=pltpu.HBM)] * 2,
        out_specs=vmem,
        scratch_shapes=[
            pltpu.VMEM((2, BLK, width), BF16),
            pltpu.VMEM((4, BLK, width), BF16),
            pltpu.VMEM((2, BLK, width), BF16),
            pltpu.VMEM((2, BLK, width), BF16),
            pltpu.VMEM((2 * NY, SHARE, width), BF16),
            pltpu.VMEM((BLK, width), BF16),
            pltpu.VMEM((NY, SHARE, width), BF16),
            pltpu.VMEM((2, SHARE, width), BF16),
            pltpu.VMEM((SHARE, width), BF16),
            dma((3,)),
            dma((4 * PARTS,)),
            dma((4 * PARTS,)),
            dma((2 * PARTS,)),
            dma((2 * PARTS,)),
            dma((8 * PARTS,)),
            dma((8 * PARTS,)),
            dma((4 * PARTS,)),
            dma((4 * PARTS,)),
            dma((4 * PARTS,)),
            dma((4 * PARTS,)),
            dma((2 * PARTS,)),
            dma((2 * PARTS,)),
            dma((PARTS,)),
        ],
        compiler_params=pltpu.CompilerParams(
            collective_id=1, has_side_effects=True, vmem_limit_bytes=VMEM_ALL - 1100 * 1024
        ),
        name="reduce_back",
    )(pa, pb)


def body(
    tokens,
    proj_in,
    attn_query,
    attn_keyval,
    attn_output,
    mlp_up,
    mlp_down,
    pair_list,
    conf_level,
    conf_table,
):
    img_dev, tok_count, enc_width = tokens.shape
    a_blk, b_blk, pairs = gather(
        tokens.reshape(img_dev * tok_count, enc_width),
        proj_in,
        pair_list.T,
        conf_level.reshape(1, PAIR_DEV),
    )
    pa, pb = cell(
        conf_table, pairs, a_blk, b_blk, attn_query, attn_keyval, attn_output, mlp_up, mlp_down
    )
    joined = reduce_back(pa, pb)
    return joined.reshape(img_dev, tok_count, joined.shape[1])


def solution(mesh):
    placed = (
        P("img", None, None),
        P(),
        P(),
        P(),
        P(),
        P(),
        P(),
        P(("img", "rep"), None),
        P(("img", "rep")),
        P(),
    )
    return jax.shard_map(
        body, mesh=mesh, in_specs=placed, out_specs=P("img", None, None), check_vma=False
    )
```

```python
import jax
import jax.numpy as jnp
from jax import lax
from jax.experimental import pallas as pl
from jax.experimental.pallas import tpu as pltpu
from jax.sharding import PartitionSpec as P

HEAD_DIM = 64
TOK = 24
IMG_DEV = 8
NX, NY, NZ = 4, 4, 8
BLK = IMG_DEV * TOK
SIDE = 4 * BLK
DEVS = NX * NY * NZ * 2
PAIR_DEV = 32
GROUP = 24
HALF = 8
SLOTS = 72
PARTS = 2
VMEM_ALL = 64 * 1024 * 1024
SHARE = BLK // NY
FAR = 128
MESH = pl.DeviceIdType.MESH
F32 = jnp.float32
BF16 = jnp.bfloat16


def place():
    img = lax.axis_index("img")
    return img // 8, (img // 2) % 4, img % 2, lax.axis_index("rep")


def dev(z, x, c, y):
    return ((z * NX + x) * 2 + c, y)


def remote(src, dst, send, recv, to):
    return pltpu.make_async_remote_copy(
        src_ref=src,
        dst_ref=dst,
        send_sem=send,
        recv_sem=recv,
        device_id=to,
        device_id_type=MESH,
    )


def row_peers(z, x, c, y):
    ks = [(x * 2 + c + d) % 8 for d in range(1, 8)]
    return [dev(z, k // 2, k % 2, y) for k in ks]


def z_peers(z, x, c, y):
    return [dev((z + d) % NZ, x, c, y) for d in range(1, NZ)]


def y_peers(z, x, c, y):
    return [dev(z, x, c, (y + d) % NY) for d in range(1, NY)]


def barrier_all(z, x, c, y):
    barrier = pltpu.get_barrier_semaphore()
    peers = row_peers(z, x, c, y) + z_peers(z, x, c, y) + y_peers(z, x, c, y)
    for p in peers:
        pl.semaphore_signal(barrier, inc=1, device_id=p, device_id_type=MESH)
    return barrier, len(peers)


def far_target(z, y):
    return (z + jnp.where(y == 1, 3, 5)) % NZ


def far_source(z, y):
    return (z + jnp.where(y == 1, 5, 3)) % NZ


def gather_kernel(
    tok_hbm,
    proj_hbm,
    pair_hbm,
    level_hbm,
    a_out,
    b_out,
    list_out,
    tok,
    proj,
    pair_ref,
    level_ref,
    own,
    a_send,
    a_recv,
    b_send,
    b_recv,
    f_send,
    f_recv,
    loc,
    lx_send,
    lx_recv,
    lz_send,
    lz_recv,
    ly_send,
    ly_recv,
):
    z, x, c, y = place()
    tok_in = pltpu.make_async_copy(tok_hbm, tok, loc.at[2])
    proj_in = pltpu.make_async_copy(proj_hbm, proj, loc.at[3])
    pair_in = pltpu.make_async_copy(pair_hbm, pair_ref, loc.at[4])
    level_in = pltpu.make_async_copy(level_hbm, level_ref, loc.at[5])
    inputs = (pair_in, level_in, tok_in, proj_in)
    for cp in inputs:
        cp.start()
    barrier, n_peers = barrier_all(z, x, c, y)
    odd = y % 2 == 1
    other = (y + 2) % NY

    @pl.when(odd)
    def _():
        source = dev(far_source(z, y), x, c, other)
        pl.semaphore_signal(barrier, inc=1, device_id=source, device_id_type=MESH)

    for cp in inputs:
        cp.wait()
    own[...] = jnp.dot(tok[...], proj[...], preferred_element_type=F32).astype(BF16)
    me8 = x * 2 + c
    row_me = y * 64 + me8 * 8 + z
    list_out[row_me, :, 0:PAIR_DEV] = pair_ref[0:1, :]
    list_out[row_me, :, PAIR_DEV : 2 * PAIR_DEV] = pair_ref[1:2, :]
    list_out[row_me, :, 2 * PAIR_DEV : 3 * PAIR_DEV] = level_ref[...]
    list_out[row_me, :, 3 * PAIR_DEV :] = jnp.zeros((1, 128 - 3 * PAIR_DEV), jnp.int32)
    pl.semaphore_wait(barrier, n_peers + jnp.where(odd, 1, 0))

    s_b = (z // 4) * 2 + c
    b_dst = b_out.at[pl.ds(pl.multiple_of(s_b * BLK, BLK), BLK)]
    z0 = (z - y + NZ) % NZ
    z1 = (z - y + NZ + 4) % NZ
    self_b = y == 0
    b0_local = pltpu.make_async_copy(own, b_dst, loc.at[0])

    @pl.when(self_b)
    def _():
        b0_local.start()

    near_dst = b_out.at[pl.ds(pl.multiple_of(s_b * BLK, BLK), FAR)]
    far_dst = b_out.at[pl.ds(pl.multiple_of(s_b * BLK + FAR, BLK - FAR), BLK - FAR)]
    over = dev(far_target(z, other), x, c, other)
    cross = remote(own.at[pl.ds(FAR, BLK - FAR)], far_dst, b_send.at[2], b_recv.at[2], over)
    b_cps = [(odd, cross)]
    for t, zt in ((1, z1), (0, z0)):
        far = y == (1 if t == 1 else 3)
        whole = remote(own, b_dst, b_send.at[t], b_recv.at[z // 4], dev(zt, x, c, y))
        most = remote(
            own.at[pl.ds(0, FAR)], near_dst, b_send.at[t], b_recv.at[z // 4], dev(zt, x, c, y)
        )
        b_cps.append((far, most))
        full = jnp.logical_not(far)
        b_cps.append((jnp.logical_and(full, jnp.logical_not(self_b)) if t == 0 else full, whole))
    for go, cp in b_cps:

        @pl.when(go)
        def _(cp=cp):
            cp.start()

    lz = []
    for d in range(1, NZ):
        mine = list_out.at[pl.ds(row_me, 1)]
        cp = remote(mine, mine, lz_send.at[d], lz_recv.at[d], dev((z + d) % NZ, x, c, y))
        cp.start()
        lz.append(cp)

    for cp in lz:
        cp.wait_recv()
    lx = []
    for d in range(1, 8):
        k = (me8 + d) % 8
        rows = list_out.at[pl.ds(y * 64 + me8 * 8, 8)]
        cp = remote(rows, rows, lx_send.at[d], lx_recv.at[d], dev(z, k // 2, k % 2, y))
        cp.start()
        lx.append(cp)

    s_a = (x % 2) * 2 + c
    a_dst = a_out.at[pl.ds(pl.multiple_of(s_a * BLK, BLK), BLK)]
    half = x // 2
    self_a = half == c
    a_cps = []
    for d in (2, 1, 3):
        cp = remote(own, a_dst, a_send.at[d], a_recv.at[s_a], dev(z, (x + d) % NX, half, y))
        cp.start()
        a_cps.append(cp)
    a0 = remote(own, a_dst, a_send.at[0], a_recv.at[s_a], dev(z, x, half, y))
    a0_local = pltpu.make_async_copy(own, a_dst, loc.at[1])

    @pl.when(jnp.logical_not(self_a))
    def _():
        a0.start()

    @pl.when(self_a)
    def _():
        a0_local.start()

    for cp in lx:
        cp.wait_recv()
    ly = []
    for d in range(1, NY):
        rows = list_out.at[pl.ds(y * 64, 64)]
        cp = remote(rows, rows, ly_send.at[d], ly_recv.at[d], dev(z, x, c, (y + d) % NY))
        cp.start()
        ly.append(cp)

    sib = dev(z, x, 1 - c, y)
    fwd = []
    for t in range(2):
        base = (t * 2 + c) * BLK
        slot = b_out.at[pl.ds(pl.multiple_of(base, BLK), BLK)]
        arrived = remote(own, slot, b_send.at[t], b_recv.at[t], sib)
        most = remote(
            own.at[pl.ds(0, FAR)],
            b_out.at[pl.ds(pl.multiple_of(base, BLK), FAR)],
            b_send.at[t],
            b_recv.at[t],
            sib,
        )
        rest = remote(
            own.at[pl.ds(FAR, BLK - FAR)],
            b_out.at[pl.ds(pl.multiple_of(base + FAR, BLK - FAR), BLK - FAR)],
            b_send.at[2],
            b_recv.at[2],
            sib,
        )
        here = jnp.logical_and(self_b, z // 4 == t)
        split = jnp.logical_and(odd, far_source(z, y) // 4 == t)

        @pl.when(jnp.logical_not(jnp.logical_or(here, split)))
        def _(arrived=arrived):
            arrived.wait_recv()

        @pl.when(split)
        def _(most=most, rest=rest):
            most.wait_recv()
            rest.wait_recv()

        @pl.when(here)
        def _():
            b0_local.wait()

        cp = remote(slot, slot, f_send.at[t], f_recv.at[t], sib)
        cp.start()
        fwd.append(cp)

    for s in range(4):
        slot = a_out.at[pl.ds(s * BLK, BLK)]
        arrived = remote(own, slot, a_send.at[0], a_recv.at[s], sib)
        here = jnp.logical_and(self_a, s_a == s)

        @pl.when(jnp.logical_not(here))
        def _(arrived=arrived):
            arrived.wait_recv()

        @pl.when(here)
        def _():
            a0_local.wait()

    for t in range(2):
        slot = b_out.at[pl.ds(pl.multiple_of((t * 2 + 1 - c) * BLK, BLK), BLK)]
        remote(slot, slot, f_send.at[t], f_recv.at[t], sib).wait_recv()
    for cp in ly:
        cp.wait_recv()

    for cp in lx + lz + ly + a_cps + fwd:
        cp.wait_send()

    for go, cp in b_cps:

        @pl.when(go)
        def _(cp=cp):
            cp.wait_send()

    @pl.when(jnp.logical_not(self_a))
    def _():
        a0.wait_send()


def gather(tokens, proj_in, pairs_t, levels):
    width = proj_in.shape[1]
    dma = pltpu.SemaphoreType.DMA
    vmem = pl.BlockSpec(memory_space=pltpu.VMEM)
    anym = pl.BlockSpec(memory_space=pltpu.HBM)
    return pl.pallas_call(
        gather_kernel,
        out_shape=(
            jax.ShapeDtypeStruct((SIDE, width), BF16),
            jax.ShapeDtypeStruct((SIDE, width), BF16),
            jax.ShapeDtypeStruct((DEVS, 1, 128), jnp.int32),
        ),
        in_specs=[anym] * 4,
        out_specs=(anym, anym, vmem),
        scratch_shapes=[
            pltpu.VMEM(tokens.shape, BF16),
            pltpu.VMEM(proj_in.shape, BF16),
            pltpu.VMEM(pairs_t.shape, jnp.int32),
            pltpu.VMEM(levels.shape, jnp.int32),
            pltpu.VMEM((BLK, width), BF16),
            dma((4,)),
            dma((4,)),
            dma((3,)),
            dma((3,)),
            dma((2,)),
            dma((2,)),
            dma((6,)),
            dma((8,)),
            dma((8,)),
            dma((8,)),
            dma((8,)),
            dma((4,)),
            dma((4,)),
        ],
        compiler_params=pltpu.CompilerParams(
            collective_id=0, has_side_effects=True, vmem_limit_bytes=VMEM_ALL
        ),
        name="gather_blocks",
    )(tokens, proj_in, pairs_t, levels)


def norm(v):
    centred = v - jnp.mean(v, axis=-1, keepdims=True)
    spread = jnp.mean(centred * centred, axis=-1, keepdims=True)
    return centred * lax.rsqrt(spread + 1e-06)


def cell_kernel(
    table_ref,
    list_hbm,
    a_hbm,
    b_hbm,
    wq_hbm,
    wkv_hbm,
    wo_hbm,
    up_hbm,
    down_hbm,
    pa_hbm,
    pb_hbm,
    list_ref,
    a_ref,
    b_ref,
    wq,
    wkv,
    wo,
    up,
    down,
    side,
    qs,
    ks,
    vs,
    acc_a,
    acc_b,
    rank_t,
    val_t,
    slots_v,
    slots_s,
    att,
    ffn,
    sems,
):
    width = wq.shape[0]
    heads_quad = 4
    quad = heads_quad * HEAD_DIM
    copies = [
        pltpu.make_async_copy(h, v, sems.at[i])
        for i, (h, v) in enumerate(
            (
                (a_hbm, a_ref),
                (wq_hbm, wq),
                (b_hbm, b_ref),
                (wkv_hbm, wkv),
                (wo_hbm, wo),
                (up_hbm, up),
                (down_hbm, down),
            )
        )
    ]
    list_in = pltpu.make_async_copy(list_hbm, list_ref, sems.at[8])
    list_in.start()
    for cp in copies[:4]:
        cp.start()
    acc_a[...] = jnp.zeros_like(acc_a)
    acc_b[...] = jnp.zeros_like(acc_b)
    list_in.wait()

    z, x, c, y = place()
    a_id, b_x, b_j = z * 2 + c, x, (z + y) % 4
    flat = list_ref[...].reshape(DEVS, 128)
    flat_t = flat.astype(F32).T.astype(jnp.int32)
    a_img = flat_t[:PAIR_DEV]
    b_img = flat_t[PAIR_DEV : 2 * PAIR_DEV]
    level = flat_t[2 * PAIR_DEV : 3 * PAIR_DEV]
    hit = (
        (lax.shift_right_logical(a_img, 5) == a_id)
        & ((lax.shift_right_logical(b_img, 4) & 3) == b_x)
        & ((lax.shift_right_logical(b_img, 6) & 3) == b_j)
    )
    hit_f = hit.astype(F32)
    r_i = lax.broadcasted_iota(jnp.int32, (DEVS, DEVS), 0)
    c_i = lax.broadcasted_iota(jnp.int32, (DEVS, DEVS), 1)
    upper = (r_i <= c_i).astype(BF16)
    across = jnp.dot(hit_f.astype(BF16), upper, preferred_element_type=F32)
    totals = across[:, DEVS - 1 : DEVS]
    k_r = lax.broadcasted_iota(jnp.int32, (PAIR_DEV, PAIR_DEV), 0)
    k_c = lax.broadcasted_iota(jnp.int32, (PAIR_DEV, PAIR_DEV), 1)
    lower = (k_c < k_r).astype(BF16)
    before = jnp.dot(
        lower,
        jnp.broadcast_to(totals, (PAIR_DEV, 128)).astype(BF16),
        preferred_element_type=F32,
    )[:, :1]
    rank = (across + before).astype(jnp.int32) - 1
    rank_t[...] = jnp.where(hit, rank, -1)
    val_t[...] = ((a_img & 31) * 32 + (lax.shift_right_logical(b_img, 8) * 16 + (b_img & 15))) * 16 + level
    count = jnp.sum(hit_f).astype(jnp.int32)

    def fetch_slots():
        return pltpu.make_async_copy(slots_v, slots_s, sems.at[7])

    def select(block):
        slot = lax.broadcasted_iota(jnp.int32, (SLOTS, DEVS), 0) + block * SLOTS
        found = jnp.zeros((SLOTS, DEVS), jnp.int32)
        for k in range(PAIR_DEV):
            found += jnp.where(rank_t[k : k + 1, :] == slot, val_t[k : k + 1, :], 0)
        col = jnp.sum(found.astype(F32), axis=1, keepdims=True).astype(jnp.int32)
        slots_v[...] = jnp.broadcast_to(col, (SLOTS, 128))
        fetch_slots().start()

    select(0)

    for cp in copies[:4]:
        cp.wait()
    for cp in copies[4:]:
        cp.start()
    for i in range(4):
        rows = pl.ds(i * BLK, BLK)
        q_side = a_ref[rows, :].astype(F32)
        side[pl.ds(i * IMG_DEV, IMG_DEV)] = q_side.reshape(IMG_DEV, TOK, width)
        qn = norm(q_side).astype(BF16)
        q = jnp.dot(qn, wq[...], preferred_element_type=F32).astype(BF16).astype(F32)
        qs[pl.ds(i * IMG_DEV, IMG_DEV)] = (q * (HEAD_DIM**-0.5)).reshape(IMG_DEV, TOK, width)
        mn = norm(b_ref[rows, :].astype(F32)).astype(BF16)
        k = jnp.dot(mn, wkv[:, :width], preferred_element_type=F32)
        ks[pl.ds(i * IMG_DEV, IMG_DEV)] = k.reshape(IMG_DEV, TOK, width)
        v = jnp.dot(mn, wkv[:, width:], preferred_element_type=F32)
        vs[pl.ds(i * IMG_DEV, IMG_DEV)] = v.reshape(IMG_DEV, TOK, width)
    for cp in copies[4:]:
        cp.wait()

    lane_head = lax.broadcasted_iota(jnp.int32, (TOK, quad), 1) // HEAD_DIM

    def attend(a_loc, b_loc):
        out = []
        for p in range(width // quad):
            cols = slice(p * quad, (p + 1) * quad)
            q = qs[a_loc, :, cols]
            k = ks[b_loc, :, cols].astype(BF16)
            v = vs[b_loc, :, cols].astype(BF16)
            q4 = jnp.concatenate(
                [jnp.where(lane_head == h, q, 0.0) for h in range(heads_quad)], axis=0
            ).astype(BF16)
            s = lax.dot_general(k, q4, (((1,), (1,)), ((), ())), preferred_element_type=F32)
            e = jnp.exp(s - jnp.max(s, axis=0, keepdims=True))
            probs = (e / jnp.sum(e, axis=0, keepdims=True)).astype(BF16)
            r = lax.dot_general(probs, v, (((0,), (0,)), ((), ())), preferred_element_type=F32)
            o = r[3 * TOK :]
            for h in (2, 1, 0):
                o = jnp.where(lane_head == h, r[h * TOK : (h + 1) * TOK], o)
            out.append(o)
        return jnp.concatenate(out, axis=1)

    def group(first, here, pairs_in):
        locs = []
        for i in range(pairs_in):
            word = slots_s[first + i, 0]
            a_loc = word // 512
            b_loc = (word // 16) % 32
            locs.append((a_loc, b_loc, word % 16))
            att[pl.ds(i * TOK, TOK), :] = attend(a_loc, b_loc)
        rows = pl.ds(0, pairs_in * TOK)
        query = jnp.concatenate([side[a_loc] for a_loc, _, _ in locs], axis=0)
        hidden = query + jnp.dot(att[rows, :].astype(BF16), wo[...], preferred_element_type=F32)
        hn = norm(hidden).astype(BF16)
        u = jnp.dot(hn, up[...], preferred_element_type=F32)
        ex = (0.5 * u) * (1.0 + lax.erf(u * (0.5**0.5)))
        ffn[rows, :] = hidden + jnp.dot(
            ex.astype(BF16), down[...], preferred_element_type=F32
        )
        for i in range(pairs_in):
            a_loc, b_loc, lev = locs[i]

            @pl.when(first + i < here)
            def _(i=i, a_loc=a_loc, b_loc=b_loc, lev=lev):
                feature = table_ref[lev] * ffn[pl.ds(i * TOK, TOK), :]
                feature = feature.astype(BF16).astype(F32)
                acc_a[a_loc] = acc_a[a_loc] + feature
                acc_b[b_loc] = acc_b[b_loc] + feature

    def slot_block(block, carry):
        here = jnp.minimum(count - block * SLOTS, SLOTS)
        wide = (here + GROUP - HALF - 1) // GROUP

        def wide_group(g, carry2):
            group(g * GROUP, here, GROUP)
            return carry2

        lax.fori_loop(0, wide, wide_group, 0)

        @pl.when(wide * GROUP < here)
        def _():
            group(wide * GROUP, here, HALF)

        @pl.when((block + 1) * SLOTS < count)
        def _():
            select(block + 1)
            fetch_slots().wait()

        return carry

    fetch_slots().wait()
    lax.fori_loop(0, (count + SLOTS - 1) // SLOTS, slot_block, 0)
    outs = []
    for i in range(4):
        rows = pl.ds(i * BLK, BLK)
        images = pl.ds(i * IMG_DEV, IMG_DEV)
        for k, (acc, buf, hbm) in enumerate(((acc_a, a_ref, pa_hbm), (acc_b, b_ref, pb_hbm))):
            buf[rows, :] = acc[images].reshape(BLK, width).astype(BF16)
            cp = pltpu.make_async_copy(buf.at[rows], hbm.at[rows], sems.at[9 + 2 * i + k])
            cp.start()
            outs.append(cp)
    for cp in outs:
        cp.wait()


def cell(table, pairs, a_blk, b_blk, wq, wkv, wo, up, down):
    width, ff = up.shape
    smem = pl.BlockSpec(memory_space=pltpu.SMEM)
    anym = pl.BlockSpec(memory_space=pltpu.HBM)
    images = 4 * IMG_DEV
    return pl.pallas_call(
        cell_kernel,
        out_shape=(
            jax.ShapeDtypeStruct((SIDE, width), BF16),
            jax.ShapeDtypeStruct((SIDE, width), BF16),
        ),
        in_specs=[smem] + [anym] * 8,
        out_specs=(anym, anym),
        scratch_shapes=[
            pltpu.VMEM((DEVS, 1, 128), jnp.int32),
            pltpu.VMEM((SIDE, width), BF16),
            pltpu.VMEM((SIDE, width), BF16),
            pltpu.VMEM((width, width), BF16),
            pltpu.VMEM((width, 2 * width), BF16),
            pltpu.VMEM((width, width), BF16),
            pltpu.VMEM((width, ff), BF16),
            pltpu.VMEM((ff, width), BF16),
            pltpu.VMEM((images, TOK, width), F32),
            pltpu.VMEM((images, TOK, width), F32),
            pltpu.VMEM((images, TOK, width), F32),
            pltpu.VMEM((images, TOK, width), F32),
            pltpu.VMEM((images, TOK, width), F32),
            pltpu.VMEM((images, TOK, width), F32),
            pltpu.VMEM((PAIR_DEV, DEVS), jnp.int32),
            pltpu.VMEM((PAIR_DEV, DEVS), jnp.int32),
            pltpu.VMEM((SLOTS, 128), jnp.int32),
            pltpu.SMEM((SLOTS, 128), jnp.int32),
            pltpu.VMEM((GROUP * TOK, width), F32),
            pltpu.VMEM((GROUP * TOK, width), F32),
            pltpu.SemaphoreType.DMA((17,)),
        ],
        compiler_params=pltpu.CompilerParams(vmem_limit_bytes=VMEM_ALL),
        name="cell_pairs",
    )(table, pairs, a_blk, b_blk, wq, wkv, wo, up, down)


def reduce_kernel(
    pa_hbm,
    pb_hbm,
    out_ref,
    pb,
    ra,
    rsib,
    sb,
    rz,
    tot,
    ry,
    rx,
    relay,
    loc,
    a_send,
    a_recv,
    s_send,
    s_recv,
    z_send,
    z_recv,
    y_send,
    y_recv,
    o_send,
    o_recv,
    x_send,
    x_recv,
    h_send,
):
    z, x, c, y = place()
    self_a = x // 2 == c
    self_b = y == 0

    def block(s):
        return pl.ds(pl.multiple_of(s * BLK, BLK), BLK)

    def y_rows(yy):
        return pl.ds(pl.multiple_of(yy * SHARE, SHARE), SHARE)

    keep = []
    for t in range(2):
        cp = pltpu.make_async_copy(pb_hbm.at[block(t * 2 + c)], pb.at[t], loc.at[t])
        cp.start()
        keep.append(cp)
    own_a = pltpu.make_async_copy(pa_hbm.at[block((x % 2) * 2 + c)], ra.at[x], loc.at[2])

    @pl.when(self_a)
    def _():
        own_a.start()

    barrier = pltpu.get_barrier_semaphore()
    for p in row_peers(z, x, c, y) + y_peers(z, x, c, y):
        pl.semaphore_signal(barrier, inc=1, device_id=p, device_id_type=MESH)
    for ys in range(NY):
        for zh in range(2):
            zs = (z + NZ - ys) % 4 + 4 * zh
            here = jnp.logical_and(ys == y, zs == z)

            @pl.when(jnp.logical_not(here))
            def _(zs=zs, ys=ys):
                pl.semaphore_signal(
                    barrier, inc=1, device_id=dev(zs, x, c, ys), device_id_type=MESH
                )

    odd = y % 2 == 1
    other = (y + 2) % NY

    @pl.when(odd)
    def _():
        for p in (dev(z, x, 1 - c, other), dev(far_target(z, other), x, c, y)):
            pl.semaphore_signal(barrier, inc=1, device_id=p, device_id_type=MESH)

    extra = jnp.where(odd, 2, jnp.where(self_b, -1, 0))
    pl.semaphore_wait(barrier, 7 + NY - 1 + 2 * NY + extra)
    sib = dev(z, x, 1 - c, y)

    width = out_ref.shape[1]

    def cols(n):
        return pl.ds(n * (width // PARTS), width // PARTS)

    sib_cps = {}
    for n in range(PARTS):
        for t in range(2):
            i = n * 2 + t
            sib_cps[i] = remote(
                pb_hbm.at[block(t * 2 + 1 - c), cols(n)],
                rsib.at[t, :, cols(n)],
                s_send.at[i],
                s_recv.at[i],
                sib,
            )
            sib_cps[i].start()

    far = far_source(z, y)
    x_cps = []
    for n in range(PARTS):
        for cc in range(2):
            s = (far // 4) * 2 + cc
            piece = pl.ds(pl.multiple_of(s * BLK + other * SHARE, SHARE), SHARE)
            cp = remote(
                pb_hbm.at[piece, cols(n)],
                rx.at[c, :, cols(n)],
                x_send.at[n * 2 + cc],
                x_recv.at[n * 2 + c],
                dev(z, x, cc, other),
            )
            x_cps.append(cp)

            @pl.when(odd)
            def _(cp=cp):
                cp.start()

    a_cps = []
    for n in range(PARTS):
        for s in range(4):
            xt = 2 * c + s // 2
            here = jnp.logical_and(xt == x, c == s % 2)
            cp = remote(
                pa_hbm.at[block(s), cols(n)],
                ra.at[x, :, cols(n)],
                a_send.at[n * 4 + s],
                a_recv.at[n * 4 + x],
                dev(z, xt, s % 2, y),
            )
            a_cps.append((here, cp))

            @pl.when(jnp.logical_not(here))
            def _(cp=cp):
                cp.start()

    j = (z + y) % 4
    z_cps = []
    slot = y * 2 + z // 4
    for cp in keep:
        cp.wait()
    for n in range(PARTS):
        for t in range(2):
            sib_cps[n * 2 + t].wait_recv()
            total = pb[t, :, cols(n)].astype(F32) + rsib[t, :, cols(n)].astype(F32)
            sb[t, :, cols(n)] = total.astype(BF16)
            zt = j + 4 * t
            for q in range(NY):
                piece = pl.ds(q * SHARE, SHARE)
                here = jnp.logical_and(zt == z, q == y)
                cp = remote(
                    sb.at[t, piece, cols(n)],
                    rz.at[slot, :, cols(n)],
                    z_send.at[n * 8 + q * 2 + t],
                    z_recv.at[n * 8 + slot],
                    dev(zt, x, c, q),
                )
                turn = jnp.logical_and(odd, jnp.logical_and(far // 4 == t, q == other))
                kept = jnp.logical_or(here, turn)
                z_cps.append((kept, cp))

                @pl.when(jnp.logical_not(kept))
                def _(cp=cp):
                    cp.start()

                @pl.when(here)
                def _(t=t, piece=piece, n=n):
                    rz[slot, :, cols(n)] = sb[t, piece, cols(n)]

    h_slot = other * 2 + z // 4
    h_cps = []
    for n in range(PARTS):
        h_cps.append(
            remote(
                relay.at[:, cols(n)],
                rz.at[h_slot, :, cols(n)],
                h_send.at[n],
                z_recv.at[n * 8 + h_slot],
                dev(far_source(z, other), x, c, y),
            )
        )

        @pl.when(odd)
        def _(n=n):
            for cc in range(2):
                remote(
                    pb_hbm.at[pl.ds(0, SHARE), cols(n)],
                    rx.at[cc, :, cols(n)],
                    x_send.at[0],
                    x_recv.at[n * 2 + cc],
                    sib,
                ).wait_recv()
            both = rx[0, :, cols(n)].astype(F32) + rx[1, :, cols(n)].astype(F32)
            relay[:, cols(n)] = both.astype(BF16)
            h_cps[n].start()

    @pl.when(self_a)
    def _():
        own_a.wait()

    y_cps = {}
    for n in range(PARTS):
        for s in range(4):
            here = jnp.logical_and(s == x, self_a)

            @pl.when(jnp.logical_not(here))
            def _(s=s, n=n):
                remote(
                    pa_hbm.at[block(0), cols(n)],
                    ra.at[s, :, cols(n)],
                    a_send.at[0],
                    a_recv.at[n * 4 + s],
                    sib,
                ).wait_recv()

        total = (
            ra[0, :, cols(n)].astype(F32)
            + ra[1, :, cols(n)].astype(F32)
            + ra[2, :, cols(n)].astype(F32)
            + ra[3, :, cols(n)].astype(F32)
        )
        tot[:, cols(n)] = total.astype(BF16)
        for d in range(1, NY):
            yt = (y + d) % NY
            cp = remote(
                tot.at[y_rows(yt), cols(n)],
                ry.at[d, :, cols(n)],
                y_send.at[n * 4 + d],
                y_recv.at[n * 4 + d],
                dev(z, x, c, yt),
            )
            cp.start()
            y_cps[n * 4 + d] = cp

    o_cps = []
    for n in range(PARTS):
        mine = tot[y_rows(y), cols(n)].astype(F32)
        for d in range(1, NY):
            y_cps[n * 4 + d].wait_recv()
            mine = mine + ry[d, :, cols(n)].astype(F32)
        for ys in range(NY):
            for zh in range(2):
                s = ys * 2 + zh
                here = jnp.logical_and(jnp.logical_and(self_b, ys == 0), z // 4 == zh)

                @pl.when(jnp.logical_not(here))
                def _(s=s, n=n):
                    remote(
                        sb.at[0, pl.ds(0, SHARE), cols(n)],
                        rz.at[s, :, cols(n)],
                        z_send.at[0],
                        z_recv.at[n * 8 + s],
                        sib,
                    ).wait_recv()

        for s in range(2 * NY):
            mine = mine + rz[s, :, cols(n)].astype(F32)
        out_ref[y_rows(y), cols(n)] = mine.astype(BF16)
        for d in range(1, NY):
            piece = out_ref.at[y_rows(y), cols(n)]
            cp = remote(
                piece,
                piece,
                o_send.at[n * 4 + d],
                o_recv.at[n * 4 + d],
                dev(z, x, c, (y + d) % NY),
            )
            cp.start()
            o_cps.append(cp)
    for n in range(PARTS):
        for d in range(1, NY):
            piece = out_ref.at[y_rows((y - d + NY) % NY), cols(n)]
            remote(piece, piece, o_send.at[d], o_recv.at[n * 4 + d], sib).wait_recv()

    for cp in list(sib_cps.values()) + list(y_cps.values()) + o_cps:
        cp.wait_send()
    for here, cp in a_cps + z_cps:

        @pl.when(jnp.logical_not(here))
        def _(cp=cp):
            cp.wait_send()

    for cp in x_cps + h_cps:

        @pl.when(odd)
        def _(cp=cp):
            cp.wait_send()


def reduce_back(pa, pb):
    width = pa.shape[1]
    dma = pltpu.SemaphoreType.DMA
    vmem = pl.BlockSpec(memory_space=pltpu.VMEM)
    return pl.pallas_call(
        reduce_kernel,
        out_shape=jax.ShapeDtypeStruct((BLK, width), BF16),
        in_specs=[pl.BlockSpec(memory_space=pltpu.HBM)] * 2,
        out_specs=vmem,
        scratch_shapes=[
            pltpu.VMEM((2, BLK, width), BF16),
            pltpu.VMEM((4, BLK, width), BF16),
            pltpu.VMEM((2, BLK, width), BF16),
            pltpu.VMEM((2, BLK, width), BF16),
            pltpu.VMEM((2 * NY, SHARE, width), BF16),
            pltpu.VMEM((BLK, width), BF16),
            pltpu.VMEM((NY, SHARE, width), BF16),
            pltpu.VMEM((2, SHARE, width), BF16),
            pltpu.VMEM((SHARE, width), BF16),
            dma((3,)),
            dma((4 * PARTS,)),
            dma((4 * PARTS,)),
            dma((2 * PARTS,)),
            dma((2 * PARTS,)),
            dma((8 * PARTS,)),
            dma((8 * PARTS,)),
            dma((4 * PARTS,)),
            dma((4 * PARTS,)),
            dma((4 * PARTS,)),
            dma((4 * PARTS,)),
            dma((2 * PARTS,)),
            dma((2 * PARTS,)),
            dma((PARTS,)),
        ],
        compiler_params=pltpu.CompilerParams(
            collective_id=1, has_side_effects=True, vmem_limit_bytes=VMEM_ALL - 1100 * 1024
        ),
        name="reduce_back",
    )(pa, pb)


def body(
    tokens,
    proj_in,
    attn_query,
    attn_keyval,
    attn_output,
    mlp_up,
    mlp_down,
    pair_list,
    conf_level,
    conf_table,
):
    img_dev, tok_count, enc_width = tokens.shape
    a_blk, b_blk, pairs = gather(
        tokens.reshape(img_dev * tok_count, enc_width),
        proj_in,
        pair_list.T,
        conf_level.reshape(1, PAIR_DEV),
    )
    pa, pb = cell(
        conf_table, pairs, a_blk, b_blk, attn_query, attn_keyval, attn_output, mlp_up, mlp_down
    )
    joined = reduce_back(pa, pb)
    return joined.reshape(img_dev, tok_count, joined.shape[1])


def solution(mesh):
    placed = (
        P("img", None, None),
        P(),
        P(),
        P(),
        P(),
        P(),
        P(),
        P(("img", "rep"), None),
        P(("img", "rep")),
        P(),
    )
    return jax.shard_map(
        body, mesh=mesh, in_specs=placed, out_specs=P("img", None, None), check_vma=False
    )
```
